32 devices in a mesh: depth: 4 (over y, core), strips: 8 (over z, x).
Axes of the slice: x: 2, y: 2, z: 4, core: 2. Of those that a mesh axis runs over, the one named last changes fastest.
Arguments:
- pressure: float32 [32, 1024, 1024], P('depth', 'strips'), may hold values from -3 to 3
- texture: int32 [32, 1024, 1024], P('depth', 'strips'), may hold values from 0 to 11
- active: int32 [32, 1024, 1024], P('depth', 'strips'), may hold values 0 or 1
- rain: float32 [1024, 1024], P('strips'), may hold values from 0 to 40
- k_sat: float32 [12], replicated, may hold values from 0.05 to 2
- alpha: float32 [12], replicated, may hold values from 0.5 to 4
- theta_sat: float32 [12], replicated, may hold values from 0.35 to 0.5
- head_old: float32 [1024, 1024], P('strips', 'depth'), may hold values from -4 to 4
- cell_code: int32 [1024, 1024], P('strips', 'depth'), may hold values from 0 to 2
- section: float32 [1024, 1024], P('strips', 'depth'), may hold values from -4 to 4
Outputs:
- moisture_new: float32 [32, 1024, 1024], P('depth', 'strips')
- head: float32 [1024, 1024], P('strips', 'depth')
The draws below stay inside these ranges and needn't reach their ends.
All inputs are finite; a program needn't handle non-finite values. No bound on the sum of `active` on one device may be relied on, other than what follows from the above.
Results may differ from the reference program's by a relative error of at most 0.00002.
Values sent between devices are 32-bit elements; how exact they have to be, the bound alone decides.
No kernel may reach another device: no remote copies, remote signals or barrier semaphores. Data moves between devices by JAX's collectives and lax.ppermute only.
A program may use at most 128 MiB of HBM per device.

```python
import math
import jax
import jax.numpy as jnp
from jax import lax

NCLASS = 12
SWEEPS = 3
LAYERS = 32
NX = 1024
NY = 1024


def plant(values, rng, smallest, high):
    longest = values.shape.index(max(values.shape))
    spots = []
    for shift in (0, 1):
        where = [jax.random.randint(jax.random.fold_in(rng, axis), (), 0, length) for axis, length in enumerate(values.shape)]
        where[longest] = (where[longest] + shift) % values.shape[longest]
        spots.append(tuple(where))
    return values.at[spots[0]].set(smallest).at[spots[1]].set(high)


def levels(stream_key, shape, cuts, least, high):
    loudness = 1.0
    for dim, blocks in cuts:
        steps = jax.random.uniform(jax.random.fold_in(jax.random.fold_in(stream_key, 6), dim), (blocks,), jnp.float32, least / len(cuts), high / len(cuts))
        loudness = loudness * jnp.repeat(jnp.exp(steps), shape[dim] // blocks).reshape((-1,) + (1,) * (len(shape) - 1 - dim))
    return loudness


def centred(own_key, extent, spread, most, shards=(), kind=jnp.bfloat16):
    drawn = jax.random.normal(own_key, extent, jnp.float32) * spread
    if len(shards) > 0:
        drawn = levels(own_key, extent, shards, -0.22, 0.18) * drawn
    return jnp.clip(drawn, min=-most, max=most).astype(kind)


def setup_inputs(seed: int = 0) -> dict:
    keys = jax.random.split(jax.random.key(seed), 11)
    pressure = centred(keys[0], (LAYERS, NX, NY), 0.5, 3.0, ((0, 4), (1, 8)), jnp.float32)
    texture = plant(jax.random.randint(keys[1], (LAYERS, NX, NY), 0, NCLASS), jax.random.fold_in(keys[1], 1), 0, NCLASS - 1).astype(jnp.int32)
    active = plant((jax.random.randint(keys[2], (LAYERS, NX, NY), 0, 8) < 7).astype(jnp.int32), jax.random.fold_in(keys[2], 1), 0, 1)
    rain = jnp.clip(40.0 * jax.random.uniform(keys[3], (NX, NY), jnp.float32) ** levels(keys[3], (NX, NY), ((0, 8),), -0.2, 0.2), 0.0, 40.0)
    k_sat = jnp.clip(jnp.exp(jax.random.uniform(keys[4], (NCLASS,), jnp.float32, math.log(0.05), math.log(2.0))), 0.05, 2.0)
    alpha = jnp.clip(jnp.exp(jax.random.uniform(keys[5], (NCLASS,), jnp.float32, math.log(0.5), math.log(4.0))), 0.5, 4.0)
    theta_sat = jnp.clip(jax.random.uniform(keys[6], (NCLASS,), jnp.float32, 0.35, 0.5), 0.35, 0.5)
    head_old = centred(keys[7], (NX, NY), 1.0, 4.0, ((0, 8), (1, 4)), jnp.float32)
    cell_code = plant(jax.random.randint(keys[8], (NX, NY), 0, 3), jax.random.fold_in(keys[8], 1), 0, 2).astype(jnp.int32)
    section = centred(keys[9], (NX, NY), 1.0, 4.0, ((0, 8), (1, 4)), jnp.float32)
    return {"pressure": pressure, "texture": texture, "active": active, "rain": rain, "k_sat": k_sat, "alpha": alpha, "theta_sat": theta_sat, "head_old": head_old, "cell_code": cell_code, "section": section}


layer_thick = 0.05
soil_step = 0.0002
spec_yield = 0.02
leak_rate = 0.5
river_cond = 0.5
fixed_cond = 3.0

def lookup(texture, table):
    result = jnp.zeros(texture.shape, jnp.float32)
    for class_id in range(table.shape[0]):
        result = result + jnp.where(texture == class_id, table[class_id], jnp.float32(0.0))
    return result

def face_flux(psi_up, cond_up, psi_low, cond_low):
    return 0.5 * (cond_up + cond_low) * ((psi_up - psi_low) / layer_thick + 1.0)

def neighbour(padded, shift_a, shift_b):
    return padded[1 + shift_a:padded.shape[0] - 1 + shift_a, 1 + shift_b:padded.shape[1] - 1 + shift_b]

def sweep(head_pad, trans_pad, base, rhs):
    centre = neighbour(trans_pad, 0, 0)
    total = base
    accum = rhs
    for shift_a, shift_b in ((1, 0), (-1, 0), (0, 1), (0, -1)):
        face = jnp.sqrt(centre * neighbour(trans_pad, shift_a, shift_b))
        accum = accum + face * neighbour(head_pad, shift_a, shift_b)
        total = total + face
    return accum / total

def reference(pressure, texture, active, rain, k_sat, alpha, theta_sat, head_old, cell_code, section):
    sat_cond = lookup(texture, k_sat)
    shape_par = lookup(texture, alpha)
    porous = lookup(texture, theta_sat)
    suction = jnp.minimum(pressure, 0.0)
    wetness = jnp.exp(0.5 * shape_par * suction)
    conduct = sat_cond * jnp.exp(shape_par * suction) * active.astype(jnp.float32)
    moisture = porous * (0.15 + 0.85 * wetness)
    trans = lax.optimization_barrier(jnp.sum(conduct, axis=0)) * layer_thick
    store = spec_yield + lax.optimization_barrier(jnp.sum(0.85 * porous * (1.0 - wetness), axis=0)) * layer_thick
    recharge = leak_rate * (lax.optimization_barrier(jnp.sum(conduct * wetness, axis=0)) * layer_thick)
    river = jnp.where(cell_code == 1, jnp.float32(river_cond), jnp.where(cell_code == 2, jnp.float32(fixed_cond), jnp.float32(0.0)))
    base = store + river
    rhs = store * head_old + recharge + river * section
    head = head_old
    trans_pad = jnp.pad(trans, 1)
    for sweep_id in range(SWEEPS):
        head = sweep(jnp.pad(head, 1), trans_pad, base, rhs)
    inner = face_flux(pressure[:-1], conduct[:-1], pressure[1:], conduct[1:])
    bottom = conduct[-1] * ((pressure[-1] - head) / (0.5 * layer_thick) + 1.0)
    lower = jnp.concatenate([inner, bottom[None]], axis=0)
    upper = jnp.concatenate([rain[None], inner], axis=0)
    moisture_new = moisture + soil_step / layer_thick * (upper - lower)
    return (moisture_new, head)
```

```python
import functools
import math

import jax
import jax.numpy as jnp
from jax import lax
from jax.experimental import pallas as pl
from jax.experimental.pallas import tpu as pltpu
from jax.sharding import PartitionSpec as P

SWEEPS = 3
SUB = 8
LANE = 128

layer_thick = 0.05
soil_step = 0.0002
spec_yield = 0.02
leak_rate = 0.5
river_cond = 0.5
fixed_cond = 3.0
residual = 0.15
mobile = 0.85

VMEM = pl.BlockSpec(memory_space=pltpu.VMEM)
ANY = pl.BlockSpec(memory_space=pl.ANY)


def params(mib):
    return pltpu.CompilerParams(vmem_limit_bytes=mib * 2**20)


def cost(flops, nbytes, trans=0):
    return pl.CostEstimate(flops=int(flops), bytes_accessed=int(nbytes), transcendentals=int(trans))


def place():
    depth = lax.axis_index("depth")
    return depth // 2, depth % 2


def gathered(table, classes):
    return jnp.take_along_axis(table, classes, axis=1, mode="promise_in_bounds")


def picked(options, bits):
    for bit in bits:
        options = [
            jnp.where(bit, options[i + 1], options[i]) if i + 1 < len(options) else options[i]
            for i in range(0, len(options), 2)
        ]
    return options[0]


def soil_kernel(
    sat_ref, alpha_ref, theta_ref, psi_ref, tex_ref, act_ref,
    moist_ref, keep_ref, send_ref, core_ref, chip_ref, tab, part,
):
    step = pl.program_id(0)
    _, core = place()
    layers, rows, cols = psi_ref.shape
    classes = sat_ref.shape[1]

    @pl.when(step == 0)
    def _():
        for i, (ref, scale) in enumerate(
            ((sat_ref, 1.0), (alpha_ref, 0.5 * math.log2(math.e)), (theta_ref, mobile))
        ):
            tab[i, :, :classes] = jnp.broadcast_to(ref[...] * scale, (SUB, classes))

    sat_tab, par_tab = tab[0], tab[1]
    theta = [jnp.broadcast_to(tab[2, :, i : i + 1], (SUB, LANE)) for i in range(classes)]
    nbits = max(1, (classes - 1).bit_length())
    face = 0.5 * soil_step / layer_thick
    core_layer = (1 - core) * (layers - 1)
    chip_layer = core * (layers - 1)

    def columns(q, carry):
        lanes = pl.ds(pl.multiple_of(q * LANE, LANE), LANE)
        for r in range(0, rows, SUB):
            rws = slice(r, r + SUB)
            trans = store = charge = jnp.zeros((SUB, LANE), jnp.float32)
            for layer in range(layers):
                kind = tex_ref[layer, rws, lanes]
                psi = psi_ref[layer, rws, lanes]
                active = act_ref[layer, rws, lanes].astype(jnp.float32)
                bits = [(kind & (1 << b)) != 0 for b in range(nbits)]
                wet = jnp.exp2(gathered(par_tab, kind) * jnp.minimum(psi, 0.0))
                cond = gathered(sat_tab, kind) * active * (wet * wet)
                mob = picked(theta, bits)
                mobwet = mob * wet
                trans = trans + cond
                charge = charge + cond * wet
                store = store + (mob - mobwet)
                held = mob * (residual / mobile) + mobwet
                if layer == 0:
                    first, own = cond, held
                else:
                    flux = (cond_up + cond) * ((psi_up - psi) * (face / layer_thick) + face)
                    moist_ref[layer - 1, rws, lanes] = own - flux
                    own = held + flux
                psi_up, cond_up = psi, cond
            moist_ref[layers - 1, rws, lanes] = own
            part[r // SUB, 0, :, lanes] = trans
            part[r // SUB, 1, :, lanes] = store
            part[r // SUB, 2, :, lanes] = charge
            core_ref[0, rws, lanes] = psi_ref[core_layer, rws, lanes]
            core_ref[1, rws, lanes] = jnp.where(core == 0, cond, first)
            chip_ref[0, rws, lanes] = psi_ref[chip_layer, rws, lanes]
            chip_ref[1, rws, lanes] = jnp.where(core == 0, first, cond)
        return carry

    lax.fori_loop(0, cols // LANE, columns, 0, unroll=2)

    blocks = rows // SUB
    half = keep_ref.shape[0] - 1
    for r in range(blocks):
        block = step * blocks + r

        def put(ref, at):
            ref[at] = part[r]

        @pl.when((block <= half) & (core == 0))
        def _():
            put(keep_ref, block)

        @pl.when((block <= half) & (core == 1))
        def _():
            put(send_ref, block)

        @pl.when((block >= half - 1) & (core == 0))
        def _():
            put(send_ref, block - (half - 1))

        @pl.when((block >= half - 1) & (core == 1))
        def _():
            put(keep_ref, block - (half - 1))


def soil(k_sat, alpha, theta_sat, pressure, texture, active):
    layers, nrows, cols = pressure.shape
    classes = k_sat.shape[0]
    rows = nrows // 4
    blocks = nrows // (2 * SUB) + 1
    whole = pl.BlockSpec((1, classes), lambda j: (0, 0))
    block = pl.BlockSpec((layers, rows, cols), lambda j: (0, j, 0))
    pair = pl.BlockSpec((2, rows, cols), lambda j: (0, j, 0))
    msg = jax.ShapeDtypeStruct((blocks, 3, SUB, cols), jnp.float32)
    msg_spec = pl.BlockSpec((blocks, 3, SUB, cols), lambda j: (0, 0, 0, 0))
    layer2 = jax.ShapeDtypeStruct((2, nrows, cols), jnp.float32)
    size = layers * nrows * cols
    return pl.pallas_call(
        soil_kernel,
        grid=(nrows // rows,),
        in_specs=[whole, whole, whole, block, block, block],
        out_specs=[block, msg_spec, msg_spec, pair, pair],
        out_shape=[jax.ShapeDtypeStruct((layers, nrows, cols), jnp.float32), msg, msg, layer2, layer2],
        scratch_shapes=[
            pltpu.VMEM((3, SUB, LANE), jnp.float32),
            pltpu.VMEM((rows // SUB, 3, SUB, cols), jnp.float32),
        ],
        compiler_params=params(56),
        cost_estimate=cost(60 * size, 20 * size, size),
        name="soil",
    )(k_sat[None], alpha[None], theta_sat[None], pressure, texture, active)


def lane_group(shape, start):
    lane = lax.broadcasted_iota(jnp.int32, shape, len(shape) - 1)
    return (lane >= start) & (lane < start + SUB)


def edge_lane(chip):
    return (1 - chip) * (LANE - SUB)


def tile_rows(own_ref, other_ref, core, which, array, first, width):
    mine = own_ref[array, pl.ds(first, SUB), width[0] : width[0] + width[1]]
    theirs = other_ref[array, pl.ds(first, SUB), width[0] : width[0] + width[1]]
    return jnp.where(core == which, mine, theirs)


def pack_kernel(keep_ref, recv_ref, own_ref, other_ref, out_ref, edge_ref):
    chip, core = place()
    blocks, _, _, cols = keep_ref.shape
    half = cols // 2
    tile = half // 2
    away = pl.ds(pl.multiple_of((1 - chip) * half, half), half)
    edge = core * (blocks - 1)
    for j in range(blocks - 1):
        b = j + (1 - core)
        out_ref[j] = keep_ref[b, :, :, away] + recv_ref[b, :, :, away]
    edge_ref[:3] = keep_ref[edge, :, :, away] + recv_ref[edge, :, :, away]
    slab = pl.ds(pl.multiple_of(half - LANE + chip * LANE, LANE), LANE)
    per = half // LANE
    base = edge_lane(chip)
    shape = (SUB, LANE)
    for b in range(blocks):
        first = pl.multiple_of(core * (blocks - 2) * SUB + b * SUB, SUB)
        packed = jnp.zeros(shape, jnp.float32)
        for a in range(6):
            if a < 3:
                piece = keep_ref[b, a, :, slab] + recv_ref[b, a, :, slab]
            else:
                left = tile_rows(own_ref, other_ref, core, 1, a - 3, first, (tile - LANE, LANE))
                right = tile_rows(own_ref, other_ref, core, 0, a - 3, first, (0, LANE))
                piece = jnp.where(chip == 0, left, right)
            piece = jnp.where(lane_group(shape, base), piece, 0.0)
            packed = packed + (pltpu.roll(piece, SUB * a, 1) if a else piece)
        edge_ref[3 + b // per, :, (b % per) * LANE : (b % per + 1) * LANE] = packed


def pack(keep, recv, own, other):
    blocks, _, _, cols = keep.shape
    half = cols // 2
    planes = 3 + -(-blocks // (half // LANE))
    return pl.pallas_call(
        pack_kernel,
        in_specs=[VMEM] * 4,
        out_specs=[VMEM] * 2,
        out_shape=[
            jax.ShapeDtypeStruct((blocks - 1, 3, SUB, half), jnp.float32),
            jax.ShapeDtypeStruct((planes, SUB, half), jnp.float32),
        ],
        compiler_params=params(24),
        cost_estimate=cost(keep.size, 12 * keep.size),
        name="pack",
    )(keep, recv, own, other)


def cells(keep_ref, recv_ref, own_ref, other_ref, far_ref, edge_ref, b, chip, core, put):
    blocks, _, _, cols = keep_ref.shape
    half = cols // 2
    tile = half // 2
    per = half // LANE
    near = pl.ds(pl.multiple_of(chip * half, half), half)
    first = pl.multiple_of(core * (blocks - 2) * SUB + b * SUB, SUB)

    def finish(sums, old, river, inflow, mask):
        trans = sums[0] * layer_thick
        store = spec_yield + sums[1] * layer_thick
        base = store + river
        rhs = store * old + leak_rate * layer_thick * sums[2] + inflow
        if mask is None:
            return trans, base, rhs, old
        zero = jnp.zeros_like(trans)
        return (
            jnp.where(mask, trans, zero),
            jnp.where(mask, base, zero + 1.0),
            jnp.where(mask, rhs, zero),
            jnp.where(mask, old, zero),
        )

    sums = [keep_ref[b, a, :, near] + recv_ref[b, a, :, near] + far_ref(a) for a in range(3)]
    for which in range(2):
        lanes = slice(which * tile, (which + 1) * tile)
        ins = [tile_rows(own_ref, other_ref, core, which, a, first, (0, tile)) for a in range(3)]
        for i, value in enumerate(finish([s[:, lanes] for s in sums], *ins, None)):
            put(i, lanes, value)
    slab = pl.ds(pl.multiple_of(half - chip * LANE, LANE), LANE)
    shape = (SUB, LANE)
    base = edge_lane(1 - chip)
    plane = 3 + b // per
    at = pl.ds(pl.multiple_of((b % per) * LANE, LANE), LANE)
    packed = edge_ref[plane, :, at]
    unpacked = [pltpu.roll(packed, LANE - SUB * a, 1) if a else packed for a in range(6)]
    sums = [keep_ref[b, a, :, slab] + recv_ref[b, a, :, slab] + unpacked[a] for a in range(3)]
    for i, value in enumerate(finish(sums, *unpacked[3:], lane_group(shape, base))):
        put(i, slice(half, half + LANE), value)


def rim_kernel(keep_ref, recv_ref, own_ref, other_ref, edge_ref, out_ref):
    chip, core = place()
    blocks = keep_ref.shape[0]

    def put(i, lanes, value):
        out_ref[i, :, lanes] = value

    cells(
        keep_ref, recv_ref, own_ref, other_ref, lambda a: edge_ref[a], edge_ref,
        core * (blocks - 1), chip, core, put,
    )


def rim(keep, recv, own, other, edge):
    half = keep.shape[3] // 2
    return pl.pallas_call(
        rim_kernel,
        in_specs=[VMEM] * 5,
        out_specs=VMEM,
        out_shape=jax.ShapeDtypeStruct((4, SUB, half + LANE), jnp.float32),
        compiler_params=params(24),
        cost_estimate=cost(keep.size, 8 * keep.size),
        name="rim",
    )(keep, recv, own, other, edge)


def sweep_kernel(keep_ref, recv_ref, own_ref, other_ref, far_ref, edge_ref, rim_ref, out_ref, work):
    chip, core = place()
    strip = lax.axis_index("strips")
    blocks = keep_ref.shape[0]
    half = keep_ref.shape[3] // 2
    edge = core * (blocks - 1)
    for b in range(blocks):
        row = jnp.clip(b - (1 - core), 0, blocks - 2)

        def far(a):
            return jnp.where(b == edge, edge_ref[a], far_ref[row, a])

        def put(i, lanes, value):
            work[i, b * SUB : (b + 1) * SUB, lanes] = value

        cells(keep_ref, recv_ref, own_ref, other_ref, far, edge_ref, b, chip, core, put)
    outside = ((core == 0) & (strip == 0)) | ((core == 1) & (strip == lax.axis_size("strips") - 1))
    for i in range(4):
        work[i, blocks * SUB :, :] = jnp.where(outside, 1.0 if i == 1 else 0.0, rim_ref[i])

    trans, base, rhs, head = (work[i] for i in range(4))
    rows, lanes = trans.shape
    right = jnp.sqrt(trans * pltpu.roll(trans, lanes - 1, 1))
    left = pltpu.roll(right, 1, 1)
    down = jnp.sqrt(trans * pltpu.roll(trans, rows - 1, 0))
    up = pltpu.roll(down, 1, 0)
    inverse = 1.0 / (base + right + left + down + up)
    for _ in range(SWEEPS):
        head = inverse * (
            rhs
            + right * pltpu.roll(head, lanes - 1, 1)
            + left * pltpu.roll(head, 1, 1)
            + down * pltpu.roll(head, rows - 1, 0)
            + up * pltpu.roll(head, 1, 0)
        )
    work[0] = head
    out_ref[...] = work[0, pl.ds(pl.multiple_of(core * SUB, SUB), out_ref.shape[0]), :half]


def sweeps(keep, recv, own, other, far, edge, rim_rows):
    blocks = keep.shape[0]
    half = keep.shape[3] // 2
    return pl.pallas_call(
        sweep_kernel,
        in_specs=[VMEM] * 7,
        out_specs=VMEM,
        out_shape=jax.ShapeDtypeStruct(((blocks - 1) * SUB, half), jnp.float32),
        scratch_shapes=[pltpu.VMEM((4, (blocks + 1) * SUB, half + LANE), jnp.float32)],
        compiler_params=params(24),
        cost_estimate=cost(20 * keep.size, 12 * keep.size),
        name="sweeps",
    )(keep, recv, own, other, far, edge, rim_rows)


def faces_kernel(moist_in, core_ref, chip_ref, core_far, chip_far, rain_ref, moist_out, ends, sems):
    del moist_in
    chip, core = place()
    layers = moist_out.shape[0]
    loads = [
        pltpu.make_async_copy(moist_out.at[layer], ends.at[i], sems.at[i])
        for i, layer in enumerate((0, layers - 1))
    ]
    for c in loads:
        c.start()
    for c in loads:
        c.wait()
    gain = soil_step / layer_thick
    face = 0.5 * gain

    def flux(upper, lower):
        return (upper[1] + lower[1]) * ((upper[0] - lower[0]) * (face / layer_thick) + face)

    @pl.when(core == 0)
    def _():
        ends[1] = ends[1] - flux(core_ref, core_far)

    @pl.when(core == 1)
    def _():
        ends[0] = ends[0] + flux(core_far, core_ref)

    @pl.when((core == 0) & (chip == 0))
    def _():
        ends[0] = ends[0] + gain * rain_ref[...]

    @pl.when((core == 0) & (chip == 1))
    def _():
        ends[0] = ends[0] + flux(chip_far, chip_ref)

    @pl.when((core == 1) & (chip == 0))
    def _():
        ends[1] = ends[1] - flux(chip_ref, chip_far)

    stores = [
        pltpu.make_async_copy(ends.at[i], moist_out.at[layer], sems.at[i])
        for i, layer in enumerate((0, layers - 1))
    ]
    for c in stores:
        c.start()
    for c in stores:
        c.wait()


def faces(moist, core_pair, chip_pair, core_far, chip_far, rain):
    return pl.pallas_call(
        faces_kernel,
        in_specs=[ANY] + [VMEM] * 5,
        out_specs=ANY,
        out_shape=jax.ShapeDtypeStruct(moist.shape, moist.dtype),
        input_output_aliases={0: 0},
        scratch_shapes=[pltpu.VMEM((2,) + moist.shape[1:], jnp.float32), pltpu.SemaphoreType.DMA((2,))],
        compiler_params=params(24),
        cost_estimate=cost(20 * rain.size, 32 * rain.size),
        name="faces",
    )(moist, core_pair, chip_pair, core_far, chip_far, rain)


def bottom_kernel(
    moist_in, chip_pair, own_ref, core_far, chip_far, both_far, moist_out, head_ref, last, sem
):
    del moist_in
    chip, core = place()
    layers = moist_out.shape[0]
    rows, half = own_ref.shape
    tile = half // 2
    mine = pl.ds(pl.multiple_of(core * rows, rows), rows)
    theirs = pl.ds(pl.multiple_of((1 - core) * rows, rows), rows)

    @pl.when((core == 1) & (chip == 1))
    def _():
        load = pltpu.make_async_copy(moist_out.at[layers - 1], last, sem)
        load.start()
        load.wait()
        gain = soil_step / layer_thick
        for ref, where, lanes in (
            (own_ref, mine, slice(half, 2 * half)),
            (core_far, theirs, slice(half, 2 * half)),
            (chip_far, mine, slice(0, half)),
            (both_far, theirs, slice(0, half)),
        ):
            drop = (chip_pair[0, where, lanes] - ref[...]) / (0.5 * layer_thick) + 1.0
            last[where, lanes] = last[where, lanes] - gain * chip_pair[1, where, lanes] * drop
        store = pltpu.make_async_copy(last, moist_out.at[layers - 1], sem)
        store.start()
        store.wait()

    lanes = pl.ds(pl.multiple_of(core * tile, tile), tile)
    head_ref[mine, :] = own_ref[:, lanes]
    head_ref[theirs, :] = core_far[:, lanes]


def bottom(moist, chip_pair, own, core_far, chip_far, both_far):
    rows, half = own.shape
    return pl.pallas_call(
        bottom_kernel,
        in_specs=[ANY] + [VMEM] * 5,
        out_specs=[ANY, VMEM],
        out_shape=[
            jax.ShapeDtypeStruct(moist.shape, moist.dtype),
            jax.ShapeDtypeStruct((2 * rows, half // 2), jnp.float32),
        ],
        input_output_aliases={0: 0},
        scratch_shapes=[pltpu.VMEM(moist.shape[1:], jnp.float32), pltpu.SemaphoreType.DMA],
        compiler_params=params(24),
        cost_estimate=cost(10 * own.size, 40 * own.size),
        name="bottom",
    )(moist, chip_pair, own, core_far, chip_far, both_far)


def core_swap(value):
    return lax.ppermute(value, "depth", [(i, i ^ 1) for i in range(lax.axis_size("depth"))])


def chip_swap(value):
    return lax.ppermute(value, "depth", [(i, i ^ 2) for i in range(lax.axis_size("depth"))])


def middle_swap(value):
    return lax.ppermute(value, "depth", [(1, 2), (2, 1)])


def strip_swap(value):
    depth, strips = lax.axis_size("depth"), lax.axis_size("strips")
    pairs = []
    for d in range(1, depth, 2):
        for s in range(strips):
            lower, upper = d * strips + s, (d - 1) * strips + (s + 1) % strips
            pairs += [(lower, upper), (upper, lower)]
    return lax.ppermute(value, ("depth", "strips"), pairs)


def shards(pressure, texture, active, rain, k_sat, alpha, theta_sat, head_old, cell_code, section):
    river = jnp.where(
        cell_code == 1,
        jnp.float32(river_cond),
        jnp.where(cell_code == 2, jnp.float32(fixed_cond), jnp.float32(0.0)),
    )
    own = jnp.stack([head_old, river, river * section])
    other = core_swap(own)
    moist, keep, send, core_pair, chip_pair = soil(k_sat, alpha, theta_sat, pressure, texture, active)
    recv = core_swap(send)
    core_far = core_swap(core_pair)
    out, edge = pack(keep, recv, own, other)
    edge = chip_swap(edge)
    far = chip_swap(out)
    chip_far = middle_swap(chip_pair)
    rim_rows = strip_swap(rim(keep, recv, own, other, edge))
    heads = sweeps(keep, recv, own, other, far, edge, rim_rows)
    heads_chip = chip_swap(heads)
    heads_core = core_swap(heads)
    heads_both = core_swap(heads_chip)
    moist = faces(moist, core_pair, chip_pair, core_far, chip_far, rain)
    return bottom(moist, chip_pair, heads, heads_core, heads_chip, heads_both)


def solution(mesh):
    in_specs = (
        P("depth", "strips", None),
        P("depth", "strips", None),
        P("depth", "strips", None),
        P("strips", None),
        P(),
        P(),
        P(),
        P("strips", "depth"),
        P("strips", "depth"),
        P("strips", "depth"),
    )
    out_specs = (P("depth", "strips", None), P("strips", "depth"))
    return jax.shard_map(shards, mesh=mesh, in_specs=in_specs, out_specs=out_specs, check_vma=False)
```

```python
import functools
import math

import jax
import jax.numpy as jnp
from jax import lax
from jax.experimental import pallas as pl
from jax.experimental.pallas import tpu as pltpu
from jax.sharding import PartitionSpec as P

SWEEPS = 3
SUB = 8
LANE = 128
WIDTH = 4

layer_thick = 0.05
soil_step = 0.0002
spec_yield = 0.02
leak_rate = 0.5
river_cond = 0.5
fixed_cond = 3.0
residual = 0.15
mobile = 0.85

VMEM = pl.BlockSpec(memory_space=pltpu.VMEM)
ANY = pl.BlockSpec(memory_space=pl.ANY)


def params(mib):
    return pltpu.CompilerParams(vmem_limit_bytes=mib * 2**20)


def cost(flops, nbytes, trans=0):
    return pl.CostEstimate(flops=int(flops), bytes_accessed=int(nbytes), transcendentals=int(trans))


def place():
    depth = lax.axis_index("depth")
    return depth // 2, depth % 2


def gathered(table, classes):
    return jnp.take_along_axis(table, classes, axis=1, mode="promise_in_bounds")


def picked(options, bits):
    for bit in bits:
        options = [
            jnp.where(bit, options[i + 1], options[i]) if i + 1 < len(options) else options[i]
            for i in range(0, len(options), 2)
        ]
    return options[0]


def fill_tables(tab, sat_ref, alpha_ref, theta_ref):
    classes = sat_ref.shape[1]
    scaled = (sat_ref, 1.0), (alpha_ref, 0.5 * math.log2(math.e)), (theta_ref, mobile)
    for i, (ref, scale) in enumerate(scaled):
        tab[i, :, :classes] = jnp.broadcast_to(ref[...] * scale, (SUB, classes))


def face_kernel(sat_ref, alpha_ref, theta_ref, psi_hbm, tex_hbm, act_hbm, out_ref, kinds, acts, tab, sems):
    _, core = place()
    layer = core * (psi_hbm.shape[0] - 1)
    nrows, cols = psi_hbm.shape[1:]
    chunk = nrows // 4

    def copies(i):
        rows = pl.ds(i * chunk, chunk)
        return [
            pltpu.make_async_copy(src.at[layer, rows], dst.at[rows], sems.at[i, k])
            for k, (src, dst) in enumerate(
                ((psi_hbm, out_ref.at[0]), (tex_hbm, kinds), (act_hbm, acts))
            )
        ]

    for i in range(4):
        for c in copies(i):
            c.start()
    fill_tables(tab, sat_ref, alpha_ref, theta_ref)
    for i in range(4):
        for c in copies(i):
            c.wait()

        def columns(q, carry):
            lanes = pl.ds(pl.multiple_of(q * LANE, LANE), LANE)
            for r in range(i * chunk, (i + 1) * chunk, SUB):
                rws = slice(r, r + SUB)
                kind = kinds[rws, lanes]
                wet = jnp.exp2(gathered(tab[1], kind) * jnp.minimum(out_ref[0, rws, lanes], 0.0))
                active = acts[rws, lanes].astype(jnp.float32)
                out_ref[1, rws, lanes] = gathered(tab[0], kind) * active * (wet * wet)
            return carry

        lax.fori_loop(0, cols // LANE, columns, 0, unroll=4)


def in_hbm(*arrays):
    return [pltpu.with_memory_space_constraint(x, pltpu.HBM) for x in arrays]


def face(tables, pressure, texture, active):
    _, nrows, cols = pressure.shape
    size = nrows * cols
    return pl.pallas_call(
        face_kernel,
        grid=(1,),
        in_specs=[pl.BlockSpec(t.shape, lambda j: (0, 0)) for t in tables]
        + [pl.BlockSpec(memory_space=pltpu.HBM)] * 3,
        out_specs=pl.BlockSpec((2, nrows, cols), lambda j: (0, 0, 0)),
        out_shape=jax.ShapeDtypeStruct((2, nrows, cols), jnp.float32),
        scratch_shapes=[
            pltpu.VMEM((nrows, cols), jnp.int32),
            pltpu.VMEM((nrows, cols), jnp.int32),
            pltpu.VMEM((3, SUB, LANE), jnp.float32),
            pltpu.SemaphoreType.DMA((4, 3)),
        ],
        compiler_params=params(8),
        cost_estimate=cost(20 * size, 20 * size, size),
        name="face",
    )(*in_hbm(*tables, pressure, texture, active))


def soil_kernel(
    sat_ref, alpha_ref, theta_ref, psi_ref, tex_ref, act_ref,
    moist_ref, keep_ref, send_ref, core_ref, tab, part,
):
    step = pl.program_id(0)
    _, core = place()
    layers, rows, cols = psi_ref.shape
    classes = sat_ref.shape[1]

    @pl.when(step == 0)
    def _():
        fill_tables(tab, sat_ref, alpha_ref, theta_ref)

    sat_tab, par_tab = tab[0], tab[1]
    theta = [jnp.broadcast_to(tab[2, :, i : i + 1], (SUB, LANE)) for i in range(classes)]
    nbits = max(1, (classes - 1).bit_length())
    face = 0.5 * soil_step / layer_thick
    core_layer = (1 - core) * (layers - 1)

    def columns(q, carry):
        lanes = pl.ds(pl.multiple_of(q * LANE, LANE), LANE)
        for r in range(0, rows, SUB):
            rws = slice(r, r + SUB)
            trans = store = charge = jnp.zeros((SUB, LANE), jnp.float32)
            for layer in range(layers):
                kind = tex_ref[layer, rws, lanes]
                psi = psi_ref[layer, rws, lanes]
                active = act_ref[layer, rws, lanes].astype(jnp.float32)
                bits = [(kind & (1 << b)) != 0 for b in range(nbits)]
                wet = jnp.exp2(gathered(par_tab, kind) * jnp.minimum(psi, 0.0))
                cond = gathered(sat_tab, kind) * active * (wet * wet)
                mob = picked(theta, bits)
                mobwet = mob * wet
                trans = trans + cond
                charge = charge + cond * wet
                store = store + (mob - mobwet)
                held = mob * (residual / mobile) + mobwet
                if layer == 0:
                    first, own = cond, held
                else:
                    flux = (cond_up + cond) * ((psi_up - psi) * (face / layer_thick) + face)
                    moist_ref[layer - 1, rws, lanes] = own - flux
                    own = held + flux
                psi_up, cond_up = psi, cond
            moist_ref[layers - 1, rws, lanes] = own
            part[r // SUB, 0, :, lanes] = trans
            part[r // SUB, 1, :, lanes] = store
            part[r // SUB, 2, :, lanes] = charge
            core_ref[0, rws, lanes] = psi_ref[core_layer, rws, lanes]
            core_ref[1, rws, lanes] = jnp.where(core == 0, cond, first)
        return carry

    lax.fori_loop(0, cols // LANE, columns, 0, unroll=4)

    blocks = rows // SUB
    half = keep_ref.shape[0] - 1
    for r in range(blocks):
        block = step * blocks + r

        def put(ref, at):
            ref[at] = part[r]

        @pl.when((block <= half) & (core == 0))
        def _():
            put(keep_ref, block)

        @pl.when((block <= half) & (core == 1))
        def _():
            put(send_ref, block)

        @pl.when((block >= half - 1) & (core == 0))
        def _():
            put(send_ref, block - (half - 1))

        @pl.when((block >= half - 1) & (core == 1))
        def _():
            put(keep_ref, block - (half - 1))


def soil(tables, pressure, texture, active):
    layers, nrows, cols = pressure.shape
    classes = tables[0].shape[1]
    rows = nrows // 4
    blocks = nrows // (2 * SUB) + 1
    whole = pl.BlockSpec((1, classes), lambda j: (0, 0))
    block = pl.BlockSpec((layers, rows, cols), lambda j: (0, j, 0))
    pair = pl.BlockSpec((2, rows, cols), lambda j: (0, j, 0))
    msg = jax.ShapeDtypeStruct((blocks, 3, SUB, cols), jnp.float32)
    msg_spec = pl.BlockSpec((blocks, 3, SUB, cols), lambda j: (0, 0, 0, 0))
    layer2 = jax.ShapeDtypeStruct((2, nrows, cols), jnp.float32)
    size = layers * nrows * cols
    return pl.pallas_call(
        soil_kernel,
        grid=(nrows // rows,),
        in_specs=[whole, whole, whole, block, block, block],
        out_specs=[block, msg_spec, msg_spec, pair],
        out_shape=[jax.ShapeDtypeStruct((layers, nrows, cols), jnp.float32), msg, msg, layer2],
        scratch_shapes=[
            pltpu.VMEM((3, SUB, LANE), jnp.float32),
            pltpu.VMEM((rows // SUB, 3, SUB, cols), jnp.float32),
        ],
        compiler_params=params(32),
        cost_estimate=cost(60 * size, 20 * size, size),
        name="soil",
    )(*in_hbm(*tables, pressure, texture, active))


def edge_lane(chip):
    return (1 - chip) * (LANE - WIDTH)


def on_edge(value, chip):
    lane = lax.broadcasted_iota(jnp.int32, value.shape, 1)
    base = edge_lane(chip)
    return jnp.where((lane >= base) & (lane < base + WIDTH), value, 0.0)


def shift(array, block=0):
    return WIDTH * (6 * block + array)


SHARE = LANE // (6 * WIDTH)


def packed(pieces, chip, block=0):
    total = None
    for a, piece in enumerate(pieces):
        moved = pltpu.roll(on_edge(piece, chip), shift(a, block), 1)
        total = moved if total is None else total + moved
    return total


def unpacked(tile, array, block=0):
    return pltpu.roll(tile, LANE - shift(array, block), 1)


def half_lanes(which, half):
    return pl.ds(pl.multiple_of(which * half, half), half)


def slab_lanes(chip, half):
    return pl.ds(pl.multiple_of(half - LANE + chip * LANE, LANE), LANE)


def first_row(core, blocks, b):
    return pl.multiple_of((core * (blocks - 2) + b) * SUB, SUB)


def tile_rows(own_ref, other_ref, core, which, array, first, lanes):
    mine = own_ref[array, pl.ds(first, SUB), lanes]
    theirs = other_ref[array, pl.ds(first, SUB), lanes]
    return jnp.where(core == which, mine, theirs)


def edge_inputs(own_ref, other_ref, chip, core, first):
    tile = own_ref.shape[2]
    out = []
    for a in range(3):
        left = tile_rows(own_ref, other_ref, core, 1, a, first, slice(tile - LANE, tile))
        right = tile_rows(own_ref, other_ref, core, 0, a, first, slice(0, LANE))
        out.append(jnp.where(chip == 0, left, right))
    return out


def pack_kernel(keep_ref, recv_ref, own_ref, other_ref, out_ref):
    chip, core = place()
    blocks, _, _, cols = keep_ref.shape
    half = cols // 2
    away = half_lanes(1 - chip, half)
    slab = slab_lanes(chip, half)
    tiles = [None] * -(-blocks // SHARE)
    for b in range(blocks):
        out_ref[3 * b : 3 * b + 3] = keep_ref[b, :, :, away] + recv_ref[b, :, :, away]
        pieces = [keep_ref[b, a, :, slab] + recv_ref[b, a, :, slab] for a in range(3)]
        pieces += edge_inputs(own_ref, other_ref, chip, core, first_row(core, blocks, b))
        piece = packed(pieces, chip, b % SHARE)
        i = b // SHARE
        tiles[i] = piece if tiles[i] is None else tiles[i] + piece
    per = half // LANE
    for i, tile in enumerate(tiles):
        out_ref[3 * blocks + i // per, :, (i % per) * LANE : (i % per + 1) * LANE] = tile


def pack(keep, recv, own, other):
    blocks, _, _, cols = keep.shape
    half = cols // 2
    tiles = -(-blocks // SHARE)
    planes = 3 * blocks - (-tiles // (half // LANE))
    return pl.pallas_call(
        pack_kernel,
        in_specs=[VMEM] * 4,
        out_specs=VMEM,
        out_shape=jax.ShapeDtypeStruct((planes, SUB, half), jnp.float32),
        compiler_params=params(8),
        cost_estimate=cost(keep.size, 12 * keep.size),
        name="pack",
    )(keep, recv, own, other)


def rim_kernel(keep_ref, recv_ref, own_ref, other_ref, first, side_ref, cross_ref):
    del first
    chip, core = place()
    blocks, _, _, cols = keep_ref.shape
    half = cols // 2
    tile = half // 2
    b = core * (blocks - 1)
    row = first_row(core, blocks, b)
    near, away = half_lanes(chip, half), half_lanes(1 - chip, half)
    side_ref[:3] = keep_ref[b, :, :, near] + recv_ref[b, :, :, near]
    cross_ref[:3] = keep_ref[b, :, :, away] + recv_ref[b, :, :, away]
    for which in range(2):
        for a in range(3):
            side_ref[3 + a, :, which * tile : (which + 1) * tile] = tile_rows(
                own_ref, other_ref, core, which, a, row, slice(0, tile)
            )

    def sums(slab):
        return [keep_ref[b, a, :, slab] + recv_ref[b, a, :, slab] for a in range(3)]

    side_ref[6, :, :LANE] = packed(sums(slab_lanes(1 - chip, half)), 1 - chip)
    inputs = edge_inputs(own_ref, other_ref, chip, core, row)
    cross_ref[3, :, :LANE] = packed(sums(slab_lanes(chip, half)) + inputs, chip)


def rim(keep, recv, own, other, first):
    half = keep.shape[3] // 2
    return pl.pallas_call(
        rim_kernel,
        in_specs=[VMEM] * 4 + [ANY],
        out_specs=[VMEM] * 2,
        out_shape=[jax.ShapeDtypeStruct((n, SUB, half), jnp.float32) for n in (7, 4)],
        compiler_params=params(8),
        cost_estimate=cost(keep.size // 8, keep.size),
        name="rim",
    )(keep, recv, own, other, first)


def sweep_kernel(keep_ref, recv_ref, own_ref, other_ref, far_ref, side_ref, cross_ref, first, out_ref, work):
    del first
    chip, core = place()
    strip = lax.axis_index("strips")
    blocks, _, _, cols = keep_ref.shape
    half = cols // 2
    tile = half // 2
    per = half // LANE

    def cells(at, lanes, sums, inputs):
        trans = sums[0] * layer_thick
        store = spec_yield + sums[1] * layer_thick
        old, river, inflow = inputs
        rows = slice(at * SUB, (at + 1) * SUB)
        work[0, rows, lanes] = trans
        work[1, rows, lanes] = store + river
        work[2, rows, lanes] = store * old + leak_rate * layer_thick * sums[2] + inflow
        work[3, rows, lanes] = old

    def halo(at, sums, inputs):
        cells(at, slice(half, half + LANE), [on_edge(v, 1 - chip) for v in sums], [on_edge(v, 1 - chip) for v in inputs])

    near, slab = half_lanes(chip, half), slab_lanes(1 - chip, half)
    for b in range(blocks):
        sums = [keep_ref[b, a, :, near] + recv_ref[b, a, :, near] + far_ref[3 * b + a] for a in range(3)]
        first_at = first_row(core, blocks, b)
        for which in range(2):
            lanes = slice(which * tile, (which + 1) * tile)
            inputs = [tile_rows(own_ref, other_ref, core, which, a, first_at, slice(0, tile)) for a in range(3)]
            cells(b, lanes, [s[:, lanes] for s in sums], inputs)
        i = b // SHARE
        far = far_ref[3 * blocks + i // per, :, (i % per) * LANE : (i % per + 1) * LANE]
        far = [unpacked(far, a, b % SHARE) for a in range(6)]
        sums = [keep_ref[b, a, :, slab] + recv_ref[b, a, :, slab] + far[a] for a in range(3)]
        halo(b, sums, far[3:])
    outside = ((core == 0) & (strip == 0)) | ((core == 1) & (strip == lax.axis_size("strips") - 1))

    def inside(value):
        return jnp.where(outside, 0.0, value)

    sums = [inside(side_ref[a] + cross_ref[a]) for a in range(3)]
    cells(blocks, slice(0, half), sums, [inside(side_ref[3 + a]) for a in range(3)])
    side, cross = side_ref[6, :, :LANE], cross_ref[3, :, :LANE]
    sums = [inside(unpacked(side, a) + unpacked(cross, a)) for a in range(3)]
    halo(blocks, sums, [inside(unpacked(cross, a)) for a in range(3, 6)])

    trans, base, rhs, head = (work[i] for i in range(4))
    rows, lanes = trans.shape
    right = jnp.sqrt(trans * pltpu.roll(trans, lanes - 1, 1))
    left = pltpu.roll(right, 1, 1)
    down = jnp.sqrt(trans * pltpu.roll(trans, rows - 1, 0))
    up = pltpu.roll(down, 1, 0)
    inverse = 1.0 / (base + right + left + down + up)
    for _ in range(SWEEPS):
        head = inverse * (
            rhs
            + right * pltpu.roll(head, lanes - 1, 1)
            + left * pltpu.roll(head, 1, 1)
            + down * pltpu.roll(head, rows - 1, 0)
            + up * pltpu.roll(head, 1, 0)
        )
    work[0] = head
    out_ref[...] = work[0, pl.ds(pl.multiple_of(core * SUB, SUB), out_ref.shape[0]), :half]


def sweeps(keep, recv, own, other, far, side, cross, first):
    blocks = keep.shape[0]
    half = keep.shape[3] // 2
    return pl.pallas_call(
        sweep_kernel,
        in_specs=[VMEM] * 7 + [pl.BlockSpec(memory_space=pltpu.HBM)],
        out_specs=VMEM,
        out_shape=jax.ShapeDtypeStruct(((blocks - 1) * SUB, half), jnp.float32),
        scratch_shapes=[pltpu.VMEM((4, (blocks + 1) * SUB, half + LANE), jnp.float32)],
        compiler_params=params(12),
        cost_estimate=cost(20 * keep.size, 12 * keep.size),
        name="sweeps",
    )(keep, recv, own, other, far, side, cross, *in_hbm(first))


def faces_kernel(moist_in, core_ref, chip_ref, core_far, chip_far, rain_ref, moist_out, ends, sems):
    del moist_in
    chip, core = place()
    layers = moist_out.shape[0]
    loads = [
        pltpu.make_async_copy(moist_out.at[layer], ends.at[i], sems.at[i])
        for i, layer in enumerate((0, layers - 1))
    ]
    for c in loads:
        c.start()
    for c in loads:
        c.wait()
    gain = soil_step / layer_thick
    face = 0.5 * gain

    def flux(upper, lower):
        return (upper[1] + lower[1]) * ((upper[0] - lower[0]) * (face / layer_thick) + face)

    @pl.when(core == 0)
    def _():
        ends[1] = ends[1] - flux(core_ref, core_far)

    @pl.when(core == 1)
    def _():
        ends[0] = ends[0] + flux(core_far, core_ref)

    @pl.when((core == 0) & (chip == 0))
    def _():
        ends[0] = ends[0] + gain * rain_ref[...]

    @pl.when((core == 0) & (chip == 1))
    def _():
        ends[0] = ends[0] + flux(chip_far, chip_ref)

    @pl.when((core == 1) & (chip == 0))
    def _():
        ends[1] = ends[1] - flux(chip_ref, chip_far)

    stores = [
        pltpu.make_async_copy(ends.at[i], moist_out.at[layer], sems.at[i])
        for i, layer in enumerate((0, layers - 1))
    ]
    for c in stores:
        c.start()
    for c in stores:
        c.wait()


def faces(moist, core_pair, chip_pair, core_far, chip_far, rain):
    return pl.pallas_call(
        faces_kernel,
        in_specs=[ANY] + [VMEM] * 5,
        out_specs=ANY,
        out_shape=jax.ShapeDtypeStruct(moist.shape, moist.dtype),
        input_output_aliases={0: 0},
        scratch_shapes=[pltpu.VMEM((2,) + moist.shape[1:], jnp.float32), pltpu.SemaphoreType.DMA((2,))],
        compiler_params=params(12),
        cost_estimate=cost(20 * rain.size, 32 * rain.size),
        name="faces",
    )(moist, core_pair, chip_pair, core_far, chip_far, rain)


def bottom_kernel(
    moist_in, chip_pair, own_ref, core_far, chip_far, both_far, moist_out, head_ref, last, sem
):
    del moist_in
    chip, core = place()
    layers = moist_out.shape[0]
    rows, half = own_ref.shape
    tile = half // 2
    mine = pl.ds(pl.multiple_of(core * rows, rows), rows)
    theirs = pl.ds(pl.multiple_of((1 - core) * rows, rows), rows)

    @pl.when((core == 1) & (chip == 1))
    def _():
        load = pltpu.make_async_copy(moist_out.at[layers - 1], last, sem)
        load.start()
        load.wait()
        gain = soil_step / layer_thick
        for ref, where, lanes in (
            (own_ref, mine, slice(half, 2 * half)),
            (core_far, theirs, slice(half, 2 * half)),
            (chip_far, mine, slice(0, half)),
            (both_far, theirs, slice(0, half)),
        ):
            drop = (chip_pair[0, where, lanes] - ref[...]) / (0.5 * layer_thick) + 1.0
            last[where, lanes] = last[where, lanes] - gain * chip_pair[1, where, lanes] * drop
        store = pltpu.make_async_copy(last, moist_out.at[layers - 1], sem)
        store.start()
        store.wait()

    lanes = pl.ds(pl.multiple_of(core * tile, tile), tile)
    head_ref[mine, :] = own_ref[:, lanes]
    head_ref[theirs, :] = core_far[:, lanes]


def bottom(moist, chip_pair, own, core_far, chip_far, both_far):
    rows, half = own.shape
    return pl.pallas_call(
        bottom_kernel,
        in_specs=[ANY] + [VMEM] * 5,
        out_specs=[ANY, VMEM],
        out_shape=[
            jax.ShapeDtypeStruct(moist.shape, moist.dtype),
            jax.ShapeDtypeStruct((2 * rows, half // 2), jnp.float32),
        ],
        input_output_aliases={0: 0},
        scratch_shapes=[pltpu.VMEM(moist.shape[1:], jnp.float32), pltpu.SemaphoreType.DMA],
        compiler_params=params(12),
        cost_estimate=cost(10 * own.size, 40 * own.size),
        name="bottom",
    )(moist, chip_pair, own, core_far, chip_far, both_far)


def gate_kernel(*refs):
    del refs


def gate(value, *first):
    return pl.pallas_call(
        gate_kernel,
        in_specs=[ANY] * (1 + len(first)),
        out_specs=ANY,
        out_shape=jax.ShapeDtypeStruct(value.shape, value.dtype),
        input_output_aliases={0: 0},
        compiler_params=params(1),
        cost_estimate=cost(1, 1),
        name="gate",
    )(value, *first)


def core_swap(value):
    return lax.ppermute(value, "depth", [(i, i ^ 1) for i in range(lax.axis_size("depth"))])


def chip_swap(value):
    return lax.ppermute(value, "depth", [(i, i ^ 2) for i in range(lax.axis_size("depth"))])


def middle_swap(value):
    return lax.ppermute(value, "depth", [(1, 2), (2, 1)])


def strip_swap(value, chips=0):
    depth, strips = lax.axis_size("depth"), lax.axis_size("strips")
    pairs = []
    for d in range(1, depth, 2):
        for s in range(strips):
            lower, upper = d * strips + s, ((d - 1) ^ chips) * strips + (s + 1) % strips
            pairs += [(lower, upper), (upper, lower)]
    return lax.ppermute(value, ("depth", "strips"), pairs)


def shards(pressure, texture, active, rain, k_sat, alpha, theta_sat, head_old, cell_code, section):
    river = jnp.where(
        cell_code == 1,
        jnp.float32(river_cond),
        jnp.where(cell_code == 2, jnp.float32(fixed_cond), jnp.float32(0.0)),
    )
    own = jnp.stack([head_old, river, river * section])
    other = core_swap(own)
    tables = (k_sat[None], alpha[None], theta_sat[None])
    chip_pair = face(tables, pressure, texture, active)
    chip_far = middle_swap(chip_pair)
    moist, keep, send, core_pair = soil(tables, pressure, texture, active)
    recv = core_swap(gate(send, chip_far, other))
    message = pack(keep, recv, own, other)
    far = chip_swap(message)
    side, cross = rim(keep, recv, own, other, message)
    side, cross = strip_swap(side), strip_swap(cross, 2)
    core_far = core_swap(gate(core_pair, message))
    moist = faces(moist, core_pair, chip_pair, core_far, chip_far, rain)
    heads = sweeps(keep, recv, own, other, far, side, cross, moist)
    heads_chip = chip_swap(heads)
    heads_core = core_swap(heads)
    heads_both = core_swap(heads_chip)
    return bottom(moist, chip_pair, heads, heads_core, heads_chip, heads_both)


def solution(mesh):
    in_specs = (
        P("depth", "strips", None),
        P("depth", "strips", None),
        P("depth", "strips", None),
        P("strips", None),
        P(),
        P(),
        P(),
        P("strips", "depth"),
        P("strips", "depth"),
        P("strips", "depth"),
    )
    out_specs = (P("depth", "strips", None), P("strips", "depth"))
    return jax.shard_map(shards, mesh=mesh, in_specs=in_specs, out_specs=out_specs, check_vma=False)
```

```python
import functools
import math

import jax
import jax.numpy as jnp
from jax import lax
from jax.experimental import pallas as pl
from jax.experimental.pallas import tpu as pltpu
from jax.sharding import PartitionSpec as P

SWEEPS = 3
SUB = 8
LANE = 128
WIDTH = 4

layer_thick = 0.05
soil_step = 0.0002
spec_yield = 0.02
leak_rate = 0.5
river_cond = 0.5
fixed_cond = 3.0
residual = 0.15
mobile = 0.85

VMEM = pl.BlockSpec(memory_space=pltpu.VMEM)
ANY = pl.BlockSpec(memory_space=pl.ANY)
HBM = pl.BlockSpec(memory_space=pltpu.HBM)


def params(mib):
    return pltpu.CompilerParams(vmem_limit_bytes=mib * 2**20)


def cost(flops, nbytes, trans=0):
    return pl.CostEstimate(flops=int(flops), bytes_accessed=int(nbytes), transcendentals=int(trans))


def place():
    depth = lax.axis_index("depth")
    return depth // 2, depth % 2


def gathered(table, classes):
    return jnp.take_along_axis(table, classes, axis=1, mode="promise_in_bounds")


def picked(options, bits):
    for bit in bits:
        options = [
            jnp.where(bit, options[i + 1], options[i]) if i + 1 < len(options) else options[i]
            for i in range(0, len(options), 2)
        ]
    return options[0]


def fill_tables(tab, sat_ref, alpha_ref, theta_ref):
    classes = sat_ref.shape[1]
    scaled = (sat_ref, 1.0), (alpha_ref, 0.5 * math.log2(math.e)), (theta_ref, mobile)
    for i, (ref, scale) in enumerate(scaled):
        tab[i, :, :classes] = jnp.broadcast_to(ref[...] * scale, (SUB, classes))


def face_kernel(
    sat_hbm, alpha_hbm, psi_hbm, tex_hbm, act_hbm, out_ref, kinds, acts, given, tab, sems
):
    _, core = place()
    layer = core * (psi_hbm.shape[0] - 1)
    cols = psi_hbm.shape[2]
    classes = sat_hbm.shape[1]
    copies = [
        pltpu.make_async_copy(src, dst, sems.at[i])
        for i, (src, dst) in enumerate(
            (
                (sat_hbm, given.at[0]),
                (alpha_hbm, given.at[1]),
                (psi_hbm.at[layer], out_ref.at[0]),
                (tex_hbm.at[layer], kinds),
                (act_hbm.at[layer], acts),
            )
        )
    ]
    for c in copies:
        c.start()
    for c in copies:
        c.wait()
    for i, scale in enumerate((1.0, 0.5 * math.log2(math.e))):
        tab[i, :, :classes] = jnp.broadcast_to(given[i] * scale, (SUB, classes))

    def columns(q, carry):
        lanes = pl.ds(pl.multiple_of(q * LANE, LANE), LANE)
        for r in range(0, kinds.shape[0], SUB):
            rws = slice(r, r + SUB)
            kind = kinds[rws, lanes]
            wet = jnp.exp2(gathered(tab[1], kind) * jnp.minimum(out_ref[0, rws, lanes], 0.0))
            active = acts[rws, lanes].astype(jnp.float32)
            out_ref[1, rws, lanes] = gathered(tab[0], kind) * active * (wet * wet)
        return carry

    lax.fori_loop(0, cols // LANE, columns, 0, unroll=4)


def in_hbm(*arrays):
    return [pltpu.with_memory_space_constraint(x, pltpu.HBM) for x in arrays]


def face(tables, pressure, texture, active):
    _, nrows, cols = pressure.shape
    size = nrows * cols
    return pl.pallas_call(
        face_kernel,
        in_specs=[HBM] * 5,
        out_specs=VMEM,
        out_shape=jax.ShapeDtypeStruct((2, nrows, cols), jnp.float32),
        scratch_shapes=[
            pltpu.VMEM((nrows, cols), jnp.int32),
            pltpu.VMEM((nrows, cols), jnp.int32),
            pltpu.VMEM((2,) + tables[0].shape, jnp.float32),
            pltpu.VMEM((2, SUB, LANE), jnp.float32),
            pltpu.SemaphoreType.DMA((5,)),
        ],
        compiler_params=params(8),
        cost_estimate=cost(20 * size, 20 * size, size),
        name="face",
    )(*in_hbm(*tables[:2], pressure, texture, active))


def soil_kernel(
    sat_ref, alpha_ref, theta_ref, psi_ref, tex_ref, act_ref,
    moist_ref, keep_ref, send_ref, core_ref, tab, part,
):
    step = pl.program_id(0)
    _, core = place()
    layers, rows, cols = psi_ref.shape
    classes = sat_ref.shape[1]

    @pl.when(step == 0)
    def _():
        fill_tables(tab, sat_ref, alpha_ref, theta_ref)

    sat_tab, par_tab = tab[0], tab[1]
    theta = [jnp.broadcast_to(tab[2, :, i : i + 1], (SUB, LANE)) for i in range(classes)]
    nbits = max(1, (classes - 1).bit_length())
    face = 0.5 * soil_step / layer_thick
    core_layer = (1 - core) * (layers - 1)

    def columns(q, carry):
        lanes = pl.ds(pl.multiple_of(q * LANE, LANE), LANE)
        for r in range(0, rows, SUB):
            rws = slice(r, r + SUB)
            trans = store = charge = jnp.zeros((SUB, LANE), jnp.float32)
            for layer in range(layers):
                kind = tex_ref[layer, rws, lanes]
                psi = psi_ref[layer, rws, lanes]
                active = act_ref[layer, rws, lanes].astype(jnp.float32)
                bits = [(kind & (1 << b)) != 0 for b in range(nbits)]
                wet = jnp.exp2(gathered(par_tab, kind) * jnp.minimum(psi, 0.0))
                cond = gathered(sat_tab, kind) * active * (wet * wet)
                mob = picked(theta, bits)
                mobwet = mob * wet
                trans = trans + cond
                charge = charge + cond * wet
                store = store + (mob - mobwet)
                held = mob * (residual / mobile) + mobwet
                if layer == 0:
                    first, own = cond, held
                else:
                    flux = (cond_up + cond) * ((psi_up - psi) * (face / layer_thick) + face)
                    moist_ref[layer - 1, rws, lanes] = own - flux
                    own = held + flux
                psi_up, cond_up = psi, cond
            moist_ref[layers - 1, rws, lanes] = own
            part[r // SUB, 0, :, lanes] = trans
            part[r // SUB, 1, :, lanes] = store
            part[r // SUB, 2, :, lanes] = charge
            core_ref[0, rws, lanes] = psi_ref[core_layer, rws, lanes]
            core_ref[1, rws, lanes] = jnp.where(core == 0, cond, first)
        return carry

    lax.fori_loop(0, cols // LANE, columns, 0, unroll=4)

    blocks = rows // SUB
    half = keep_ref.shape[0] - 1
    for r in range(blocks):
        block = step * blocks + r

        def put(ref, at):
            ref[at] = part[r]

        @pl.when((block <= half) & (core == 0))
        def _():
            put(keep_ref, block)

        @pl.when((block <= half) & (core == 1))
        def _():
            put(send_ref, block)

        @pl.when((block >= half - 1) & (core == 0))
        def _():
            put(send_ref, block - (half - 1))

        @pl.when((block >= half - 1) & (core == 1))
        def _():
            put(keep_ref, block - (half - 1))


def soil(tables, pressure, texture, active):
    layers, nrows, cols = pressure.shape
    classes = tables[0].shape[1]
    rows = nrows // 4
    blocks = nrows // (2 * SUB) + 1
    whole = pl.BlockSpec((1, classes), lambda j: (0, 0))
    block = pl.BlockSpec((layers, rows, cols), lambda j: (0, j, 0))
    pair = pl.BlockSpec((2, rows, cols), lambda j: (0, j, 0))
    msg = jax.ShapeDtypeStruct((blocks, 3, SUB, cols), jnp.float32)
    msg_spec = pl.BlockSpec((blocks, 3, SUB, cols), lambda j: (0, 0, 0, 0))
    layer2 = jax.ShapeDtypeStruct((2, nrows, cols), jnp.float32)
    size = layers * nrows * cols
    return pl.pallas_call(
        soil_kernel,
        grid=(nrows // rows,),
        in_specs=[whole, whole, whole, block, block, block],
        out_specs=[block, msg_spec, msg_spec, pair],
        out_shape=[jax.ShapeDtypeStruct((layers, nrows, cols), jnp.float32), msg, msg, layer2],
        scratch_shapes=[
            pltpu.VMEM((3, SUB, LANE), jnp.float32),
            pltpu.VMEM((rows // SUB, 3, SUB, cols), jnp.float32),
        ],
        compiler_params=params(32),
        cost_estimate=cost(60 * size, 20 * size, size),
        name="soil",
    )(*in_hbm(*tables, pressure, texture, active))


def edge_lane(chip):
    return (1 - chip) * (LANE - WIDTH)


def on_edge(value, chip):
    lane = lax.broadcasted_iota(jnp.int32, value.shape, 1)
    base = edge_lane(chip)
    return jnp.where((lane >= base) & (lane < base + WIDTH), value, 0.0)


def shift(array, block=0):
    return WIDTH * (6 * block + array)


SHARE = LANE // (6 * WIDTH)


def packed(pieces, chip, block=0):
    total = None
    for a, piece in enumerate(pieces):
        moved = pltpu.roll(on_edge(piece, chip), shift(a, block), 1)
        total = moved if total is None else total + moved
    return total


def unpacked(tile, array, block=0):
    return pltpu.roll(tile, LANE - shift(array, block), 1)


def nearest(block, core):
    return jnp.where(core == 0, block[:SWEEPS], block[SUB - SWEEPS :])


def spread(rows, core):
    zeros = jnp.zeros((SUB - SWEEPS, rows.shape[1]), rows.dtype)
    return jnp.where(core == 0, jnp.concatenate([rows, zeros], 0), jnp.concatenate([zeros, rows], 0))


def put_rows(ref, plane, pieces):
    used = sum(piece.shape[0] for piece in pieces)
    spare = jnp.zeros((2 * SUB - used, pieces[0].shape[1]), jnp.float32)
    rows = jnp.concatenate([*pieces, spare], 0)
    ref[plane] = rows[:SUB]
    ref[plane + 1] = rows[SUB:]


def get_rows(ref, plane, counts):
    rows = jnp.concatenate([ref[plane], ref[plane + 1]], 0)
    out, at = [], 0
    for count in counts:
        out.append(rows[at : at + count])
        at += count
    return out


def fold(tiles):
    mid = SUB // 2
    return jnp.concatenate([part for tile in tiles for part in (tile[:mid], tile[mid:])], 1)


def unfold(rows):
    parts = [rows[:, i : i + LANE] for i in range(0, rows.shape[1], LANE)]
    return [jnp.concatenate(parts[i : i + 2], 0) for i in range(0, len(parts), 2)]


def half_lanes(which, half):
    return pl.ds(pl.multiple_of(which * half, half), half)


def slab_lanes(chip, half):
    return pl.ds(pl.multiple_of(half - LANE + chip * LANE, LANE), LANE)


def first_row(core, blocks, b):
    return pl.multiple_of((core * (blocks - 2) + b) * SUB, SUB)


def tile_rows(own_ref, other_ref, core, which, array, first, lanes):
    mine = own_ref[array, pl.ds(first, SUB), lanes]
    theirs = other_ref[array, pl.ds(first, SUB), lanes]
    return jnp.where(core == which, mine, theirs)


def edge_inputs(own_ref, other_ref, chip, core, first):
    tile = own_ref.shape[2]
    out = []
    for a in range(3):
        left = tile_rows(own_ref, other_ref, core, 1, a, first, slice(tile - LANE, tile))
        right = tile_rows(own_ref, other_ref, core, 0, a, first, slice(0, LANE))
        out.append(jnp.where(chip == 0, left, right))
    return out


def pack_kernel(keep_ref, recv_ref, own_ref, other_ref, out_ref):
    chip, core = place()
    blocks, _, _, cols = keep_ref.shape
    half = cols // 2
    away = half_lanes(1 - chip, half)
    slab = slab_lanes(chip, half)
    main = 3 * (blocks - 1)
    tiles = [None] * -(-blocks // SHARE)
    for j in range(blocks):
        b = j + core if j < blocks - 1 else (1 - core) * (blocks - 1)
        sums = [keep_ref[b, a, :, away] + recv_ref[b, a, :, away] for a in range(3)]
        if j < blocks - 1:
            for a in range(3):
                out_ref[3 * j + a] = sums[a]
        else:
            rows = [nearest(v, core) for v in sums]
        pieces = [keep_ref[b, a, :, slab] + recv_ref[b, a, :, slab] for a in range(3)]
        pieces += edge_inputs(own_ref, other_ref, chip, core, first_row(core, blocks, b))
        piece = packed(pieces, chip, j % SHARE)
        i = j // SHARE
        tiles[i] = piece if tiles[i] is None else tiles[i] + piece
    put_rows(out_ref, main, [*rows, fold(tiles)])


def pack(keep, recv, own, other):
    blocks, _, _, cols = keep.shape
    half = cols // 2
    return pl.pallas_call(
        pack_kernel,
        in_specs=[VMEM] * 4,
        out_specs=VMEM,
        out_shape=jax.ShapeDtypeStruct((3 * blocks - 1, SUB, half), jnp.float32),
        compiler_params=params(8),
        cost_estimate=cost(keep.size, 12 * keep.size),
        name="pack",
    )(keep, recv, own, other)


def rim_kernel(keep_ref, recv_ref, own_ref, other_ref, first, side_ref, cross_ref):
    del first
    chip, core = place()
    blocks, _, _, cols = keep_ref.shape
    half = cols // 2
    tile = half // 2
    b = core * (blocks - 1)
    row = first_row(core, blocks, b)
    near, away = half_lanes(chip, half), half_lanes(1 - chip, half)
    side_ref[:3] = keep_ref[b, :, :, near] + recv_ref[b, :, :, near]
    rows = [nearest(keep_ref[b, a, :, away] + recv_ref[b, a, :, away], core) for a in range(3)]
    for which in range(2):
        for a in range(3):
            side_ref[3 + a, :, which * tile : (which + 1) * tile] = tile_rows(
                own_ref, other_ref, core, which, a, row, slice(0, tile)
            )

    def sums(slab):
        return [keep_ref[b, a, :, slab] + recv_ref[b, a, :, slab] for a in range(3)]

    side_ref[6, :, :LANE] = packed(sums(slab_lanes(1 - chip, half)), 1 - chip)
    inputs = edge_inputs(own_ref, other_ref, chip, core, row)
    halo = nearest(packed(sums(slab_lanes(chip, half)) + inputs, chip), core)
    spare = jnp.zeros((SWEEPS, half - LANE), jnp.float32)
    put_rows(cross_ref, 0, [*rows, jnp.concatenate([halo, spare], 1)])


def rim(keep, recv, own, other, first):
    half = keep.shape[3] // 2
    return pl.pallas_call(
        rim_kernel,
        in_specs=[VMEM] * 4 + [ANY],
        out_specs=[VMEM] * 2,
        out_shape=[jax.ShapeDtypeStruct((n, SUB, half), jnp.float32) for n in (7, 2)],
        compiler_params=params(8),
        cost_estimate=cost(keep.size // 8, keep.size),
        name="rim",
    )(keep, recv, own, other, first)


def sweep_kernel(keep_ref, recv_ref, own_ref, other_ref, far_ref, side_ref, cross_ref, out_ref, work):
    chip, core = place()
    strip = lax.axis_index("strips")
    blocks, _, _, cols = keep_ref.shape
    half = cols // 2
    tile = half // 2
    main = 3 * (blocks - 1)

    def cells(at, lanes, sums, inputs):
        trans = sums[0] * layer_thick
        store = spec_yield + sums[1] * layer_thick
        old, river, inflow = inputs
        rows = pl.ds(pl.multiple_of(at * SUB, SUB), SUB)
        work[0, rows, lanes] = trans
        work[1, rows, lanes] = store + river
        work[2, rows, lanes] = store * old + leak_rate * layer_thick * sums[2] + inflow
        work[3, rows, lanes] = old

    def halo(at, sums, inputs):
        sums, inputs = ([on_edge(v, 1 - chip) for v in values] for values in (sums, inputs))
        cells(at, slice(half, half + LANE), sums, inputs)

    near, slab = half_lanes(chip, half), slab_lanes(1 - chip, half)
    *beyond, tiles = get_rows(far_ref, main, (SWEEPS, SWEEPS, SWEEPS, SUB // 2))
    tiles = unfold(tiles)
    for j in range(blocks):
        b = j + core if j < blocks - 1 else (1 - core) * (blocks - 1)
        if j < blocks - 1:
            far = [far_ref[3 * j + a] for a in range(3)]
        else:
            far = [spread(v, core) for v in beyond]
        sums = [keep_ref[b, a, :, near] + recv_ref[b, a, :, near] + far[a] for a in range(3)]
        first_at = first_row(core, blocks, b)
        for which in range(2):
            lanes = slice(which * tile, (which + 1) * tile)
            inputs = [tile_rows(own_ref, other_ref, core, which, a, first_at, slice(0, tile)) for a in range(3)]
            cells(b, lanes, [s[:, lanes] for s in sums], inputs)
        far = [unpacked(tiles[j // SHARE], a, j % SHARE) for a in range(6)]
        sums = [keep_ref[b, a, :, slab] + recv_ref[b, a, :, slab] + far[a] for a in range(3)]
        halo(b, sums, far[3:])
    outside = ((core == 0) & (strip == 0)) | ((core == 1) & (strip == lax.axis_size("strips") - 1))

    def inside(value):
        return jnp.where(outside, 0.0, value)

    *cross, corner = [spread(v, 1 - core) for v in get_rows(cross_ref, 0, (SWEEPS,) * 4)]
    sums = [inside(side_ref[a] + cross[a]) for a in range(3)]
    cells(blocks, slice(0, half), sums, [inside(side_ref[3 + a]) for a in range(3)])
    side, cross = side_ref[6, :, :LANE], corner[:, :LANE]
    sums = [inside(unpacked(side, a) + unpacked(cross, a)) for a in range(3)]
    halo(blocks, sums, [inside(unpacked(cross, a)) for a in range(3, 6)])

    trans, base, rhs, head = (work[i] for i in range(4))
    rows, lanes = trans.shape
    right = jnp.sqrt(trans * pltpu.roll(trans, lanes - 1, 1))
    left = pltpu.roll(right, 1, 1)
    down = jnp.sqrt(trans * pltpu.roll(trans, rows - 1, 0))
    up = pltpu.roll(down, 1, 0)
    inverse = 1.0 / (base + right + left + down + up)
    for _ in range(SWEEPS):
        head = inverse * (
            rhs
            + right * pltpu.roll(head, lanes - 1, 1)
            + left * pltpu.roll(head, 1, 1)
            + down * pltpu.roll(head, rows - 1, 0)
            + up * pltpu.roll(head, 1, 0)
        )
    work[0] = head
    out_ref[...] = work[0, pl.ds(pl.multiple_of(core * SUB, SUB), out_ref.shape[0]), :half]


def sweeps(keep, recv, own, other, far, side, cross):
    blocks = keep.shape[0]
    half = keep.shape[3] // 2
    return pl.pallas_call(
        sweep_kernel,
        in_specs=[VMEM] * 7,
        out_specs=VMEM,
        out_shape=jax.ShapeDtypeStruct(((blocks - 1) * SUB, half), jnp.float32),
        scratch_shapes=[pltpu.VMEM((4, (blocks + 1) * SUB, half + LANE), jnp.float32)],
        compiler_params=params(12),
        cost_estimate=cost(20 * keep.size, 12 * keep.size),
        name="sweeps",
    )(keep, recv, own, other, far, side, cross)


def faces_kernel(moist_in, core_ref, chip_ref, core_far, chip_far, rain_ref, moist_out, tail_ref, ends, sems):
    del moist_in
    chip, core = place()
    layers = moist_out.shape[0]
    copies = [
        (moist_out.at[layer], ends.at[i], sems.at[i]) for i, layer in enumerate((0, layers - 1))
    ]
    loads = [pltpu.make_async_copy(src, dst, sem) for src, dst, sem in copies]
    stores = [pltpu.make_async_copy(dst, src, sem) for src, dst, sem in copies]
    for c in loads:
        c.start()
    for c in loads:
        c.wait()
    gain = soil_step / layer_thick
    face = 0.5 * gain
    last = (core == 1) & (chip == 1)

    def flux(upper, lower):
        return (upper[1] + lower[1]) * ((upper[0] - lower[0]) * (face / layer_thick) + face)

    @pl.when(core == 0)
    def _():
        ends[1] = ends[1] - flux(core_ref, core_far)

    @pl.when(core == 1)
    def _():
        ends[0] = ends[0] + flux(core_far, core_ref)

    @pl.when((core == 0) & (chip == 0))
    def _():
        ends[0] = ends[0] + gain * rain_ref[...]

    @pl.when((core == 0) & (chip == 1))
    def _():
        ends[0] = ends[0] + flux(chip_far, chip_ref)

    @pl.when((core == 1) & (chip == 0))
    def _():
        ends[1] = ends[1] - flux(chip_ref, chip_far)

    stores[0].start()

    @pl.when(last)
    def _():
        slope = chip_ref[1] * (gain / (0.5 * layer_thick))
        tail_ref[0] = ends[1] - (chip_ref[0] * slope + gain * chip_ref[1])
        tail_ref[1] = slope

    @pl.when(jnp.logical_not(last))
    def _():
        stores[1].start()
        stores[1].wait()

    stores[0].wait()


def faces(moist, core_pair, chip_pair, core_far, chip_far, rain):
    return pl.pallas_call(
        faces_kernel,
        in_specs=[ANY] + [VMEM] * 5,
        out_specs=[ANY, VMEM],
        out_shape=[
            jax.ShapeDtypeStruct(moist.shape, moist.dtype),
            jax.ShapeDtypeStruct((2,) + moist.shape[1:], moist.dtype),
        ],
        input_output_aliases={0: 0},
        scratch_shapes=[pltpu.VMEM((2,) + moist.shape[1:], jnp.float32), pltpu.SemaphoreType.DMA((2,))],
        compiler_params=params(12),
        cost_estimate=cost(20 * rain.size, 32 * rain.size),
        name="faces",
    )(moist, core_pair, chip_pair, core_far, chip_far, rain)


def bottom_kernel(moist_in, tail_ref, own_ref, core_far, chip_far, both_far, moist_out, head_ref, last, sems):
    del moist_in
    chip, core = place()
    layers = moist_out.shape[0]
    rows, half = own_ref.shape
    tile = half // 2
    mine = pl.ds(pl.multiple_of(core * rows, rows), rows)
    theirs = pl.ds(pl.multiple_of((1 - core) * rows, rows), rows)

    @pl.when((core == 1) & (chip == 1))
    def _():
        copies = []
        for i, (left, right) in enumerate(((both_far, core_far), (chip_far, own_ref))):
            where = slice(i * rows, (i + 1) * rows)
            for ref, lanes in ((left, slice(0, half)), (right, slice(half, 2 * half))):
                last[where, lanes] = tail_ref[0, where, lanes] + tail_ref[1, where, lanes] * ref[...]
            copies.append(
                pltpu.make_async_copy(last.at[where], moist_out.at[layers - 1, where], sems.at[i])
            )
            copies[-1].start()
        for c in copies:
            c.wait()

    lanes = pl.ds(pl.multiple_of(core * tile, tile), tile)
    head_ref[mine, :] = own_ref[:, lanes]
    head_ref[theirs, :] = core_far[:, lanes]


def bottom(moist, tail, own, core_far, chip_far, both_far):
    rows, half = own.shape
    return pl.pallas_call(
        bottom_kernel,
        in_specs=[ANY] + [VMEM] * 5,
        out_specs=[ANY, VMEM],
        out_shape=[
            jax.ShapeDtypeStruct(moist.shape, moist.dtype),
            jax.ShapeDtypeStruct((2 * rows, half // 2), jnp.float32),
        ],
        input_output_aliases={0: 0},
        scratch_shapes=[pltpu.VMEM(moist.shape[1:], jnp.float32), pltpu.SemaphoreType.DMA((2,))],
        compiler_params=params(12),
        cost_estimate=cost(10 * own.size, 40 * own.size),
        name="bottom",
    )(moist, tail, own, core_far, chip_far, both_far)


def inputs_kernel(old_ref, code_ref, section_ref, first, out_ref):
    del first
    code = code_ref[...]
    river = jnp.where(code == 1, river_cond, jnp.where(code == 2, fixed_cond, 0.0))
    out_ref[0] = old_ref[...]
    out_ref[1] = river
    out_ref[2] = river * section_ref[...]


def inputs(head_old, cell_code, section, first):
    return pl.pallas_call(
        inputs_kernel,
        in_specs=[VMEM] * 3 + [ANY],
        out_specs=VMEM,
        out_shape=jax.ShapeDtypeStruct((3,) + head_old.shape, jnp.float32),
        compiler_params=params(4),
        cost_estimate=cost(4 * head_old.size, 24 * head_old.size),
        name="inputs",
    )(head_old, cell_code, section, first)


def gate_kernel(*refs):
    del refs


def gate(value, *first, stored=()):
    return pl.pallas_call(
        gate_kernel,
        in_specs=[ANY] * (1 + len(first)) + [HBM] * len(stored),
        out_specs=ANY,
        out_shape=jax.ShapeDtypeStruct(value.shape, value.dtype),
        input_output_aliases={0: 0},
        compiler_params=params(1),
        cost_estimate=cost(1, 1),
        name="gate",
    )(value, *first, *in_hbm(*stored))


def core_swap(value):
    return lax.ppermute(value, "depth", [(i, i ^ 1) for i in range(lax.axis_size("depth"))])


def chip_swap(value):
    return lax.ppermute(value, "depth", [(i, i ^ 2) for i in range(lax.axis_size("depth"))])


def middle_swap(value):
    return lax.ppermute(value, "depth", [(1, 2), (2, 1)])


def strip_swap(value, chips=0):
    depth, strips = lax.axis_size("depth"), lax.axis_size("strips")
    pairs = []
    for d in range(1, depth, 2):
        for s in range(strips):
            lower, upper = d * strips + s, ((d - 1) ^ chips) * strips + (s + 1) % strips
            pairs += [(lower, upper), (upper, lower)]
    return lax.ppermute(value, ("depth", "strips"), pairs)


def shards(pressure, texture, active, rain, k_sat, alpha, theta_sat, head_old, cell_code, section):
    tables = (k_sat[None], alpha[None], theta_sat[None])
    chip_pair = face(tables, pressure, texture, active)
    chip_far = middle_swap(chip_pair)
    own = inputs(head_old, cell_code, section, chip_pair)
    other = core_swap(own)
    moist, keep, send, core_pair = soil(tables, pressure, texture, active)
    recv = core_swap(gate(send, other))
    keep = gate(keep, chip_far)
    message = pack(keep, recv, own, other)
    far = chip_swap(message)
    side, cross = rim(keep, recv, own, other, message)
    heads = sweeps(keep, recv, own, other, far, strip_swap(side), strip_swap(cross, 2))
    core_far = core_swap(gate(core_pair, side))
    moist, tail = faces(moist, core_pair, chip_pair, core_far, chip_far, rain)
    heads_chip = gate(chip_swap(heads), stored=(moist,))
    heads_core = core_swap(heads)
    heads_both = core_swap(heads_chip)
    return bottom(moist, tail, heads, heads_core, heads_chip, heads_both)


def solution(mesh):
    in_specs = (
        P("depth", "strips", None),
        P("depth", "strips", None),
        P("depth", "strips", None),
        P("strips", None),
        P(),
        P(),
        P(),
        P("strips", "depth"),
        P("strips", "depth"),
        P("strips", "depth"),
    )
    out_specs = (P("depth", "strips", None), P("strips", "depth"))
    return jax.shard_map(shards, mesh=mesh, in_specs=in_specs, out_specs=out_specs, check_vma=False)
```

```python
import functools
import math

import jax
import jax.numpy as jnp
from jax import lax
from jax.experimental import pallas as pl
from jax.experimental.pallas import tpu as pltpu
from jax.sharding import PartitionSpec as P

SWEEPS = 3
SUB = 8
LANE = 128
WIDTH = 4

layer_thick = 0.05
soil_step = 0.0002
spec_yield = 0.02
leak_rate = 0.5
river_cond = 0.5
fixed_cond = 3.0
residual = 0.15
mobile = 0.85

VMEM = pl.BlockSpec(memory_space=pltpu.VMEM)
ANY = pl.BlockSpec(memory_space=pl.ANY)
HBM = pl.BlockSpec(memory_space=pltpu.HBM)


def params(mib):
    return pltpu.CompilerParams(vmem_limit_bytes=mib * 2**20)


def cost(flops, nbytes, trans=0):
    return pl.CostEstimate(flops=int(flops), bytes_accessed=int(nbytes), transcendentals=int(trans))


def place():
    depth = lax.axis_index("depth")
    return depth // 2, depth % 2


def gathered(table, classes):
    return jnp.take_along_axis(table, classes, axis=1, mode="promise_in_bounds")


def picked(options, bits):
    for bit in bits:
        options = [
            jnp.where(bit, options[i + 1], options[i]) if i + 1 < len(options) else options[i]
            for i in range(0, len(options), 2)
        ]
    return options[0]


def fill_tables(tab, sat_ref, alpha_ref, theta_ref):
    classes = sat_ref.shape[1]
    scaled = (sat_ref, 1.0), (alpha_ref, 0.5 * math.log2(math.e)), (theta_ref, mobile)
    for i, (ref, scale) in enumerate(scaled):
        tab[i, :, :classes] = jnp.broadcast_to(ref[...] * scale, (SUB, classes))


def face_kernel(
    sat_hbm, alpha_hbm, psi_hbm, tex_hbm, act_hbm, out_ref, kinds, acts, given, tab, sems
):
    chip, _ = place()
    layer = (1 - chip) * (psi_hbm.shape[0] - 1)
    cols = psi_hbm.shape[2]
    classes = sat_hbm.shape[1]
    copies = [
        pltpu.make_async_copy(src, dst, sems.at[i])
        for i, (src, dst) in enumerate(
            (
                (sat_hbm, given.at[0]),
                (alpha_hbm, given.at[1]),
                (psi_hbm.at[layer], out_ref.at[0]),
                (tex_hbm.at[layer], kinds),
                (act_hbm.at[layer], acts),
            )
        )
    ]
    for c in copies:
        c.start()
    for c in copies:
        c.wait()
    for i, scale in enumerate((1.0, 0.5 * math.log2(math.e))):
        tab[i, :, :classes] = jnp.broadcast_to(given[i] * scale, (SUB, classes))

    def columns(q, carry):
        lanes = pl.ds(pl.multiple_of(q * LANE, LANE), LANE)
        for r in range(0, kinds.shape[0], SUB):
            rws = slice(r, r + SUB)
            kind = kinds[rws, lanes]
            wet = jnp.exp2(gathered(tab[1], kind) * jnp.minimum(out_ref[0, rws, lanes], 0.0))
            active = acts[rws, lanes].astype(jnp.float32)
            out_ref[1, rws, lanes] = gathered(tab[0], kind) * active * (wet * wet)
        return carry

    lax.fori_loop(0, cols // LANE, columns, 0, unroll=4)


def in_hbm(*arrays):
    return [pltpu.with_memory_space_constraint(x, pltpu.HBM) for x in arrays]


def face(tables, pressure, texture, active):
    _, nrows, cols = pressure.shape
    size = nrows * cols
    return pl.pallas_call(
        face_kernel,
        in_specs=[HBM] * 5,
        out_specs=VMEM,
        out_shape=jax.ShapeDtypeStruct((2, nrows, cols), jnp.float32),
        scratch_shapes=[
            pltpu.VMEM((nrows, cols), jnp.int32),
            pltpu.VMEM((nrows, cols), jnp.int32),
            pltpu.VMEM((2,) + tables[0].shape, jnp.float32),
            pltpu.VMEM((2, SUB, LANE), jnp.float32),
            pltpu.SemaphoreType.DMA((5,)),
        ],
        compiler_params=params(8),
        cost_estimate=cost(20 * size, 20 * size, size),
        name="face",
    )(*in_hbm(*tables[:2], pressure, texture, active))


def soil_kernel(
    sat_ref, alpha_ref, theta_ref, psi_ref, tex_ref, act_ref,
    moist_ref, keep_ref, send_ref, core_ref, rest_ref, tab, part,
):
    step = pl.program_id(0)
    _, core = place()
    layers, rows, cols = psi_ref.shape
    classes = sat_ref.shape[1]

    @pl.when(step == 0)
    def _():
        fill_tables(tab, sat_ref, alpha_ref, theta_ref)

    sat_tab, par_tab = tab[0], tab[1]
    theta = [jnp.broadcast_to(tab[2, :, i : i + 1], (SUB, LANE)) for i in range(classes)]
    nbits = max(1, (classes - 1).bit_length())
    face = 0.5 * soil_step / layer_thick
    core_layer = (1 - core) * (layers - 1)
    rest_layer = core * (layers - 1)

    def columns(q, carry):
        lanes = pl.ds(pl.multiple_of(q * LANE, LANE), LANE)
        for r in range(0, rows, SUB):
            rws = slice(r, r + SUB)
            trans = store = charge = jnp.zeros((SUB, LANE), jnp.float32)
            for layer in range(layers):
                kind = tex_ref[layer, rws, lanes]
                psi = psi_ref[layer, rws, lanes]
                active = act_ref[layer, rws, lanes].astype(jnp.float32)
                bits = [(kind & (1 << b)) != 0 for b in range(nbits)]
                wet = jnp.exp2(gathered(par_tab, kind) * jnp.minimum(psi, 0.0))
                cond = gathered(sat_tab, kind) * active * (wet * wet)
                mob = picked(theta, bits)
                mobwet = mob * wet
                trans = trans + cond
                charge = charge + cond * wet
                store = store + (mob - mobwet)
                held = mob * (residual / mobile) + mobwet
                if layer == 0:
                    first, own = cond, held
                else:
                    flux = (cond_up + cond) * ((psi_up - psi) * (face / layer_thick) + face)
                    moist_ref[layer - 1, rws, lanes] = own - flux
                    own = held + flux
                psi_up, cond_up = psi, cond
            moist_ref[layers - 1, rws, lanes] = own
            part[r // SUB, 0, :, lanes] = trans
            part[r // SUB, 1, :, lanes] = store
            part[r // SUB, 2, :, lanes] = charge
            core_ref[0, rws, lanes] = psi_ref[core_layer, rws, lanes]
            core_ref[1, rws, lanes] = jnp.where(core == 0, cond, first)
            rest_ref[0, rws, lanes] = psi_ref[rest_layer, rws, lanes]
            rest_ref[1, rws, lanes] = jnp.where(core == 0, first, cond)
        return carry

    lax.fori_loop(0, cols // LANE, columns, 0, unroll=8)

    blocks = rows // SUB
    half = keep_ref.shape[0] - 1
    for r in range(blocks):
        block = step * blocks + r

        def put(ref, at):
            ref[at] = part[r]

        @pl.when((block <= half) & (core == 0))
        def _():
            put(keep_ref, block)

        @pl.when((block <= half) & (core == 1))
        def _():
            put(send_ref, block)

        @pl.when((block >= half - 1) & (core == 0))
        def _():
            put(send_ref, block - (half - 1))

        @pl.when((block >= half - 1) & (core == 1))
        def _():
            put(keep_ref, block - (half - 1))


def soil(tables, pressure, texture, active):
    layers, nrows, cols = pressure.shape
    classes = tables[0].shape[1]
    rows = nrows // 4
    blocks = nrows // (2 * SUB) + 1
    whole = pl.BlockSpec((1, classes), lambda j: (0, 0))
    block = pl.BlockSpec((layers, rows, cols), lambda j: (0, j, 0))
    pair = pl.BlockSpec((2, rows, cols), lambda j: (0, j, 0))
    msg = jax.ShapeDtypeStruct((blocks, 3, SUB, cols), jnp.float32)
    msg_spec = pl.BlockSpec((blocks, 3, SUB, cols), lambda j: (0, 0, 0, 0))
    layer2 = jax.ShapeDtypeStruct((2, nrows, cols), jnp.float32)
    size = layers * nrows * cols
    return pl.pallas_call(
        soil_kernel,
        grid=(nrows // rows,),
        in_specs=[whole, whole, whole, block, block, block],
        out_specs=[block, msg_spec, msg_spec, pair, pair],
        out_shape=[jax.ShapeDtypeStruct((layers, nrows, cols), jnp.float32), msg, msg, layer2, layer2],
        scratch_shapes=[
            pltpu.VMEM((3, SUB, LANE), jnp.float32),
            pltpu.VMEM((rows // SUB, 3, SUB, cols), jnp.float32),
        ],
        compiler_params=params(32),
        cost_estimate=cost(60 * size, 20 * size, size),
        name="soil",
    )(*in_hbm(*tables, pressure, texture, active))


def edge_lane(chip):
    return (1 - chip) * (LANE - WIDTH)


def on_edge(value, chip):
    lane = lax.broadcasted_iota(jnp.int32, value.shape, 1)
    base = edge_lane(chip)
    return jnp.where((lane >= base) & (lane < base + WIDTH), value, 0.0)


def shift(array, block=0):
    return WIDTH * (6 * block + array)


SHARE = LANE // (6 * WIDTH)


def packed(pieces, chip, block=0):
    total = None
    for a, piece in enumerate(pieces):
        moved = pltpu.roll(on_edge(piece, chip), shift(a, block), 1)
        total = moved if total is None else total + moved
    return total


def unpacked(tile, array, block=0):
    return pltpu.roll(tile, LANE - shift(array, block), 1)


def nearest(block, core):
    return jnp.where(core == 0, block[:SWEEPS], block[SUB - SWEEPS :])


def spread(rows, core):
    zeros = jnp.zeros((SUB - SWEEPS, rows.shape[1]), rows.dtype)
    return jnp.where(core == 0, jnp.concatenate([rows, zeros], 0), jnp.concatenate([zeros, rows], 0))


def put_rows(ref, plane, pieces):
    used = sum(piece.shape[0] for piece in pieces)
    spare = jnp.zeros((2 * SUB - used, pieces[0].shape[1]), jnp.float32)
    rows = jnp.concatenate([*pieces, spare], 0)
    ref[plane] = rows[:SUB]
    ref[plane + 1] = rows[SUB:]


def get_rows(ref, plane, counts):
    rows = jnp.concatenate([ref[plane], ref[plane + 1]], 0)
    out, at = [], 0
    for count in counts:
        out.append(rows[at : at + count])
        at += count
    return out


def fold(tiles):
    mid = SUB // 2
    return jnp.concatenate([part for tile in tiles for part in (tile[:mid], tile[mid:])], 1)


def unfold(rows):
    parts = [rows[:, i : i + LANE] for i in range(0, rows.shape[1], LANE)]
    return [jnp.concatenate(parts[i : i + 2], 0) for i in range(0, len(parts), 2)]


def half_lanes(which, half):
    return pl.ds(pl.multiple_of(which * half, half), half)


def slab_lanes(chip, half):
    return pl.ds(pl.multiple_of(half - LANE + chip * LANE, LANE), LANE)


def first_row(core, blocks, b):
    return pl.multiple_of((core * (blocks - 2) + b) * SUB, SUB)


def tile_rows(own_ref, other_ref, core, which, array, first, lanes):
    mine = own_ref[array, pl.ds(first, SUB), lanes]
    theirs = other_ref[array, pl.ds(first, SUB), lanes]
    return jnp.where(core == which, mine, theirs)


def edge_inputs(own_ref, other_ref, chip, core, first):
    tile = own_ref.shape[2]
    out = []
    for a in range(3):
        left = tile_rows(own_ref, other_ref, core, 1, a, first, slice(tile - LANE, tile))
        right = tile_rows(own_ref, other_ref, core, 0, a, first, slice(0, LANE))
        out.append(jnp.where(chip == 0, left, right))
    return out


def pack_kernel(keep_ref, recv_ref, own_ref, other_ref, out_ref):
    chip, core = place()
    blocks, _, _, cols = keep_ref.shape
    half = cols // 2
    away = half_lanes(1 - chip, half)
    slab = slab_lanes(chip, half)
    main = 3 * (blocks - 1)
    tiles = [None] * -(-blocks // SHARE)
    for j in range(blocks):
        b = j + core if j < blocks - 1 else (1 - core) * (blocks - 1)
        sums = [keep_ref[b, a, :, away] + recv_ref[b, a, :, away] for a in range(3)]
        if j < blocks - 1:
            for a in range(3):
                out_ref[3 * j + a] = sums[a]
        else:
            rows = [nearest(v, core) for v in sums]
        pieces = [keep_ref[b, a, :, slab] + recv_ref[b, a, :, slab] for a in range(3)]
        pieces += edge_inputs(own_ref, other_ref, chip, core, first_row(core, blocks, b))
        piece = packed(pieces, chip, j % SHARE)
        i = j // SHARE
        tiles[i] = piece if tiles[i] is None else tiles[i] + piece
    put_rows(out_ref, main, [*rows, fold(tiles)])


def pack(keep, recv, own, other):
    blocks, _, _, cols = keep.shape
    half = cols // 2
    return pl.pallas_call(
        pack_kernel,
        in_specs=[VMEM] * 4,
        out_specs=VMEM,
        out_shape=jax.ShapeDtypeStruct((3 * blocks - 1, SUB, half), jnp.float32),
        compiler_params=params(8),
        cost_estimate=cost(keep.size, 12 * keep.size),
        name="pack",
    )(keep, recv, own, other)


def rim_kernel(keep_ref, recv_ref, own_ref, other_ref, first, second, side_ref, cross_ref):
    del first, second
    chip, core = place()
    blocks, _, _, cols = keep_ref.shape
    half = cols // 2
    tile = half // 2
    b = core * (blocks - 1)
    row = first_row(core, blocks, b)
    near, away = half_lanes(chip, half), half_lanes(1 - chip, half)
    side_ref[:3] = keep_ref[b, :, :, near] + recv_ref[b, :, :, near]
    rows = [nearest(keep_ref[b, a, :, away] + recv_ref[b, a, :, away], core) for a in range(3)]
    for which in range(2):
        for a in range(3):
            side_ref[3 + a, :, which * tile : (which + 1) * tile] = tile_rows(
                own_ref, other_ref, core, which, a, row, slice(0, tile)
            )

    def sums(slab):
        return [keep_ref[b, a, :, slab] + recv_ref[b, a, :, slab] for a in range(3)]

    side_ref[6, :, :LANE] = packed(sums(slab_lanes(1 - chip, half)), 1 - chip)
    inputs = edge_inputs(own_ref, other_ref, chip, core, row)
    halo = nearest(packed(sums(slab_lanes(chip, half)) + inputs, chip), core)
    spare = jnp.zeros((SWEEPS, half - LANE), jnp.float32)
    put_rows(cross_ref, 0, [*rows, jnp.concatenate([halo, spare], 1)])


def rim(keep, recv, own, other, *first):
    half = keep.shape[3] // 2
    return pl.pallas_call(
        rim_kernel,
        in_specs=[VMEM] * 4 + [ANY] * 2,
        out_specs=[VMEM] * 2,
        out_shape=[jax.ShapeDtypeStruct((n, SUB, half), jnp.float32) for n in (7, 2)],
        compiler_params=params(8),
        cost_estimate=cost(keep.size // 8, keep.size),
        name="rim",
    )(keep, recv, own, other, *first)


def sweep_kernel(keep_ref, recv_ref, own_ref, other_ref, far_ref, side_ref, cross_ref, out_ref, work):
    chip, core = place()
    strip = lax.axis_index("strips")
    blocks, _, _, cols = keep_ref.shape
    half = cols // 2
    tile = half // 2
    main = 3 * (blocks - 1)

    def cells(at, lanes, sums, inputs):
        trans = sums[0] * layer_thick
        store = spec_yield + sums[1] * layer_thick
        old, river, inflow = inputs
        rows = pl.ds(pl.multiple_of(at * SUB, SUB), SUB)
        work[0, rows, lanes] = trans
        work[1, rows, lanes] = store + river
        work[2, rows, lanes] = store * old + leak_rate * layer_thick * sums[2] + inflow
        work[3, rows, lanes] = old

    def halo(at, sums, inputs):
        sums, inputs = ([on_edge(v, 1 - chip) for v in values] for values in (sums, inputs))
        cells(at, slice(half, half + LANE), sums, inputs)

    near, slab = half_lanes(chip, half), slab_lanes(1 - chip, half)
    *beyond, tiles = get_rows(far_ref, main, (SWEEPS, SWEEPS, SWEEPS, SUB // 2))
    tiles = unfold(tiles)
    for j in range(blocks):
        b = j + core if j < blocks - 1 else (1 - core) * (blocks - 1)
        if j < blocks - 1:
            far = [far_ref[3 * j + a] for a in range(3)]
        else:
            far = [spread(v, core) for v in beyond]
        sums = [keep_ref[b, a, :, near] + recv_ref[b, a, :, near] + far[a] for a in range(3)]
        first_at = first_row(core, blocks, b)
        for which in range(2):
            lanes = slice(which * tile, (which + 1) * tile)
            inputs = [tile_rows(own_ref, other_ref, core, which, a, first_at, slice(0, tile)) for a in range(3)]
            cells(b, lanes, [s[:, lanes] for s in sums], inputs)
        far = [unpacked(tiles[j // SHARE], a, j % SHARE) for a in range(6)]
        sums = [keep_ref[b, a, :, slab] + recv_ref[b, a, :, slab] + far[a] for a in range(3)]
        halo(b, sums, far[3:])
    outside = ((core == 0) & (strip == 0)) | ((core == 1) & (strip == lax.axis_size("strips") - 1))

    def inside(value):
        return jnp.where(outside, 0.0, value)

    *cross, corner = [spread(v, 1 - core) for v in get_rows(cross_ref, 0, (SWEEPS,) * 4)]
    sums = [inside(side_ref[a] + cross[a]) for a in range(3)]
    cells(blocks, slice(0, half), sums, [inside(side_ref[3 + a]) for a in range(3)])
    side, cross = side_ref[6, :, :LANE], corner[:, :LANE]
    sums = [inside(unpacked(side, a) + unpacked(cross, a)) for a in range(3)]
    halo(blocks, sums, [inside(unpacked(cross, a)) for a in range(3, 6)])

    trans, base, rhs, head = (work[i] for i in range(4))
    rows, lanes = trans.shape
    right = jnp.sqrt(trans * pltpu.roll(trans, lanes - 1, 1))
    left = pltpu.roll(right, 1, 1)
    down = jnp.sqrt(trans * pltpu.roll(trans, rows - 1, 0))
    up = pltpu.roll(down, 1, 0)
    inverse = 1.0 / (base + right + left + down + up)
    for _ in range(SWEEPS):
        head = inverse * (
            rhs
            + right * pltpu.roll(head, lanes - 1, 1)
            + left * pltpu.roll(head, 1, 1)
            + down * pltpu.roll(head, rows - 1, 0)
            + up * pltpu.roll(head, 1, 0)
        )
    work[0] = head
    out_ref[...] = work[0, pl.ds(pl.multiple_of(core * SUB, SUB), out_ref.shape[0]), :half]


def sweeps(keep, recv, own, other, far, side, cross):
    blocks = keep.shape[0]
    half = keep.shape[3] // 2
    return pl.pallas_call(
        sweep_kernel,
        in_specs=[VMEM] * 7,
        out_specs=VMEM,
        out_shape=jax.ShapeDtypeStruct(((blocks - 1) * SUB, half), jnp.float32),
        scratch_shapes=[pltpu.VMEM((4, (blocks + 1) * SUB, half + LANE), jnp.float32)],
        compiler_params=params(12),
        cost_estimate=cost(20 * keep.size, 12 * keep.size),
        name="sweeps",
    )(keep, recv, own, other, far, side, cross)


def pass_on_kernel(core_ref, ring_ref, first, out_ref):
    del first
    chip, core = place()

    @pl.when(chip == core)
    def _():
        out_ref[...] = ring_ref[...]

    @pl.when(chip != core)
    def _():
        out_ref[...] = core_ref[...]


def pass_on(core_pair, ring, first):
    return pl.pallas_call(
        pass_on_kernel,
        in_specs=[VMEM] * 2 + [ANY],
        out_specs=VMEM,
        out_shape=jax.ShapeDtypeStruct(ring.shape, ring.dtype),
        compiler_params=params(8),
        cost_estimate=cost(ring.size, 8 * ring.size),
        name="pass_on",
    )(core_pair, ring, first)


def faces_kernel(moist_in, core_ref, rest_ref, ring_ref, got_ref, rain_ref, moist_out, tail_ref, ends, sems):
    del moist_in
    chip, core = place()
    layers = moist_out.shape[0]
    copies = [
        (moist_out.at[layer], ends.at[i], sems.at[i]) for i, layer in enumerate((0, layers - 1))
    ]
    loads = [pltpu.make_async_copy(src, dst, sem) for src, dst, sem in copies]
    stores = [pltpu.make_async_copy(dst, src, sem) for src, dst, sem in copies]
    for c in loads:
        c.start()
    for c in loads:
        c.wait()
    gain = soil_step / layer_thick
    face = 0.5 * gain
    last = (core == 1) & (chip == 1)

    def flux(upper, lower):
        return (upper[1] + lower[1]) * ((upper[0] - lower[0]) * (face / layer_thick) + face)

    @pl.when((core == 0) & (chip == 0))
    def _():
        ends[0] = ends[0] + gain * rain_ref[...]
        ends[1] = ends[1] - flux(core_ref, got_ref)

    @pl.when((core == 1) & (chip == 0))
    def _():
        ends[0] = ends[0] + flux(ring_ref, core_ref)
        ends[1] = ends[1] - flux(rest_ref, got_ref)

    @pl.when((core == 0) & (chip == 1))
    def _():
        ends[0] = ends[0] + flux(got_ref, rest_ref)
        ends[1] = ends[1] - flux(core_ref, ring_ref)

    @pl.when(last)
    def _():
        ends[0] = ends[0] + flux(got_ref, core_ref)

    stores[0].start()

    @pl.when(last)
    def _():
        slope = rest_ref[1] * (gain / (0.5 * layer_thick))
        tail_ref[0] = ends[1] - (rest_ref[0] * slope + gain * rest_ref[1])
        tail_ref[1] = slope

    @pl.when(jnp.logical_not(last))
    def _():
        stores[1].start()
        stores[1].wait()

    stores[0].wait()


def faces(moist, core_pair, rest_pair, ring, got, rain):
    return pl.pallas_call(
        faces_kernel,
        in_specs=[ANY] + [VMEM] * 5,
        out_specs=[ANY, VMEM],
        out_shape=[
            jax.ShapeDtypeStruct(moist.shape, moist.dtype),
            jax.ShapeDtypeStruct((2,) + moist.shape[1:], moist.dtype),
        ],
        input_output_aliases={0: 0},
        scratch_shapes=[pltpu.VMEM((2,) + moist.shape[1:], jnp.float32), pltpu.SemaphoreType.DMA((2,))],
        compiler_params=params(12),
        cost_estimate=cost(20 * rain.size, 32 * rain.size),
        name="faces",
    )(moist, core_pair, rest_pair, ring, got, rain)


def bottom_kernel(moist_in, tail_ref, own_ref, core_far, chip_far, both_far, moist_out, head_ref, last, sems):
    del moist_in
    chip, core = place()
    layers = moist_out.shape[0]
    rows, half = own_ref.shape
    tile = half // 2
    mine = pl.ds(pl.multiple_of(core * rows, rows), rows)
    theirs = pl.ds(pl.multiple_of((1 - core) * rows, rows), rows)

    @pl.when((core == 1) & (chip == 1))
    def _():
        copies = []
        for i, (left, right) in enumerate(((both_far, core_far), (chip_far, own_ref))):
            where = slice(i * rows, (i + 1) * rows)
            for ref, lanes in ((left, slice(0, half)), (right, slice(half, 2 * half))):
                last[where, lanes] = tail_ref[0, where, lanes] + tail_ref[1, where, lanes] * ref[...]
            copies.append(
                pltpu.make_async_copy(last.at[where], moist_out.at[layers - 1, where], sems.at[i])
            )
            copies[-1].start()
        for c in copies:
            c.wait()

    lanes = pl.ds(pl.multiple_of(core * tile, tile), tile)
    head_ref[mine, :] = own_ref[:, lanes]
    head_ref[theirs, :] = core_far[:, lanes]


def bottom(moist, tail, own, core_far, chip_far, both_far):
    rows, half = own.shape
    return pl.pallas_call(
        bottom_kernel,
        in_specs=[ANY] + [VMEM] * 5,
        out_specs=[ANY, VMEM],
        out_shape=[
            jax.ShapeDtypeStruct(moist.shape, moist.dtype),
            jax.ShapeDtypeStruct((2 * rows, half // 2), jnp.float32),
        ],
        input_output_aliases={0: 0},
        scratch_shapes=[pltpu.VMEM(moist.shape[1:], jnp.float32), pltpu.SemaphoreType.DMA((2,))],
        compiler_params=params(12),
        cost_estimate=cost(10 * own.size, 40 * own.size),
        name="bottom",
    )(moist, tail, own, core_far, chip_far, both_far)


def inputs_kernel(old_ref, code_ref, section_ref, first, out_ref):
    del first
    code = code_ref[...]
    river = jnp.where(code == 1, river_cond, jnp.where(code == 2, fixed_cond, 0.0))
    out_ref[0] = old_ref[...]
    out_ref[1] = river
    out_ref[2] = river * section_ref[...]


def inputs(head_old, cell_code, section, first):
    return pl.pallas_call(
        inputs_kernel,
        in_specs=[VMEM] * 3 + [ANY],
        out_specs=VMEM,
        out_shape=jax.ShapeDtypeStruct((3,) + head_old.shape, jnp.float32),
        compiler_params=params(4),
        cost_estimate=cost(4 * head_old.size, 24 * head_old.size),
        name="inputs",
    )(head_old, cell_code, section, first)


def gate_kernel(*refs):
    del refs


def gate(value, *first, stored=()):
    return pl.pallas_call(
        gate_kernel,
        in_specs=[ANY] * (1 + len(first)) + [HBM] * len(stored),
        out_specs=ANY,
        out_shape=jax.ShapeDtypeStruct(value.shape, value.dtype),
        input_output_aliases={0: 0},
        compiler_params=params(1),
        cost_estimate=cost(1, 1),
        name="gate",
    )(value, *first, *in_hbm(*stored))


def core_swap(value):
    return lax.ppermute(value, "depth", [(i, i ^ 1) for i in range(lax.axis_size("depth"))])


def chip_swap(value):
    return lax.ppermute(value, "depth", [(i, i ^ 2) for i in range(lax.axis_size("depth"))])


def ring_shift(value):
    return lax.ppermute(value, "depth", [(1, 3), (3, 2), (2, 0), (0, 1)])


def strip_swap(value, chips=0):
    depth, strips = lax.axis_size("depth"), lax.axis_size("strips")
    pairs = []
    for d in range(1, depth, 2):
        for s in range(strips):
            lower, upper = d * strips + s, ((d - 1) ^ chips) * strips + (s + 1) % strips
            pairs += [(lower, upper), (upper, lower)]
    return lax.ppermute(value, ("depth", "strips"), pairs)


def shards(pressure, texture, active, rain, k_sat, alpha, theta_sat, head_old, cell_code, section):
    tables = (k_sat[None], alpha[None], theta_sat[None])
    face_pair = face(tables, pressure, texture, active)
    ring = ring_shift(face_pair)
    own = inputs(head_old, cell_code, section, face_pair)
    other = core_swap(own)
    moist, keep, send, core_pair, rest_pair = soil(tables, pressure, texture, active)
    recv = core_swap(gate(send, other))
    message = pack(keep, recv, own, other)
    far = chip_swap(message)
    side, cross = rim(keep, recv, own, other, message, ring)
    heads = sweeps(keep, recv, own, other, far, strip_swap(side), strip_swap(cross, 2))
    got = core_swap(pass_on(core_pair, ring, side))
    moist, tail = faces(moist, core_pair, rest_pair, ring, got, rain)
    heads_chip = gate(chip_swap(heads), stored=(moist,))
    heads_core = core_swap(heads)
    heads_both = core_swap(heads_chip)
    return bottom(moist, tail, heads, heads_core, heads_chip, heads_both)


def solution(mesh):
    in_specs = (
        P("depth", "strips", None),
        P("depth", "strips", None),
        P("depth", "strips", None),
        P("strips", None),
        P(),
        P(),
        P(),
        P("strips", "depth"),
        P("strips", "depth"),
        P("strips", "depth"),
    )
    out_specs = (P("depth", "strips", None), P("strips", "depth"))
    return jax.shard_map(shards, mesh=mesh, in_specs=in_specs, out_specs=out_specs, check_vma=False)
```

```python
import functools
import math

import jax
import jax.numpy as jnp
from jax import lax
from jax.experimental import pallas as pl
from jax.experimental.pallas import tpu as pltpu
from jax.sharding import PartitionSpec as P

SWEEPS = 3
SUB = 8
PARTS = 2
LANE = 128
WIDTH = 4

layer_thick = 0.05
soil_step = 0.0002
spec_yield = 0.02
leak_rate = 0.5
river_cond = 0.5
fixed_cond = 3.0
residual = 0.15
mobile = 0.85

VMEM = pl.BlockSpec(memory_space=pltpu.VMEM)
ANY = pl.BlockSpec(memory_space=pl.ANY)
HBM = pl.BlockSpec(memory_space=pltpu.HBM)


def params(mib):
    return pltpu.CompilerParams(vmem_limit_bytes=mib * 2**20)


def cost(flops, nbytes, trans=0):
    return pl.CostEstimate(flops=int(flops), bytes_accessed=int(nbytes), transcendentals=int(trans))


def place():
    depth = lax.axis_index("depth")
    return depth // 2, depth % 2


def gathered(table, classes):
    return jnp.take_along_axis(table, classes, axis=1, mode="promise_in_bounds")


def picked(options, bits):
    for bit in bits:
        options = [
            jnp.where(bit, options[i + 1], options[i]) if i + 1 < len(options) else options[i]
            for i in range(0, len(options), 2)
        ]
    return options[0]


def fill_tables(tab, sat_ref, alpha_ref, theta_ref):
    classes = sat_ref.shape[1]
    scaled = (sat_ref, 1.0), (alpha_ref, 0.5 * math.log2(math.e)), (theta_ref, mobile)
    for i, (ref, scale) in enumerate(scaled):
        tab[i, :, :classes] = jnp.broadcast_to(ref[...] * scale, (SUB, classes))


def face_kernel(
    sat_hbm, alpha_hbm, psi_hbm, tex_hbm, act_hbm, out_ref, kinds, acts, given, tab, sems
):
    chip, _ = place()
    layer = (1 - chip) * (psi_hbm.shape[0] - 1)
    cols = psi_hbm.shape[2]
    classes = sat_hbm.shape[1]
    copies = [
        pltpu.make_async_copy(src, dst, sems.at[i])
        for i, (src, dst) in enumerate(
            (
                (sat_hbm, given.at[0]),
                (alpha_hbm, given.at[1]),
                (psi_hbm.at[layer], out_ref.at[0]),
                (tex_hbm.at[layer], kinds),
                (act_hbm.at[layer], acts),
            )
        )
    ]
    for c in copies:
        c.start()
    for c in copies:
        c.wait()
    for i, scale in enumerate((1.0, 0.5 * math.log2(math.e))):
        tab[i, :, :classes] = jnp.broadcast_to(given[i] * scale, (SUB, classes))

    def columns(q, carry):
        lanes = pl.ds(pl.multiple_of(q * LANE, LANE), LANE)
        for r in range(0, kinds.shape[0], SUB):
            rws = slice(r, r + SUB)
            kind = kinds[rws, lanes]
            wet = jnp.exp2(gathered(tab[1], kind) * jnp.minimum(out_ref[0, rws, lanes], 0.0))
            active = acts[rws, lanes].astype(jnp.float32)
            out_ref[1, rws, lanes] = gathered(tab[0], kind) * active * (wet * wet)
        return carry

    lax.fori_loop(0, cols // LANE, columns, 0, unroll=4)


def in_hbm(*arrays):
    return [pltpu.with_memory_space_constraint(x, pltpu.HBM) for x in arrays]


def face(tables, pressure, texture, active):
    _, nrows, cols = pressure.shape
    size = nrows * cols
    return pl.pallas_call(
        face_kernel,
        in_specs=[HBM] * 5,
        out_specs=VMEM,
        out_shape=jax.ShapeDtypeStruct((2, nrows, cols), jnp.float32),
        scratch_shapes=[
            pltpu.VMEM((nrows, cols), jnp.int32),
            pltpu.VMEM((nrows, cols), jnp.int32),
            pltpu.VMEM((2,) + tables[0].shape, jnp.float32),
            pltpu.VMEM((2, SUB, LANE), jnp.float32),
            pltpu.SemaphoreType.DMA((5,)),
        ],
        compiler_params=params(8),
        cost_estimate=cost(20 * size, 20 * size, size),
        name="face",
    )(*in_hbm(*tables[:2], pressure, texture, active))


def soil_kernel(
    sat_ref, alpha_ref, theta_ref, psi_ref, tex_ref, act_ref, old_ref, code_ref, section_ref,
    moist_ref, keep_ref, send_ref, mine_ref, give_ref, core_ref, rest_ref, tab, part, tile,
):
    step = pl.program_id(0)
    _, core = place()
    layers, rows, cols = psi_ref.shape
    classes = sat_ref.shape[1]

    @pl.when(step == 0)
    def _():
        fill_tables(tab, sat_ref, alpha_ref, theta_ref)

    sat_tab, par_tab = tab[0], tab[1]
    theta = [jnp.broadcast_to(tab[2, :, i : i + 1], (SUB, LANE)) for i in range(classes)]
    nbits = max(1, (classes - 1).bit_length())
    face = 0.5 * soil_step / layer_thick
    core_layer = (1 - core) * (layers - 1)
    rest_layer = core * (layers - 1)

    def columns(q, carry):
        lanes = pl.ds(pl.multiple_of(q * LANE, LANE), LANE)
        for r in range(0, rows, SUB):
            rws = slice(r, r + SUB)
            trans = store = charge = jnp.zeros((SUB, LANE), jnp.float32)
            for layer in range(layers):
                kind = tex_ref[layer, rws, lanes]
                psi = psi_ref[layer, rws, lanes]
                active = act_ref[layer, rws, lanes].astype(jnp.float32)
                bits = [(kind & (1 << b)) != 0 for b in range(nbits)]
                wet = jnp.exp2(gathered(par_tab, kind) * jnp.minimum(psi, 0.0))
                cond = gathered(sat_tab, kind) * active * (wet * wet)
                mob = picked(theta, bits)
                mobwet = mob * wet
                trans = trans + cond
                charge = charge + cond * wet
                store = store + (mob - mobwet)
                held = mob * (residual / mobile) + mobwet
                if layer == 0:
                    first, own = cond, held
                else:
                    flux = (cond_up + cond) * ((psi_up - psi) * (face / layer_thick) + face)
                    moist_ref[layer - 1, rws, lanes] = own - flux
                    own = held + flux
                psi_up, cond_up = psi, cond
            moist_ref[layers - 1, rws, lanes] = own
            part[r // SUB, 0, :, lanes] = trans
            part[r // SUB, 1, :, lanes] = store
            part[r // SUB, 2, :, lanes] = charge
            core_ref[0, rws, lanes] = psi_ref[core_layer, rws, lanes]
            core_ref[1, rws, lanes] = jnp.where(core == 0, cond, first)
            rest_ref[0, rws, lanes] = psi_ref[rest_layer, rws, lanes]
            rest_ref[1, rws, lanes] = jnp.where(core == 0, first, cond)
        return carry

    lax.fori_loop(0, cols // LANE, columns, 0, unroll=8)

    blocks = rows // SUB
    for r in range(blocks):
        at = pl.ds(pl.multiple_of(step * rows + r * SUB, SUB), SUB)
        code = code_ref[at]
        river = jnp.where(code == 1, river_cond, jnp.where(code == 2, fixed_cond, 0.0))
        for a, value in enumerate((old_ref[at], river, river * section_ref[at])):
            tile[r, a] = value

    half = keep_ref.shape[0] - 1
    for r in range(blocks):
        block = step * blocks + r

        def put(ref, tile_ref, at):
            ref[at] = part[r]
            tile_ref[at] = tile[r]

        @pl.when((block <= half) & (core == 0))
        def _():
            put(keep_ref, mine_ref, block)

        @pl.when((block <= half) & (core == 1))
        def _():
            put(send_ref, give_ref, block)

        @pl.when((block >= half - 1) & (core == 0))
        def _():
            put(send_ref, give_ref, block - (half - 1))

        @pl.when((block >= half - 1) & (core == 1))
        def _():
            put(keep_ref, mine_ref, block - (half - 1))


def soil(tables, pressure, texture, active, head_old, cell_code, section):
    layers, nrows, cols = pressure.shape
    classes = tables[0].shape[1]
    rows = nrows // 4
    blocks = nrows // (2 * SUB) + 1
    whole = pl.BlockSpec((1, classes), lambda j: (0, 0))
    block = pl.BlockSpec((layers, rows, cols), lambda j: (0, j, 0))
    pair = pl.BlockSpec((2, rows, cols), lambda j: (0, j, 0))
    msg = jax.ShapeDtypeStruct((blocks, 3, SUB, cols), jnp.float32)
    msg_spec = pl.BlockSpec(msg.shape, lambda j: (0, 0, 0, 0))
    tile = pl.BlockSpec(head_old.shape, lambda j: (0, 0))
    part = jax.ShapeDtypeStruct((blocks, 3, SUB, head_old.shape[1]), jnp.float32)
    part_spec = pl.BlockSpec(part.shape, lambda j: (0, 0, 0, 0))
    layer2 = jax.ShapeDtypeStruct((2, nrows, cols), jnp.float32)
    size = layers * nrows * cols
    return pl.pallas_call(
        soil_kernel,
        grid=(nrows // rows,),
        in_specs=[whole, whole, whole, block, block, block, tile, tile, tile],
        out_specs=[block, msg_spec, msg_spec, part_spec, part_spec, pair, pair],
        out_shape=[jax.ShapeDtypeStruct((layers, nrows, cols), jnp.float32), msg, msg, part, part, layer2, layer2],
        scratch_shapes=[
            pltpu.VMEM((3, SUB, LANE), jnp.float32),
            pltpu.VMEM((rows // SUB, 3, SUB, cols), jnp.float32),
            pltpu.VMEM((rows // SUB, 3, SUB, head_old.shape[1]), jnp.float32),
        ],
        compiler_params=params(32),
        cost_estimate=cost(60 * size, 20 * size, size),
        name="soil",
    )(*in_hbm(*tables, pressure, texture, active, head_old, cell_code, section))


def edge_lane(chip):
    return (1 - chip) * (LANE - WIDTH)


def on_edge(value, chip):
    lane = lax.broadcasted_iota(jnp.int32, value.shape, 1)
    base = edge_lane(chip)
    return jnp.where((lane >= base) & (lane < base + WIDTH), value, 0.0)


def shift(array, block=0):
    return WIDTH * (6 * block + array)


SHARE = LANE // (6 * WIDTH)


def packed(pieces, chip, block=0):
    total = None
    for a, piece in enumerate(pieces):
        moved = pltpu.roll(on_edge(piece, chip), shift(a, block), 1)
        total = moved if total is None else total + moved
    return total


def unpacked(tile, array, block=0):
    return pltpu.roll(tile, LANE - shift(array, block), 1)


def nearest(block, core):
    return jnp.where(core == 0, block[:SWEEPS], block[SUB - SWEEPS :])


def spread(rows, core):
    zeros = jnp.zeros((SUB - SWEEPS, rows.shape[1]), rows.dtype)
    return jnp.where(core == 0, jnp.concatenate([rows, zeros], 0), jnp.concatenate([zeros, rows], 0))


def put_rows(ref, plane, pieces):
    used = sum(piece.shape[0] for piece in pieces)
    spare = jnp.zeros((2 * SUB - used, pieces[0].shape[1]), jnp.float32)
    rows = jnp.concatenate([*pieces, spare], 0)
    ref[plane] = rows[:SUB]
    ref[plane + 1] = rows[SUB:]


def get_rows(ref, plane, counts):
    rows = jnp.concatenate([ref[plane], ref[plane + 1]], 0)
    out, at = [], 0
    for count in counts:
        out.append(rows[at : at + count])
        at += count
    return out


def fold(tiles):
    mid = SUB // 2
    return jnp.concatenate([part for tile in tiles for part in (tile[:mid], tile[mid:])], 1)


def unfold(rows):
    parts = [rows[:, i : i + LANE] for i in range(0, rows.shape[1], LANE)]
    return [jnp.concatenate(parts[i : i + 2], 0) for i in range(0, len(parts), 2)]


def half_lanes(which, half):
    return pl.ds(pl.multiple_of(which * half, half), half)


def slab_lanes(chip, half):
    return pl.ds(pl.multiple_of(half - LANE + chip * LANE, LANE), LANE)


def tile_rows(mine_ref, other_ref, b, core, which, array, start, stop):
    lanes = slice(start, stop)
    return jnp.where(core == which, mine_ref[b, array, :, lanes], other_ref[b, array, :, lanes])


def edge_inputs(mine_ref, other_ref, b, chip, core):
    tile = mine_ref.shape[3]
    out = []
    for a in range(3):
        left = tile_rows(mine_ref, other_ref, b, core, 1, a, tile - LANE, tile)
        right = tile_rows(mine_ref, other_ref, b, core, 0, a, 0, LANE)
        out.append(jnp.where(chip == 0, left, right))
    return out


def pack_kernel(keep_ref, recv_ref, mine_ref, other_ref, out_ref):
    chip, core = place()
    blocks, _, _, cols = keep_ref.shape
    half = cols // 2
    away = half_lanes(1 - chip, half)
    slab = slab_lanes(chip, half)
    main = 3 * (blocks - 1)
    tiles = [None] * -(-blocks // SHARE)
    for j in range(blocks):
        b = j + core if j < blocks - 1 else (1 - core) * (blocks - 1)
        sums = [keep_ref[b, a, :, away] + recv_ref[b, a, :, away] for a in range(3)]
        if j < blocks - 1:
            for a in range(3):
                out_ref[3 * j + a] = sums[a]
        else:
            rows = [nearest(v, core) for v in sums]
        pieces = [keep_ref[b, a, :, slab] + recv_ref[b, a, :, slab] for a in range(3)]
        pieces += edge_inputs(mine_ref, other_ref, b, chip, core)
        piece = packed(pieces, chip, j % SHARE)
        i = j // SHARE
        tiles[i] = piece if tiles[i] is None else tiles[i] + piece
    put_rows(out_ref, main, [*rows, fold(tiles)])


def pack(keep, recv, mine, other):
    blocks, _, _, cols = keep.shape
    half = cols // 2
    return pl.pallas_call(
        pack_kernel,
        in_specs=[VMEM] * 4,
        out_specs=VMEM,
        out_shape=jax.ShapeDtypeStruct((3 * blocks - 1, SUB, half), jnp.float32),
        compiler_params=params(8),
        cost_estimate=cost(keep.size, 12 * keep.size),
        name="pack",
    )(keep, recv, mine, other)


def rim_kernel(keep_ref, recv_ref, mine_ref, other_ref, *refs):
    side_ref, cross_ref = refs[-2:]
    chip, core = place()
    blocks, _, _, cols = keep_ref.shape
    half = cols // 2
    tile = half // 2
    b = core * (blocks - 1)
    near, away = half_lanes(chip, half), half_lanes(1 - chip, half)
    side_ref[:3] = keep_ref[b, :, :, near] + recv_ref[b, :, :, near]
    rows = [nearest(keep_ref[b, a, :, away] + recv_ref[b, a, :, away], core) for a in range(3)]
    for which in range(2):
        for a in range(3):
            side_ref[3 + a, :, which * tile : (which + 1) * tile] = tile_rows(
                mine_ref, other_ref, b, core, which, a, 0, tile
            )

    def sums(slab):
        return [keep_ref[b, a, :, slab] + recv_ref[b, a, :, slab] for a in range(3)]

    side_ref[6, :, :LANE] = packed(sums(slab_lanes(1 - chip, half)), 1 - chip)
    inputs = edge_inputs(mine_ref, other_ref, b, chip, core)
    halo = nearest(packed(sums(slab_lanes(chip, half)) + inputs, chip), core)
    spare = jnp.zeros((SWEEPS, half - LANE), jnp.float32)
    put_rows(cross_ref, 0, [*rows, jnp.concatenate([halo, spare], 1)])


def rim(keep, recv, mine, other, *first):
    half = keep.shape[3] // 2
    return pl.pallas_call(
        rim_kernel,
        in_specs=[VMEM] * 4 + [ANY] * len(first),
        out_specs=[VMEM] * 2,
        out_shape=[jax.ShapeDtypeStruct((n, SUB, half), jnp.float32) for n in (7, 2)],
        compiler_params=params(8),
        cost_estimate=cost(keep.size // 8, keep.size),
        name="rim",
    )(keep, recv, mine, other, *first)


def sweep_kernel(keep_ref, recv_ref, mine_ref, other_ref, far_ref, side_ref, cross_ref, out_ref, left_ref, right_ref, work):
    chip, core = place()
    strip = lax.axis_index("strips")
    blocks, _, _, cols = keep_ref.shape
    half = cols // 2
    tile = half // 2
    main = 3 * (blocks - 1)

    def cells(at, lanes, sums, inputs):
        trans = sums[0] * layer_thick
        store = spec_yield + sums[1] * layer_thick
        old, river, inflow = inputs
        rows = pl.ds(pl.multiple_of(at * SUB, SUB), SUB)
        work[0, rows, lanes] = trans
        work[1, rows, lanes] = store + river
        work[2, rows, lanes] = store * old + leak_rate * layer_thick * sums[2] + inflow
        work[3, rows, lanes] = old

    def halo(at, sums, inputs):
        sums, inputs = ([on_edge(v, 1 - chip) for v in values] for values in (sums, inputs))
        cells(at, slice(half, half + LANE), sums, inputs)

    near, slab = half_lanes(chip, half), slab_lanes(1 - chip, half)
    *beyond, tiles = get_rows(far_ref, main, (SWEEPS, SWEEPS, SWEEPS, SUB // 2))
    tiles = unfold(tiles)
    for j in range(blocks):
        b = j + core if j < blocks - 1 else (1 - core) * (blocks - 1)
        if j < blocks - 1:
            far = [far_ref[3 * j + a] for a in range(3)]
        else:
            far = [spread(v, core) for v in beyond]
        sums = [keep_ref[b, a, :, near] + recv_ref[b, a, :, near] + far[a] for a in range(3)]
        for which in range(2):
            lanes = slice(which * tile, (which + 1) * tile)
            inputs = [tile_rows(mine_ref, other_ref, b, core, which, a, 0, tile) for a in range(3)]
            cells(b, lanes, [s[:, lanes] for s in sums], inputs)
        far = [unpacked(tiles[j // SHARE], a, j % SHARE) for a in range(6)]
        sums = [keep_ref[b, a, :, slab] + recv_ref[b, a, :, slab] + far[a] for a in range(3)]
        halo(b, sums, far[3:])
    outside = ((core == 0) & (strip == 0)) | ((core == 1) & (strip == lax.axis_size("strips") - 1))

    def inside(value):
        return jnp.where(outside, 0.0, value)

    *cross, corner = [spread(v, 1 - core) for v in get_rows(cross_ref, 0, (SWEEPS,) * 4)]
    sums = [inside(side_ref[a] + cross[a]) for a in range(3)]
    cells(blocks, slice(0, half), sums, [inside(side_ref[3 + a]) for a in range(3)])
    side, cross = side_ref[6, :, :LANE], corner[:, :LANE]
    sums = [inside(unpacked(side, a) + unpacked(cross, a)) for a in range(3)]
    halo(blocks, sums, [inside(unpacked(cross, a)) for a in range(3, 6)])

    trans, base, rhs, head = (work[i] for i in range(4))
    rows, lanes = trans.shape
    right = jnp.sqrt(trans * pltpu.roll(trans, lanes - 1, 1))
    left = pltpu.roll(right, 1, 1)
    down = jnp.sqrt(trans * pltpu.roll(trans, rows - 1, 0))
    up = pltpu.roll(down, 1, 0)
    inverse = 1.0 / (base + right + left + down + up)
    for _ in range(SWEEPS):
        head = inverse * (
            rhs
            + right * pltpu.roll(head, lanes - 1, 1)
            + left * pltpu.roll(head, 1, 1)
            + down * pltpu.roll(head, rows - 1, 0)
            + up * pltpu.roll(head, 1, 0)
        )
    work[0] = head
    out_ref[...] = work[0, pl.ds(pl.multiple_of(core * SUB, SUB), out_ref.shape[0]), :half]
    left_ref[...] = out_ref[:, :tile]
    right_ref[...] = out_ref[:, tile:]


def sweeps(keep, recv, mine, other, far, side, cross):
    blocks = keep.shape[0]
    half = keep.shape[3] // 2
    return pl.pallas_call(
        sweep_kernel,
        in_specs=[VMEM] * 7,
        out_specs=[VMEM] * 3,
        out_shape=[
            jax.ShapeDtypeStruct(((blocks - 1) * SUB, half // part), jnp.float32) for part in (1, 2, 2)
        ],
        scratch_shapes=[pltpu.VMEM((4, (blocks + 1) * SUB, half + LANE), jnp.float32)],
        compiler_params=params(12),
        cost_estimate=cost(20 * keep.size, 12 * keep.size),
        name="sweeps",
    )(keep, recv, mine, other, far, side, cross)


def pass_on_kernel(core_ref, ring_ref, first, *out_refs):
    del first
    chip, core = place()
    rows = out_refs[0].shape[1]
    for i, out_ref in enumerate(out_refs):
        part = slice(i * rows, (i + 1) * rows)

        @pl.when(chip == core)
        def _():
            out_ref[...] = ring_ref[:, part]

        @pl.when(chip != core)
        def _():
            out_ref[...] = core_ref[:, part]


def pass_on(core_pair, ring, first):
    return pl.pallas_call(
        pass_on_kernel,
        in_specs=[VMEM] * 2 + [ANY],
        out_specs=[VMEM] * PARTS,
        out_shape=[jax.ShapeDtypeStruct((2, ring.shape[1] // PARTS, ring.shape[2]), ring.dtype)] * PARTS,
        compiler_params=params(8),
        cost_estimate=cost(ring.size, 8 * ring.size),
        name="pass_on",
    )(core_pair, ring, first)


def faces_kernel(moist_in, core_ref, rest_ref, ring_ref, rain_ref, *refs):
    del moist_in
    got_refs, (moist_out, tail_ref, ends, sems) = refs[:PARTS], refs[PARTS:]
    chip, core = place()
    layers = moist_out.shape[0]
    copies = [
        (moist_out.at[layer], ends.at[i], sems.at[i]) for i, layer in enumerate((0, layers - 1))
    ]
    loads = [pltpu.make_async_copy(src, dst, sem) for src, dst, sem in copies]
    stores = [pltpu.make_async_copy(dst, src, sem) for src, dst, sem in copies]
    for c in loads:
        c.start()
    for c in loads:
        c.wait()
    gain = soil_step / layer_thick
    face = 0.5 * gain
    last = (core == 1) & (chip == 1)

    def flux(upper, lower):
        return (upper[1] + lower[1]) * ((upper[0] - lower[0]) * (face / layer_thick) + face)

    def got_faces(which, sign, ref, below):
        for i, got in enumerate(got_refs):
            rows = got.shape[1]
            part = slice(i * rows, (i + 1) * rows)
            mine = ref[0, part], ref[1, part]
            change = flux(mine, got) if below else flux(got, mine)
            ends[which, part] = ends[which, part] + sign * change

    @pl.when((core == 0) & (chip == 0))
    def _():
        ends[0] = ends[0] + gain * rain_ref[...]
        got_faces(1, -1.0, core_ref, True)

    @pl.when((core == 1) & (chip == 0))
    def _():
        ends[0] = ends[0] + flux(ring_ref, core_ref)
        got_faces(1, -1.0, rest_ref, True)

    @pl.when((core == 0) & (chip == 1))
    def _():
        got_faces(0, 1.0, rest_ref, False)
        ends[1] = ends[1] - flux(core_ref, ring_ref)

    @pl.when(last)
    def _():
        got_faces(0, 1.0, core_ref, False)

    stores[0].start()

    @pl.when(last)
    def _():
        slope = rest_ref[1] * (gain / (0.5 * layer_thick))
        tail_ref[0] = ends[1] - (rest_ref[0] * slope + gain * rest_ref[1])
        tail_ref[1] = slope

    @pl.when(jnp.logical_not(last))
    def _():
        stores[1].start()
        stores[1].wait()

    stores[0].wait()


def faces(moist, core_pair, rest_pair, ring, got, rain):
    return pl.pallas_call(
        faces_kernel,
        in_specs=[ANY] + [VMEM] * (4 + PARTS),
        out_specs=[ANY, VMEM],
        out_shape=[
            jax.ShapeDtypeStruct(moist.shape, moist.dtype),
            jax.ShapeDtypeStruct((2,) + moist.shape[1:], moist.dtype),
        ],
        input_output_aliases={0: 0},
        scratch_shapes=[pltpu.VMEM((2,) + moist.shape[1:], jnp.float32), pltpu.SemaphoreType.DMA((2,))],
        compiler_params=params(12),
        cost_estimate=cost(20 * rain.size, 32 * rain.size),
        name="faces",
    )(moist, core_pair, rest_pair, ring, rain, *got)


def near_bottom_kernel(moist_in, tail_ref, own_ref, left_ref, right_ref, moist_out, head_ref, done, sem):
    del moist_in
    chip, core = place()
    layers = moist_out.shape[0]
    rows, half = own_ref.shape
    tile = half // 2
    mine = pl.ds(pl.multiple_of(core * rows, rows), rows)
    theirs = pl.ds(pl.multiple_of((1 - core) * rows, rows), rows)
    store = pltpu.make_async_copy(done, moist_out.at[layers - 1, :, half:], sem)

    @pl.when((core == 1) & (chip == 1))
    def _():
        for i, ref in enumerate((left_ref, right_ref)):
            to, at = slice(i * tile, (i + 1) * tile), slice(half + i * tile, half + (i + 1) * tile)
            done[:rows, to] = tail_ref[0, :rows, at] + tail_ref[1, :rows, at] * ref[...]
        done[rows:] = tail_ref[0, rows:, half:] + tail_ref[1, rows:, half:] * own_ref[...]
        store.start()

    head_ref[mine, :] = own_ref[:, pl.ds(pl.multiple_of(core * tile, tile), tile)]
    head_ref[theirs, :] = jnp.where(core == 0, left_ref[...], right_ref[...])

    @pl.when((core == 1) & (chip == 1))
    def _():
        store.wait()


def near_bottom(moist, tail, own, left, right):
    rows, half = own.shape
    return pl.pallas_call(
        near_bottom_kernel,
        in_specs=[ANY] + [VMEM] * 4,
        out_specs=[ANY, VMEM],
        out_shape=[
            jax.ShapeDtypeStruct(moist.shape, moist.dtype),
            jax.ShapeDtypeStruct((2 * rows, half // 2), jnp.float32),
        ],
        input_output_aliases={0: 0},
        scratch_shapes=[pltpu.VMEM((2 * rows, half), jnp.float32), pltpu.SemaphoreType.DMA],
        compiler_params=params(12),
        cost_estimate=cost(10 * own.size, 40 * own.size),
        name="near_bottom",
    )(moist, tail, own, left, right)


def bottom_kernel(moist_in, tail_ref, chip_far, both_far, moist_out, done, sem):
    del moist_in
    chip, core = place()
    layers = moist_out.shape[0]
    rows, half = chip_far.shape

    @pl.when((core == 1) & (chip == 1))
    def _():
        store = pltpu.make_async_copy(done, moist_out.at[layers - 1, :, :half], sem)
        for ref, where in ((both_far, slice(0, rows)), (chip_far, slice(rows, 2 * rows))):
            done[where] = tail_ref[0, where, :half] + tail_ref[1, where, :half] * ref[...]
        store.start()
        store.wait()


def bottom(moist, tail, chip_far, both_far):
    rows, half = chip_far.shape
    return pl.pallas_call(
        bottom_kernel,
        in_specs=[ANY] + [VMEM] * 3,
        out_specs=ANY,
        out_shape=jax.ShapeDtypeStruct(moist.shape, moist.dtype),
        input_output_aliases={0: 0},
        scratch_shapes=[pltpu.VMEM((2 * rows, half), jnp.float32), pltpu.SemaphoreType.DMA],
        compiler_params=params(12),
        cost_estimate=cost(4 * chip_far.size, 24 * chip_far.size),
        name="bottom",
    )(moist, tail, chip_far, both_far)


def gate_kernel(*refs):
    del refs


def gate(value, *first, stored=()):
    return pl.pallas_call(
        gate_kernel,
        in_specs=[ANY] * (1 + len(first)) + [HBM] * len(stored),
        out_specs=ANY,
        out_shape=jax.ShapeDtypeStruct(value.shape, value.dtype),
        input_output_aliases={0: 0},
        compiler_params=params(1),
        cost_estimate=cost(1, 1),
        name="gate",
    )(value, *first, *in_hbm(*stored))


def core_swap(value):
    return lax.ppermute(value, "depth", [(i, i ^ 1) for i in range(lax.axis_size("depth"))])


def chip_swap(value):
    return lax.ppermute(value, "depth", [(i, i ^ 2) for i in range(lax.axis_size("depth"))])


def ring_shift(value):
    return lax.ppermute(value, "depth", [(1, 3), (3, 2), (2, 0), (0, 1)])


def strip_swap(value, chips=0):
    depth, strips = lax.axis_size("depth"), lax.axis_size("strips")
    pairs = []
    for d in range(1, depth, 2):
        for s in range(strips):
            lower, upper = d * strips + s, ((d - 1) ^ chips) * strips + (s + 1) % strips
            pairs += [(lower, upper), (upper, lower)]
    return lax.ppermute(value, ("depth", "strips"), pairs)


def shards(pressure, texture, active, rain, k_sat, alpha, theta_sat, head_old, cell_code, section):
    tables = (k_sat[None], alpha[None], theta_sat[None])
    face_pair = face(tables, pressure, texture, active)
    ring = ring_shift(face_pair)
    moist, keep, send, mine, give, core_pair, rest_pair = soil(
        tables, pressure, texture, active, head_old, cell_code, section
    )
    recv, other = core_swap(send), core_swap(give)
    keep = gate(keep, ring)
    message = pack(keep, recv, mine, other)
    far = chip_swap(message)
    side, cross = rim(keep, recv, mine, other, message)
    heads, left, right = sweeps(keep, recv, mine, other, far, strip_swap(side), strip_swap(cross, 2))
    got = [core_swap(part) for part in pass_on(core_pair, ring, side)]
    moist, tail = faces(moist, core_pair, rest_pair, ring, got, rain)
    moist, head = near_bottom(moist, tail, heads, core_swap(left), core_swap(right))
    heads_chip = gate(chip_swap(heads), stored=(moist,))
    return bottom(moist, tail, heads_chip, core_swap(heads_chip)), head


def solution(mesh):
    in_specs = (
        P("depth", "strips", None),
        P("depth", "strips", None),
        P("depth", "strips", None),
        P("strips", None),
        P(),
        P(),
        P(),
        P("strips", "depth"),
        P("strips", "depth"),
        P("strips", "depth"),
    )
    out_specs = (P("depth", "strips", None), P("strips", "depth"))
    return jax.shard_map(shards, mesh=mesh, in_specs=in_specs, out_specs=out_specs, check_vma=False)
```

```python
import functools
import math

import jax
import jax.numpy as jnp
from jax import lax
from jax.experimental import pallas as pl
from jax.experimental.pallas import tpu as pltpu
from jax.sharding import PartitionSpec as P

SWEEPS = 3
SUB = 8
PARTS = 2
LANE = 128
WIDTH = 4

layer_thick = 0.05
soil_step = 0.0002
spec_yield = 0.02
leak_rate = 0.5
river_cond = 0.5
fixed_cond = 3.0
residual = 0.15
mobile = 0.85

VMEM = pl.BlockSpec(memory_space=pltpu.VMEM)
ANY = pl.BlockSpec(memory_space=pl.ANY)
HBM = pl.BlockSpec(memory_space=pltpu.HBM)


def params(mib):
    return pltpu.CompilerParams(vmem_limit_bytes=mib * 2**20)


def cost(flops, nbytes, trans=0):
    return pl.CostEstimate(flops=int(flops), bytes_accessed=int(nbytes), transcendentals=int(trans))


def place():
    depth = lax.axis_index("depth")
    return depth // 2, depth % 2


def gathered(table, classes):
    return jnp.take_along_axis(table, classes, axis=1, mode="promise_in_bounds")


def picked(options, bits):
    for bit in bits:
        options = [
            jnp.where(bit, options[i + 1], options[i]) if i + 1 < len(options) else options[i]
            for i in range(0, len(options), 2)
        ]
    return options[0]


def fill_tables(tab, sat_ref, alpha_ref, theta_ref):
    classes = sat_ref.shape[1]
    scaled = (sat_ref, 1.0), (alpha_ref, 0.5 * math.log2(math.e)), (theta_ref, mobile)
    for i, (ref, scale) in enumerate(scaled):
        tab[i, :, :classes] = jnp.broadcast_to(ref[...] * scale, (SUB, classes))


def face_kernel(
    sat_hbm, alpha_hbm, psi_hbm, tex_hbm, act_hbm, out_ref, kinds, acts, given, tab, sems
):
    chip, _ = place()
    layer = (1 - chip) * (psi_hbm.shape[0] - 1)
    cols = psi_hbm.shape[2]
    classes = sat_hbm.shape[1]
    chunks = 2
    rows = kinds.shape[0] // chunks

    def copies(i):
        part = pl.ds(i * rows, rows)
        pairs = (
            (psi_hbm.at[layer, part], out_ref.at[0, part]),
            (tex_hbm.at[layer, part], kinds.at[part]),
            (act_hbm.at[layer, part], acts.at[part]),
        )
        return [pltpu.make_async_copy(src, dst, sems.at[i, k]) for k, (src, dst) in enumerate(pairs)]

    tables = [
        pltpu.make_async_copy(src, given.at[k], sems.at[chunks, k]) for k, src in enumerate((sat_hbm, alpha_hbm))
    ]
    for c in tables:
        c.start()
    for i in range(chunks):
        for c in copies(i):
            c.start()
    for c in tables:
        c.wait()
    for i, scale in enumerate((1.0, 0.5 * math.log2(math.e))):
        tab[i, :, :classes] = jnp.broadcast_to(given[i] * scale, (SUB, classes))

    for i in range(chunks):
        for c in copies(i):
            c.wait()

        def columns(q, carry):
            lanes = pl.ds(pl.multiple_of(q * LANE, LANE), LANE)
            for r in range(i * rows, (i + 1) * rows, SUB):
                rws = slice(r, r + SUB)
                kind = kinds[rws, lanes]
                wet = jnp.exp2(gathered(tab[1], kind) * jnp.minimum(out_ref[0, rws, lanes], 0.0))
                active = acts[rws, lanes].astype(jnp.float32)
                out_ref[1, rws, lanes] = gathered(tab[0], kind) * active * (wet * wet)
            return carry

        lax.fori_loop(0, cols // LANE, columns, 0, unroll=8)


def in_hbm(*arrays):
    return [pltpu.with_memory_space_constraint(x, pltpu.HBM) for x in arrays]


def face(tables, pressure, texture, active):
    _, nrows, cols = pressure.shape
    size = nrows * cols
    return pl.pallas_call(
        face_kernel,
        in_specs=[HBM] * 5,
        out_specs=VMEM,
        out_shape=jax.ShapeDtypeStruct((2, nrows, cols), jnp.float32),
        scratch_shapes=[
            pltpu.VMEM((nrows, cols), jnp.int32),
            pltpu.VMEM((nrows, cols), jnp.int32),
            pltpu.VMEM((2,) + tables[0].shape, jnp.float32),
            pltpu.VMEM((2, SUB, LANE), jnp.float32),
            pltpu.SemaphoreType.DMA((3, 3)),
        ],
        compiler_params=params(8),
        cost_estimate=cost(20 * size, 20 * size, size),
        name="face",
    )(*in_hbm(*tables[:2], pressure, texture, active))


def soil_kernel(
    sat_ref, alpha_ref, theta_ref, psi_ref, tex_ref, act_ref, old_ref, code_ref, section_ref,
    moist_ref, keep_ref, send_ref, mine_ref, give_ref, core_ref, rest_ref, tab, part, tile,
):
    step = pl.program_id(0)
    _, core = place()
    layers, rows, cols = psi_ref.shape
    classes = sat_ref.shape[1]

    @pl.when(step == 0)
    def _():
        fill_tables(tab, sat_ref, alpha_ref, theta_ref)

    sat_tab, par_tab = tab[0], tab[1]
    theta = [jnp.broadcast_to(tab[2, :, i : i + 1], (SUB, LANE)) for i in range(classes)]
    nbits = max(1, (classes - 1).bit_length())
    face = 0.5 * soil_step / layer_thick
    core_layer = (1 - core) * (layers - 1)
    rest_layer = core * (layers - 1)

    def columns(q, carry):
        lanes = pl.ds(pl.multiple_of(q * LANE, LANE), LANE)
        for r in range(0, rows, SUB):
            rws = slice(r, r + SUB)
            trans = store = charge = jnp.zeros((SUB, LANE), jnp.float32)
            for layer in range(layers):
                kind = tex_ref[layer, rws, lanes]
                psi = psi_ref[layer, rws, lanes]
                active = act_ref[layer, rws, lanes].astype(jnp.float32)
                bits = [(kind & (1 << b)) != 0 for b in range(nbits)]
                wet = jnp.exp2(gathered(par_tab, kind) * jnp.minimum(psi, 0.0))
                cond = gathered(sat_tab, kind) * active * (wet * wet)
                mob = picked(theta, bits)
                mobwet = mob * wet
                trans = trans + cond
                charge = charge + cond * wet
                store = store + (mob - mobwet)
                held = mob * (residual / mobile) + mobwet
                if layer == 0:
                    first, own = cond, held
                else:
                    flux = (cond_up + cond) * ((psi_up - psi) * (face / layer_thick) + face)
                    moist_ref[layer - 1, rws, lanes] = own - flux
                    own = held + flux
                psi_up, cond_up = psi, cond
            moist_ref[layers - 1, rws, lanes] = own
            part[r // SUB, 0, :, lanes] = trans
            part[r // SUB, 1, :, lanes] = store
            part[r // SUB, 2, :, lanes] = charge
            core_ref[0, rws, lanes] = psi_ref[core_layer, rws, lanes]
            core_ref[1, rws, lanes] = jnp.where(core == 0, cond, first)
            rest_ref[0, rws, lanes] = psi_ref[rest_layer, rws, lanes]
            rest_ref[1, rws, lanes] = jnp.where(core == 0, first, cond)
        return carry

    lax.fori_loop(0, cols // LANE, columns, 0, unroll=8)

    blocks = rows // SUB
    for r in range(blocks):
        at = pl.ds(pl.multiple_of(step * rows + r * SUB, SUB), SUB)
        code = code_ref[at]
        river = jnp.where(code == 1, river_cond, jnp.where(code == 2, fixed_cond, 0.0))
        for a, value in enumerate((old_ref[at], river, river * section_ref[at])):
            tile[r, a] = value

    half = keep_ref.shape[0] - 1
    for r in range(blocks):
        block = step * blocks + r

        def put(ref, tile_ref, at):
            ref[at] = part[r]
            tile_ref[at] = tile[r]

        @pl.when((block <= half) & (core == 0))
        def _():
            put(keep_ref, mine_ref, block)

        @pl.when((block <= half) & (core == 1))
        def _():
            put(send_ref, give_ref, block)

        @pl.when((block >= half - 1) & (core == 0))
        def _():
            put(send_ref, give_ref, block - (half - 1))

        @pl.when((block >= half - 1) & (core == 1))
        def _():
            put(keep_ref, mine_ref, block - (half - 1))


def soil(tables, pressure, texture, active, head_old, cell_code, section):
    layers, nrows, cols = pressure.shape
    classes = tables[0].shape[1]
    rows = nrows // 4
    blocks = nrows // (2 * SUB) + 1
    whole = pl.BlockSpec((1, classes), lambda j: (0, 0))
    block = pl.BlockSpec((layers, rows, cols), lambda j: (0, j, 0))
    pair = pl.BlockSpec((2, rows, cols), lambda j: (0, j, 0))
    msg = jax.ShapeDtypeStruct((blocks, 3, SUB, cols), jnp.float32)
    msg_spec = pl.BlockSpec(msg.shape, lambda j: (0, 0, 0, 0))
    tile = pl.BlockSpec(head_old.shape, lambda j: (0, 0))
    part = jax.ShapeDtypeStruct((blocks, 3, SUB, head_old.shape[1]), jnp.float32)
    part_spec = pl.BlockSpec(part.shape, lambda j: (0, 0, 0, 0))
    layer2 = jax.ShapeDtypeStruct((2, nrows, cols), jnp.float32)
    size = layers * nrows * cols
    return pl.pallas_call(
        soil_kernel,
        grid=(nrows // rows,),
        in_specs=[whole, whole, whole, block, block, block, tile, tile, tile],
        out_specs=[block, msg_spec, msg_spec, part_spec, part_spec, pair, pair],
        out_shape=[jax.ShapeDtypeStruct((layers, nrows, cols), jnp.float32), msg, msg, part, part, layer2, layer2],
        scratch_shapes=[
            pltpu.VMEM((3, SUB, LANE), jnp.float32),
            pltpu.VMEM((rows // SUB, 3, SUB, cols), jnp.float32),
            pltpu.VMEM((rows // SUB, 3, SUB, head_old.shape[1]), jnp.float32),
        ],
        compiler_params=params(32),
        cost_estimate=cost(60 * size, 20 * size, size),
        name="soil",
    )(*in_hbm(*tables, pressure, texture, active, head_old, cell_code, section))


def edge_lane(chip):
    return (1 - chip) * (LANE - WIDTH)


def on_edge(value, chip):
    lane = lax.broadcasted_iota(jnp.int32, value.shape, 1)
    base = edge_lane(chip)
    return jnp.where((lane >= base) & (lane < base + WIDTH), value, 0.0)


def shift(array, block=0):
    return WIDTH * (6 * block + array)


SHARE = LANE // (6 * WIDTH)


def packed(pieces, chip, block=0):
    total = None
    for a, piece in enumerate(pieces):
        moved = pltpu.roll(on_edge(piece, chip), shift(a, block), 1)
        total = moved if total is None else total + moved
    return total


def unpacked(tile, array, block=0):
    return pltpu.roll(tile, LANE - shift(array, block), 1)


def nearest(block, core):
    return jnp.where(core == 0, block[:SWEEPS], block[SUB - SWEEPS :])


def spread(rows, core):
    zeros = jnp.zeros((SUB - SWEEPS, rows.shape[1]), rows.dtype)
    return jnp.where(core == 0, jnp.concatenate([rows, zeros], 0), jnp.concatenate([zeros, rows], 0))


def put_rows(ref, plane, pieces):
    used = sum(piece.shape[0] for piece in pieces)
    spare = jnp.zeros((2 * SUB - used, pieces[0].shape[1]), jnp.float32)
    rows = jnp.concatenate([*pieces, spare], 0)
    ref[plane] = rows[:SUB]
    ref[plane + 1] = rows[SUB:]


def get_rows(ref, plane, counts):
    rows = jnp.concatenate([ref[plane], ref[plane + 1]], 0)
    out, at = [], 0
    for count in counts:
        out.append(rows[at : at + count])
        at += count
    return out


def fold(tiles):
    mid = SUB // 2
    return jnp.concatenate([part for tile in tiles for part in (tile[:mid], tile[mid:])], 1)


def unfold(rows):
    parts = [rows[:, i : i + LANE] for i in range(0, rows.shape[1], LANE)]
    return [jnp.concatenate(parts[i : i + 2], 0) for i in range(0, len(parts), 2)]


def half_lanes(which, half):
    return pl.ds(pl.multiple_of(which * half, half), half)


def slab_lanes(chip, half):
    return pl.ds(pl.multiple_of(half - LANE + chip * LANE, LANE), LANE)


def tile_rows(mine_ref, other_ref, b, core, which, array, start, stop):
    lanes = slice(start, stop)
    return jnp.where(core == which, mine_ref[b, array, :, lanes], other_ref[b, array, :, lanes])


def edge_inputs(mine_ref, other_ref, b, chip, core):
    tile = mine_ref.shape[3]
    out = []
    for a in range(3):
        left = tile_rows(mine_ref, other_ref, b, core, 1, a, tile - LANE, tile)
        right = tile_rows(mine_ref, other_ref, b, core, 0, a, 0, LANE)
        out.append(jnp.where(chip == 0, left, right))
    return out


def pack_kernel(keep_ref, recv_ref, mine_ref, other_ref, out_ref):
    chip, core = place()
    blocks, _, _, cols = keep_ref.shape
    half = cols // 2
    away = half_lanes(1 - chip, half)
    slab = slab_lanes(chip, half)
    main = 3 * (blocks - 1)
    tiles = [None] * -(-blocks // SHARE)
    for j in range(blocks):
        b = j + core if j < blocks - 1 else (1 - core) * (blocks - 1)
        sums = [keep_ref[b, a, :, away] + recv_ref[b, a, :, away] for a in range(3)]
        if j < blocks - 1:
            for a in range(3):
                out_ref[3 * j + a] = sums[a]
        else:
            rows = [nearest(v, core) for v in sums]
        pieces = [keep_ref[b, a, :, slab] + recv_ref[b, a, :, slab] for a in range(3)]
        pieces += edge_inputs(mine_ref, other_ref, b, chip, core)
        piece = packed(pieces, chip, j % SHARE)
        i = j // SHARE
        tiles[i] = piece if tiles[i] is None else tiles[i] + piece
    put_rows(out_ref, main, [*rows, fold(tiles)])


def pack(keep, recv, mine, other):
    blocks, _, _, cols = keep.shape
    half = cols // 2
    return pl.pallas_call(
        pack_kernel,
        in_specs=[VMEM] * 4,
        out_specs=VMEM,
        out_shape=jax.ShapeDtypeStruct((3 * blocks - 1, SUB, half), jnp.float32),
        compiler_params=params(8),
        cost_estimate=cost(keep.size, 12 * keep.size),
        name="pack",
    )(keep, recv, mine, other)


def rim_kernel(keep_ref, recv_ref, mine_ref, other_ref, *refs):
    side_ref, cross_ref = refs[-2:]
    chip, core = place()
    blocks, _, _, cols = keep_ref.shape
    half = cols // 2
    tile = half // 2
    b = core * (blocks - 1)
    near, away = half_lanes(chip, half), half_lanes(1 - chip, half)
    side_ref[:3] = keep_ref[b, :, :, near] + recv_ref[b, :, :, near]
    rows = [nearest(keep_ref[b, a, :, away] + recv_ref[b, a, :, away], core) for a in range(3)]
    for which in range(2):
        for a in range(3):
            side_ref[3 + a, :, which * tile : (which + 1) * tile] = tile_rows(
                mine_ref, other_ref, b, core, which, a, 0, tile
            )

    def sums(slab):
        return [keep_ref[b, a, :, slab] + recv_ref[b, a, :, slab] for a in range(3)]

    side_ref[6, :, :LANE] = packed(sums(slab_lanes(1 - chip, half)), 1 - chip)
    inputs = edge_inputs(mine_ref, other_ref, b, chip, core)
    halo = nearest(packed(sums(slab_lanes(chip, half)) + inputs, chip), core)
    spare = jnp.zeros((SWEEPS, half - LANE), jnp.float32)
    put_rows(cross_ref, 0, [*rows, jnp.concatenate([halo, spare], 1)])


def rim(keep, recv, mine, other, *first):
    half = keep.shape[3] // 2
    return pl.pallas_call(
        rim_kernel,
        in_specs=[VMEM] * 4 + [ANY] * len(first),
        out_specs=[VMEM] * 2,
        out_shape=[jax.ShapeDtypeStruct((n, SUB, half), jnp.float32) for n in (7, 2)],
        compiler_params=params(8),
        cost_estimate=cost(keep.size // 8, keep.size),
        name="rim",
    )(keep, recv, mine, other, *first)


def sweep_kernel(keep_ref, recv_ref, mine_ref, other_ref, far_ref, side_ref, cross_ref, out_ref, left_ref, right_ref, work):
    chip, core = place()
    strip = lax.axis_index("strips")
    blocks, _, _, cols = keep_ref.shape
    half = cols // 2
    tile = half // 2
    main = 3 * (blocks - 1)

    def cells(at, lanes, sums, inputs):
        trans = sums[0] * layer_thick
        store = spec_yield + sums[1] * layer_thick
        old, river, inflow = inputs
        rows = pl.ds(pl.multiple_of(at * SUB, SUB), SUB)
        work[0, rows, lanes] = trans
        work[1, rows, lanes] = store + river
        work[2, rows, lanes] = store * old + leak_rate * layer_thick * sums[2] + inflow
        work[3, rows, lanes] = old

    def halo(at, sums, inputs):
        sums, inputs = ([on_edge(v, 1 - chip) for v in values] for values in (sums, inputs))
        cells(at, slice(half, half + LANE), sums, inputs)

    near, slab = half_lanes(chip, half), slab_lanes(1 - chip, half)
    *beyond, tiles = get_rows(far_ref, main, (SWEEPS, SWEEPS, SWEEPS, SUB // 2))
    tiles = unfold(tiles)
    for j in range(blocks):
        b = j + core if j < blocks - 1 else (1 - core) * (blocks - 1)
        if j < blocks - 1:
            far = [far_ref[3 * j + a] for a in range(3)]
        else:
            far = [spread(v, core) for v in beyond]
        sums = [keep_ref[b, a, :, near] + recv_ref[b, a, :, near] + far[a] for a in range(3)]
        for which in range(2):
            lanes = slice(which * tile, (which + 1) * tile)
            inputs = [tile_rows(mine_ref, other_ref, b, core, which, a, 0, tile) for a in range(3)]
            cells(b, lanes, [s[:, lanes] for s in sums], inputs)
        far = [unpacked(tiles[j // SHARE], a, j % SHARE) for a in range(6)]
        sums = [keep_ref[b, a, :, slab] + recv_ref[b, a, :, slab] + far[a] for a in range(3)]
        halo(b, sums, far[3:])
    outside = ((core == 0) & (strip == 0)) | ((core == 1) & (strip == lax.axis_size("strips") - 1))

    def inside(value):
        return jnp.where(outside, 0.0, value)

    *cross, corner = [spread(v, 1 - core) for v in get_rows(cross_ref, 0, (SWEEPS,) * 4)]
    sums = [inside(side_ref[a] + cross[a]) for a in range(3)]
    cells(blocks, slice(0, half), sums, [inside(side_ref[3 + a]) for a in range(3)])
    side, cross = side_ref[6, :, :LANE], corner[:, :LANE]
    sums = [inside(unpacked(side, a) + unpacked(cross, a)) for a in range(3)]
    halo(blocks, sums, [inside(unpacked(cross, a)) for a in range(3, 6)])

    trans, base, rhs, head = (work[i] for i in range(4))
    rows, lanes = trans.shape
    right = jnp.sqrt(trans * pltpu.roll(trans, lanes - 1, 1))
    left = pltpu.roll(right, 1, 1)
    down = jnp.sqrt(trans * pltpu.roll(trans, rows - 1, 0))
    up = pltpu.roll(down, 1, 0)
    inverse = 1.0 / (base + right + left + down + up)
    for _ in range(SWEEPS):
        head = inverse * (
            rhs
            + right * pltpu.roll(head, lanes - 1, 1)
            + left * pltpu.roll(head, 1, 1)
            + down * pltpu.roll(head, rows - 1, 0)
            + up * pltpu.roll(head, 1, 0)
        )
    work[0] = head
    out_ref[...] = work[0, pl.ds(pl.multiple_of(core * SUB, SUB), out_ref.shape[0]), :half]
    left_ref[...] = out_ref[:, :tile]
    right_ref[...] = out_ref[:, tile:]


def sweeps(keep, recv, mine, other, far, side, cross):
    blocks = keep.shape[0]
    half = keep.shape[3] // 2
    return pl.pallas_call(
        sweep_kernel,
        in_specs=[VMEM] * 7,
        out_specs=[VMEM] * 3,
        out_shape=[
            jax.ShapeDtypeStruct(((blocks - 1) * SUB, half // part), jnp.float32) for part in (1, 2, 2)
        ],
        scratch_shapes=[pltpu.VMEM((4, (blocks + 1) * SUB, half + LANE), jnp.float32)],
        compiler_params=params(12),
        cost_estimate=cost(20 * keep.size, 12 * keep.size),
        name="sweeps",
    )(keep, recv, mine, other, far, side, cross)


def pass_on_kernel(core_ref, ring_ref, first, *out_refs):
    del first
    chip, core = place()
    rows = out_refs[0].shape[1]
    for i, out_ref in enumerate(out_refs):
        part = slice(i * rows, (i + 1) * rows)

        @pl.when(chip == core)
        def _():
            out_ref[...] = ring_ref[:, part]

        @pl.when(chip != core)
        def _():
            out_ref[...] = core_ref[:, part]


def pass_on(core_pair, ring, first):
    return pl.pallas_call(
        pass_on_kernel,
        in_specs=[VMEM] * 2 + [ANY],
        out_specs=[VMEM] * PARTS,
        out_shape=[jax.ShapeDtypeStruct((2, ring.shape[1] // PARTS, ring.shape[2]), ring.dtype)] * PARTS,
        compiler_params=params(8),
        cost_estimate=cost(ring.size, 8 * ring.size),
        name="pass_on",
    )(core_pair, ring, first)


def faces_kernel(moist_in, core_ref, rest_ref, ring_ref, rain_ref, *refs):
    del moist_in
    got_refs, (moist_out, tail_ref, ends, sems) = refs[:PARTS], refs[PARTS:]
    chip, core = place()
    layers = moist_out.shape[0]
    copies = [
        (moist_out.at[layer], ends.at[i], sems.at[i]) for i, layer in enumerate((0, layers - 1))
    ]
    loads = [pltpu.make_async_copy(src, dst, sem) for src, dst, sem in copies]
    stores = [pltpu.make_async_copy(dst, src, sem) for src, dst, sem in copies]
    for c in loads:
        c.start()
    for c in loads:
        c.wait()
    gain = soil_step / layer_thick
    face = 0.5 * gain
    last = (core == 1) & (chip == 1)

    def flux(upper, lower):
        return (upper[1] + lower[1]) * ((upper[0] - lower[0]) * (face / layer_thick) + face)

    def got_faces(which, sign, ref, below):
        for i, got in enumerate(got_refs):
            rows = got.shape[1]
            part = slice(i * rows, (i + 1) * rows)
            mine = ref[0, part], ref[1, part]
            change = flux(mine, got) if below else flux(got, mine)
            ends[which, part] = ends[which, part] + sign * change

    @pl.when((core == 0) & (chip == 0))
    def _():
        ends[0] = ends[0] + gain * rain_ref[...]
        got_faces(1, -1.0, core_ref, True)

    @pl.when((core == 1) & (chip == 0))
    def _():
        ends[0] = ends[0] + flux(ring_ref, core_ref)
        got_faces(1, -1.0, rest_ref, True)

    @pl.when((core == 0) & (chip == 1))
    def _():
        got_faces(0, 1.0, rest_ref, False)
        ends[1] = ends[1] - flux(core_ref, ring_ref)

    @pl.when(last)
    def _():
        got_faces(0, 1.0, core_ref, False)

    stores[0].start()

    @pl.when(last)
    def _():
        slope = rest_ref[1] * (gain / (0.5 * layer_thick))
        tail_ref[0] = ends[1] - (rest_ref[0] * slope + gain * rest_ref[1])
        tail_ref[1] = slope

    @pl.when(jnp.logical_not(last))
    def _():
        stores[1].start()
        stores[1].wait()

    stores[0].wait()


def faces(moist, core_pair, rest_pair, ring, got, rain):
    return pl.pallas_call(
        faces_kernel,
        in_specs=[ANY] + [VMEM] * (4 + PARTS),
        out_specs=[ANY, VMEM],
        out_shape=[
            jax.ShapeDtypeStruct(moist.shape, moist.dtype),
            jax.ShapeDtypeStruct((2,) + moist.shape[1:], moist.dtype),
        ],
        input_output_aliases={0: 0},
        scratch_shapes=[pltpu.VMEM((2,) + moist.shape[1:], jnp.float32), pltpu.SemaphoreType.DMA((2,))],
        compiler_params=params(12),
        cost_estimate=cost(20 * rain.size, 32 * rain.size),
        name="faces",
    )(moist, core_pair, rest_pair, ring, rain, *got)


def near_bottom_kernel(moist_in, tail_ref, own_ref, left_ref, right_ref, moist_out, head_ref, done, sem):
    del moist_in
    chip, core = place()
    layers = moist_out.shape[0]
    rows, half = own_ref.shape
    tile = half // 2
    mine = pl.ds(pl.multiple_of(core * rows, rows), rows)
    theirs = pl.ds(pl.multiple_of((1 - core) * rows, rows), rows)
    store = pltpu.make_async_copy(done, moist_out.at[layers - 1, :, half:], sem)

    @pl.when((core == 1) & (chip == 1))
    def _():
        for i, ref in enumerate((left_ref, right_ref)):
            to, at = slice(i * tile, (i + 1) * tile), slice(half + i * tile, half + (i + 1) * tile)
            done[:rows, to] = tail_ref[0, :rows, at] + tail_ref[1, :rows, at] * ref[...]
        done[rows:] = tail_ref[0, rows:, half:] + tail_ref[1, rows:, half:] * own_ref[...]
        store.start()

    head_ref[mine, :] = own_ref[:, pl.ds(pl.multiple_of(core * tile, tile), tile)]
    head_ref[theirs, :] = jnp.where(core == 0, left_ref[...], right_ref[...])

    @pl.when((core == 1) & (chip == 1))
    def _():
        store.wait()


def near_bottom(moist, tail, own, left, right):
    rows, half = own.shape
    return pl.pallas_call(
        near_bottom_kernel,
        in_specs=[ANY] + [VMEM] * 4,
        out_specs=[ANY, VMEM],
        out_shape=[
            jax.ShapeDtypeStruct(moist.shape, moist.dtype),
            jax.ShapeDtypeStruct((2 * rows, half // 2), jnp.float32),
        ],
        input_output_aliases={0: 0},
        scratch_shapes=[pltpu.VMEM((2 * rows, half), jnp.float32), pltpu.SemaphoreType.DMA],
        compiler_params=params(12),
        cost_estimate=cost(10 * own.size, 40 * own.size),
        name="near_bottom",
    )(moist, tail, own, left, right)


def bottom_kernel(moist_in, tail_ref, chip_far, both_far, moist_out, done, sem):
    del moist_in
    chip, core = place()
    layers = moist_out.shape[0]
    rows, half = chip_far.shape

    @pl.when((core == 1) & (chip == 1))
    def _():
        store = pltpu.make_async_copy(done, moist_out.at[layers - 1, :, :half], sem)
        for ref, where in ((both_far, slice(0, rows)), (chip_far, slice(rows, 2 * rows))):
            done[where] = tail_ref[0, where, :half] + tail_ref[1, where, :half] * ref[...]
        store.start()
        store.wait()


def bottom(moist, tail, chip_far, both_far):
    rows, half = chip_far.shape
    return pl.pallas_call(
        bottom_kernel,
        in_specs=[ANY] + [VMEM] * 3,
        out_specs=ANY,
        out_shape=jax.ShapeDtypeStruct(moist.shape, moist.dtype),
        input_output_aliases={0: 0},
        scratch_shapes=[pltpu.VMEM((2 * rows, half), jnp.float32), pltpu.SemaphoreType.DMA],
        compiler_params=params(12),
        cost_estimate=cost(4 * chip_far.size, 24 * chip_far.size),
        name="bottom",
    )(moist, tail, chip_far, both_far)


def gate_kernel(*refs):
    del refs


def gate(value, *first, stored=()):
    return pl.pallas_call(
        gate_kernel,
        in_specs=[ANY] * (1 + len(first)) + [HBM] * len(stored),
        out_specs=ANY,
        out_shape=jax.ShapeDtypeStruct(value.shape, value.dtype),
        input_output_aliases={0: 0},
        compiler_params=params(1),
        cost_estimate=cost(1, 1),
        name="gate",
    )(value, *first, *in_hbm(*stored))


def core_swap(value):
    return lax.ppermute(value, "depth", [(i, i ^ 1) for i in range(lax.axis_size("depth"))])


def chip_swap(value):
    return lax.ppermute(value, "depth", [(i, i ^ 2) for i in range(lax.axis_size("depth"))])


def ring_shift(value):
    return lax.ppermute(value, "depth", [(1, 3), (3, 2), (2, 0), (0, 1)])


def strip_swap(value, chips=0):
    depth, strips = lax.axis_size("depth"), lax.axis_size("strips")
    pairs = []
    for d in range(1, depth, 2):
        for s in range(strips):
            lower, upper = d * strips + s, ((d - 1) ^ chips) * strips + (s + 1) % strips
            pairs += [(lower, upper), (upper, lower)]
    return lax.ppermute(value, ("depth", "strips"), pairs)


def shards(pressure, texture, active, rain, k_sat, alpha, theta_sat, head_old, cell_code, section):
    tables = (k_sat[None], alpha[None], theta_sat[None])
    face_pair = face(tables, pressure, texture, active)
    ring = ring_shift(face_pair)
    moist, keep, send, mine, give, core_pair, rest_pair = soil(
        tables, pressure, texture, active, head_old, cell_code, section
    )
    recv, other = core_swap(send), core_swap(give)
    message = pack(keep, recv, mine, other)
    far = chip_swap(message)
    side, cross = rim(keep, recv, mine, other, message, ring)
    heads, left, right = sweeps(keep, recv, mine, other, far, strip_swap(side), strip_swap(cross, 2))
    got = [core_swap(part) for part in pass_on(core_pair, ring, side)]
    moist, tail = faces(moist, core_pair, rest_pair, ring, got, rain)
    moist, head = near_bottom(moist, tail, heads, core_swap(left), core_swap(right))
    heads_chip = gate(chip_swap(heads), stored=(moist,))
    return bottom(moist, tail, heads_chip, core_swap(heads_chip)), head


def solution(mesh):
    in_specs = (
        P("depth", "strips", None),
        P("depth", "strips", None),
        P("depth", "strips", None),
        P("strips", None),
        P(),
        P(),
        P(),
        P("strips", "depth"),
        P("strips", "depth"),
        P("strips", "depth"),
    )
    out_specs = (P("depth", "strips", None), P("strips", "depth"))
    return jax.shard_map(shards, mesh=mesh, in_specs=in_specs, out_specs=out_specs, check_vma=False)
```

```python
import functools
import math

import jax
import jax.numpy as jnp
from jax import lax
from jax.experimental import pallas as pl
from jax.experimental.pallas import tpu as pltpu
from jax.sharding import PartitionSpec as P

SWEEPS = 3
SUB = 8
PARTS = 2
LANE = 128
WIDTH = 4

layer_thick = 0.05
soil_step = 0.0002
spec_yield = 0.02
leak_rate = 0.5
river_cond = 0.5
fixed_cond = 3.0
residual = 0.15
mobile = 0.85

VMEM = pl.BlockSpec(memory_space=pltpu.VMEM)
ANY = pl.BlockSpec(memory_space=pl.ANY)
HBM = pl.BlockSpec(memory_space=pltpu.HBM)


def params(mib):
    return pltpu.CompilerParams(vmem_limit_bytes=mib * 2**20)


def cost(flops, nbytes, trans=0):
    return pl.CostEstimate(flops=int(flops), bytes_accessed=int(nbytes), transcendentals=int(trans))


def place():
    depth = lax.axis_index("depth")
    return depth // 2, depth % 2


def gathered(table, classes):
    return jnp.take_along_axis(table, classes, axis=1, mode="promise_in_bounds")


def picked(options, bits):
    for bit in bits:
        options = [
            jnp.where(bit, options[i + 1], options[i]) if i + 1 < len(options) else options[i]
            for i in range(0, len(options), 2)
        ]
    return options[0]


def fill_tables(tab, sat_ref, alpha_ref, theta_ref):
    classes = sat_ref.shape[1]
    scaled = (sat_ref, 1.0), (alpha_ref, 0.5 * math.log2(math.e)), (theta_ref, mobile)
    for i, (ref, scale) in enumerate(scaled):
        tab[i, :, :classes] = jnp.broadcast_to(ref[...] * scale, (SUB, classes))


def face_kernel(
    sat_hbm, alpha_hbm, psi_hbm, tex_hbm, act_hbm, out_ref, kinds, acts, given, tab, sems
):
    chip, _ = place()
    layer = (1 - chip) * (psi_hbm.shape[0] - 1)
    cols = psi_hbm.shape[2]
    classes = sat_hbm.shape[1]
    chunks = 2
    rows = kinds.shape[0] // chunks

    def copies(i):
        part = pl.ds(i * rows, rows)
        pairs = (
            (psi_hbm.at[layer, part], out_ref.at[0, part]),
            (tex_hbm.at[layer, part], kinds.at[part]),
            (act_hbm.at[layer, part], acts.at[part]),
        )
        return [pltpu.make_async_copy(src, dst, sems.at[i, k]) for k, (src, dst) in enumerate(pairs)]

    tables = [
        pltpu.make_async_copy(src, given.at[k], sems.at[chunks, k]) for k, src in enumerate((sat_hbm, alpha_hbm))
    ]
    for c in tables:
        c.start()
    for i in range(chunks):
        for c in copies(i):
            c.start()
    for c in tables:
        c.wait()
    for i, scale in enumerate((1.0, 0.5 * math.log2(math.e))):
        tab[i, :, :classes] = jnp.broadcast_to(given[i] * scale, (SUB, classes))

    for i in range(chunks):
        for c in copies(i):
            c.wait()

        def columns(q, carry):
            lanes = pl.ds(pl.multiple_of(q * LANE, LANE), LANE)
            for r in range(i * rows, (i + 1) * rows, SUB):
                rws = slice(r, r + SUB)
                kind = kinds[rws, lanes]
                wet = jnp.exp2(gathered(tab[1], kind) * jnp.minimum(out_ref[0, rws, lanes], 0.0))
                active = acts[rws, lanes].astype(jnp.float32)
                out_ref[1, rws, lanes] = gathered(tab[0], kind) * active * (wet * wet)
            return carry

        lax.fori_loop(0, cols // LANE, columns, 0, unroll=8)


def in_hbm(*arrays):
    return [pltpu.with_memory_space_constraint(x, pltpu.HBM) for x in arrays]


def face(tables, pressure, texture, active):
    _, nrows, cols = pressure.shape
    size = nrows * cols
    return pl.pallas_call(
        face_kernel,
        in_specs=[HBM] * 5,
        out_specs=VMEM,
        out_shape=jax.ShapeDtypeStruct((2, nrows, cols), jnp.float32),
        scratch_shapes=[
            pltpu.VMEM((nrows, cols), jnp.int32),
            pltpu.VMEM((nrows, cols), jnp.int32),
            pltpu.VMEM((2,) + tables[0].shape, jnp.float32),
            pltpu.VMEM((2, SUB, LANE), jnp.float32),
            pltpu.SemaphoreType.DMA((3, 3)),
        ],
        compiler_params=params(8),
        cost_estimate=cost(20 * size, 20 * size, size),
        name="face",
    )(*in_hbm(*tables[:2], pressure, texture, active))


def soil_kernel(
    sat_ref, alpha_ref, theta_ref, psi_ref, tex_ref, act_ref, old_ref, code_ref, section_ref,
    moist_ref, keep_ref, send_ref, mine_ref, give_ref, core_ref, rest_ref, tab, part, tile,
):
    step = pl.program_id(0)
    _, core = place()
    layers, rows, cols = psi_ref.shape
    classes = sat_ref.shape[1]

    @pl.when(step == 0)
    def _():
        fill_tables(tab, sat_ref, alpha_ref, theta_ref)

    sat_tab, par_tab = tab[0], tab[1]
    theta = [jnp.broadcast_to(tab[2, :, i : i + 1], (SUB, LANE)) for i in range(classes)]
    nbits = max(1, (classes - 1).bit_length())
    face = 0.5 * soil_step / layer_thick
    core_layer = (1 - core) * (layers - 1)
    rest_layer = core * (layers - 1)

    def columns(q, carry):
        lanes = pl.ds(pl.multiple_of(q * LANE, LANE), LANE)
        for r in range(0, rows, SUB):
            rws = slice(r, r + SUB)
            trans = store = charge = jnp.zeros((SUB, LANE), jnp.float32)
            for layer in range(layers):
                kind = tex_ref[layer, rws, lanes]
                psi = psi_ref[layer, rws, lanes]
                active = act_ref[layer, rws, lanes].astype(jnp.float32)
                bits = [(kind & (1 << b)) != 0 for b in range(nbits)]
                wet = jnp.exp2(gathered(par_tab, kind) * jnp.minimum(psi, 0.0))
                cond = gathered(sat_tab, kind) * active * (wet * wet)
                mob = picked(theta, bits)
                mobwet = mob * wet
                trans = trans + cond
                charge = charge + cond * wet
                store = store + (mob - mobwet)
                held = mob * (residual / mobile) + mobwet
                if layer == 0:
                    first, own = cond, held
                else:
                    flux = (cond_up + cond) * ((psi_up - psi) * (face / layer_thick) + face)
                    moist_ref[layer - 1, rws, lanes] = own - flux
                    own = held + flux
                psi_up, cond_up = psi, cond
            moist_ref[layers - 1, rws, lanes] = own
            part[r // SUB, 0, :, lanes] = trans
            part[r // SUB, 1, :, lanes] = store
            part[r // SUB, 2, :, lanes] = charge
            core_ref[0, rws, lanes] = psi_ref[core_layer, rws, lanes]
            core_ref[1, rws, lanes] = jnp.where(core == 0, cond, first)
            rest_ref[0, rws, lanes] = psi_ref[rest_layer, rws, lanes]
            rest_ref[1, rws, lanes] = jnp.where(core == 0, first, cond)
        return carry

    lax.fori_loop(0, cols // LANE, columns, 0, unroll=8)

    blocks = rows // SUB
    for r in range(blocks):
        at = pl.ds(pl.multiple_of(step * rows + r * SUB, SUB), SUB)
        code = code_ref[at]
        river = jnp.where(code == 1, river_cond, jnp.where(code == 2, fixed_cond, 0.0))
        for a, value in enumerate((old_ref[at], river, river * section_ref[at])):
            tile[r, a] = value

    half = keep_ref.shape[0] - 1
    for r in range(blocks):
        block = step * blocks + r

        def put(ref, tile_ref, at):
            ref[at] = part[r]
            tile_ref[at] = tile[r]

        @pl.when((block <= half) & (core == 0))
        def _():
            put(keep_ref, mine_ref, block)

        @pl.when((block <= half) & (core == 1))
        def _():
            put(send_ref, give_ref, block)

        @pl.when((block >= half - 1) & (core == 0))
        def _():
            put(send_ref, give_ref, block - (half - 1))

        @pl.when((block >= half - 1) & (core == 1))
        def _():
            put(keep_ref, mine_ref, block - (half - 1))


def soil(tables, pressure, texture, active, head_old, cell_code, section):
    layers, nrows, cols = pressure.shape
    classes = tables[0].shape[1]
    rows = nrows // 4
    blocks = nrows // (2 * SUB) + 1
    whole = pl.BlockSpec((1, classes), lambda j: (0, 0))
    block = pl.BlockSpec((layers, rows, cols), lambda j: (0, j, 0))
    pair = pl.BlockSpec((2, rows, cols), lambda j: (0, j, 0))
    msg = jax.ShapeDtypeStruct((blocks, 3, SUB, cols), jnp.float32)
    msg_spec = pl.BlockSpec(msg.shape, lambda j: (0, 0, 0, 0))
    tile = pl.BlockSpec(head_old.shape, lambda j: (0, 0))
    part = jax.ShapeDtypeStruct((blocks, 3, SUB, head_old.shape[1]), jnp.float32)
    part_spec = pl.BlockSpec(part.shape, lambda j: (0, 0, 0, 0))
    layer2 = jax.ShapeDtypeStruct((2, nrows, cols), jnp.float32)
    size = layers * nrows * cols
    return pl.pallas_call(
        soil_kernel,
        grid=(nrows // rows,),
        in_specs=[whole, whole, whole, block, block, block, tile, tile, tile],
        out_specs=[block, msg_spec, msg_spec, part_spec, part_spec, pair, pair],
        out_shape=[jax.ShapeDtypeStruct((layers, nrows, cols), jnp.float32), msg, msg, part, part, layer2, layer2],
        scratch_shapes=[
            pltpu.VMEM((3, SUB, LANE), jnp.float32),
            pltpu.VMEM((rows // SUB, 3, SUB, cols), jnp.float32),
            pltpu.VMEM((rows // SUB, 3, SUB, head_old.shape[1]), jnp.float32),
        ],
        compiler_params=params(32),
        cost_estimate=cost(60 * size, 20 * size, size),
        name="soil",
    )(*in_hbm(*tables, pressure, texture, active, head_old, cell_code, section))


def edge_lane(chip):
    return (1 - chip) * (LANE - WIDTH)


def on_edge(value, chip):
    lane = lax.broadcasted_iota(jnp.int32, value.shape, 1)
    base = edge_lane(chip)
    return jnp.where((lane >= base) & (lane < base + WIDTH), value, 0.0)


def shift(array, block=0):
    return WIDTH * (6 * block + array)


SHARE = LANE // (6 * WIDTH)


def packed(pieces, chip, block=0):
    total = None
    for a, piece in enumerate(pieces):
        moved = pltpu.roll(on_edge(piece, chip), shift(a, block), 1)
        total = moved if total is None else total + moved
    return total


def unpacked(tile, array, block=0):
    return pltpu.roll(tile, LANE - shift(array, block), 1)


def nearest(block, core):
    return jnp.where(core == 0, block[:SWEEPS], block[SUB - SWEEPS :])


def spread(rows, core):
    zeros = jnp.zeros((SUB - SWEEPS, rows.shape[1]), rows.dtype)
    return jnp.where(core == 0, jnp.concatenate([rows, zeros], 0), jnp.concatenate([zeros, rows], 0))


def put_rows(ref, plane, pieces):
    planes = ref.shape[0] - plane
    used = sum(piece.shape[0] for piece in pieces)
    spare = jnp.zeros((planes * SUB - used, pieces[0].shape[1]), jnp.float32)
    rows = jnp.concatenate([*pieces, spare], 0)
    for i in range(planes):
        ref[plane + i] = rows[i * SUB : (i + 1) * SUB]


def get_rows(ref, plane, counts):
    rows = jnp.concatenate([ref[i] for i in range(plane, ref.shape[0])], 0)
    out, at = [], 0
    for count in counts:
        out.append(rows[at : at + count])
        at += count
    return out


def fold(tiles):
    mid = SUB // 2
    return jnp.concatenate([part for tile in tiles for part in (tile[:mid], tile[mid:])], 1)


def unfold(rows):
    parts = [rows[:, i : i + LANE] for i in range(0, rows.shape[1], LANE)]
    return [jnp.concatenate(parts[i : i + 2], 0) for i in range(0, len(parts), 2)]


def half_lanes(which, half):
    return pl.ds(pl.multiple_of(which * half, half), half)


def slab_lanes(chip, half):
    return pl.ds(pl.multiple_of(half - LANE + chip * LANE, LANE), LANE)


def tile_rows(mine_ref, other_ref, b, core, which, array, start, stop):
    lanes = slice(start, stop)
    return jnp.where(core == which, mine_ref[b, array, :, lanes], other_ref[b, array, :, lanes])


def edge_inputs(mine_ref, other_ref, b, chip, core):
    tile = mine_ref.shape[3]
    out = []
    for a in range(3):
        left = tile_rows(mine_ref, other_ref, b, core, 1, a, tile - LANE, tile)
        right = tile_rows(mine_ref, other_ref, b, core, 0, a, 0, LANE)
        out.append(jnp.where(chip == 0, left, right))
    return out


def pack_kernel(keep_ref, recv_ref, mine_ref, other_ref, out_ref):
    chip, core = place()
    blocks, _, _, cols = keep_ref.shape
    half = cols // 2
    away = half_lanes(1 - chip, half)
    slab = slab_lanes(chip, half)
    main = 3 * (blocks - 1)
    tiles = [None] * -(-blocks // SHARE)
    for j in range(blocks):
        b = j + core if j < blocks - 1 else (1 - core) * (blocks - 1)
        sums = [keep_ref[b, a, :, away] + recv_ref[b, a, :, away] for a in range(3)]
        if j < blocks - 1:
            for a in range(3):
                out_ref[3 * j + a] = sums[a]
        else:
            rows = [nearest(v, core) for v in sums]
        pieces = [keep_ref[b, a, :, slab] + recv_ref[b, a, :, slab] for a in range(3)]
        pieces += edge_inputs(mine_ref, other_ref, b, chip, core)
        piece = packed(pieces, chip, j % SHARE)
        i = j // SHARE
        tiles[i] = piece if tiles[i] is None else tiles[i] + piece
    put_rows(out_ref, main, [*rows, fold(tiles)])


def pack(keep, recv, mine, other):
    blocks, _, _, cols = keep.shape
    half = cols // 2
    return pl.pallas_call(
        pack_kernel,
        in_specs=[VMEM] * 4,
        out_specs=VMEM,
        out_shape=jax.ShapeDtypeStruct((3 * blocks - 1, SUB, half), jnp.float32),
        compiler_params=params(8),
        cost_estimate=cost(keep.size, 12 * keep.size),
        name="pack",
    )(keep, recv, mine, other)


def rim_kernel(keep_ref, recv_ref, mine_ref, other_ref, *refs):
    side_ref, cross_ref = refs[-2:]
    chip, core = place()
    blocks, _, _, cols = keep_ref.shape
    half = cols // 2
    tile = half // 2
    b = core * (blocks - 1)
    near, away = half_lanes(chip, half), half_lanes(1 - chip, half)
    spare = jnp.zeros((SWEEPS, half - LANE), jnp.float32)

    def sums(lanes):
        return [keep_ref[b, a, :, lanes] + recv_ref[b, a, :, lanes] for a in range(3)]

    def rows(values):
        return [nearest(v, core) for v in values]

    tiles = [
        jnp.concatenate([tile_rows(mine_ref, other_ref, b, core, which, a, 0, tile) for which in range(2)], 1)
        for a in range(3)
    ]
    halo = nearest(packed(sums(slab_lanes(1 - chip, half)), 1 - chip), core)
    put_rows(side_ref, 0, [*rows(sums(near)), *rows(tiles), jnp.concatenate([halo, spare], 1)])
    inputs = edge_inputs(mine_ref, other_ref, b, chip, core)
    halo = nearest(packed(sums(slab_lanes(chip, half)) + inputs, chip), core)
    put_rows(cross_ref, 0, [*rows(sums(away)), jnp.concatenate([halo, spare], 1)])


def rim(keep, recv, mine, other, *first):
    half = keep.shape[3] // 2
    return pl.pallas_call(
        rim_kernel,
        in_specs=[VMEM] * 4 + [ANY] * len(first),
        out_specs=[VMEM] * 2,
        out_shape=[jax.ShapeDtypeStruct((n, SUB, half), jnp.float32) for n in (3, 2)],
        compiler_params=params(8),
        cost_estimate=cost(keep.size // 8, keep.size),
        name="rim",
    )(keep, recv, mine, other, *first)


def sweep_kernel(keep_ref, recv_ref, mine_ref, other_ref, far_ref, side_ref, cross_ref, out_ref, left_ref, right_ref, work):
    chip, core = place()
    strip = lax.axis_index("strips")
    blocks, _, _, cols = keep_ref.shape
    half = cols // 2
    tile = half // 2
    main = 3 * (blocks - 1)

    def cells(at, lanes, sums, inputs):
        trans = sums[0] * layer_thick
        store = spec_yield + sums[1] * layer_thick
        old, river, inflow = inputs
        rows = pl.ds(pl.multiple_of(at * SUB, SUB), SUB)
        work[0, rows, lanes] = trans
        work[1, rows, lanes] = store + river
        work[2, rows, lanes] = store * old + leak_rate * layer_thick * sums[2] + inflow
        work[3, rows, lanes] = old

    def halo(at, sums, inputs):
        sums, inputs = ([on_edge(v, 1 - chip) for v in values] for values in (sums, inputs))
        cells(at, slice(half, half + LANE), sums, inputs)

    near, slab = half_lanes(chip, half), slab_lanes(1 - chip, half)
    *beyond, tiles = get_rows(far_ref, main, (SWEEPS, SWEEPS, SWEEPS, SUB // 2))
    tiles = unfold(tiles)
    for j in range(blocks):
        b = j + core if j < blocks - 1 else (1 - core) * (blocks - 1)
        if j < blocks - 1:
            far = [far_ref[3 * j + a] for a in range(3)]
        else:
            far = [spread(v, core) for v in beyond]
        sums = [keep_ref[b, a, :, near] + recv_ref[b, a, :, near] + far[a] for a in range(3)]
        for which in range(2):
            lanes = slice(which * tile, (which + 1) * tile)
            inputs = [tile_rows(mine_ref, other_ref, b, core, which, a, 0, tile) for a in range(3)]
            cells(b, lanes, [s[:, lanes] for s in sums], inputs)
        far = [unpacked(tiles[j // SHARE], a, j % SHARE) for a in range(6)]
        sums = [keep_ref[b, a, :, slab] + recv_ref[b, a, :, slab] + far[a] for a in range(3)]
        halo(b, sums, far[3:])
    outside = ((core == 0) & (strip == 0)) | ((core == 1) & (strip == lax.axis_size("strips") - 1))

    def inside(value):
        return jnp.where(outside, 0.0, value)

    side = [spread(v, 1 - core) for v in get_rows(side_ref, 0, (SWEEPS,) * 7)]
    cross = [spread(v, 1 - core) for v in get_rows(cross_ref, 0, (SWEEPS,) * 4)]
    cells(blocks, slice(0, half), [inside(side[a] + cross[a]) for a in range(3)], [inside(v) for v in side[3:6]])
    side, cross = side[6][:, :LANE], cross[3][:, :LANE]
    sums = [inside(unpacked(side, a) + unpacked(cross, a)) for a in range(3)]
    halo(blocks, sums, [inside(unpacked(cross, a)) for a in range(3, 6)])

    trans, base, rhs, head = (work[i] for i in range(4))
    rows, lanes = trans.shape
    right = jnp.sqrt(trans * pltpu.roll(trans, lanes - 1, 1))
    left = pltpu.roll(right, 1, 1)
    down = jnp.sqrt(trans * pltpu.roll(trans, rows - 1, 0))
    up = pltpu.roll(down, 1, 0)
    inverse = 1.0 / (base + right + left + down + up)
    for _ in range(SWEEPS):
        head = inverse * (
            rhs
            + right * pltpu.roll(head, lanes - 1, 1)
            + left * pltpu.roll(head, 1, 1)
            + down * pltpu.roll(head, rows - 1, 0)
            + up * pltpu.roll(head, 1, 0)
        )
    work[0] = head
    out_ref[...] = work[0, pl.ds(pl.multiple_of(core * SUB, SUB), out_ref.shape[0]), :half]
    left_ref[...] = out_ref[:, :tile]
    right_ref[...] = out_ref[:, tile:]


def sweeps(keep, recv, mine, other, far, side, cross):
    blocks = keep.shape[0]
    half = keep.shape[3] // 2
    return pl.pallas_call(
        sweep_kernel,
        in_specs=[VMEM] * 7,
        out_specs=[VMEM] * 3,
        out_shape=[
            jax.ShapeDtypeStruct(((blocks - 1) * SUB, half // part), jnp.float32) for part in (1, 2, 2)
        ],
        scratch_shapes=[pltpu.VMEM((4, (blocks + 1) * SUB, half + LANE), jnp.float32)],
        compiler_params=params(12),
        cost_estimate=cost(20 * keep.size, 12 * keep.size),
        name="sweeps",
    )(keep, recv, mine, other, far, side, cross)


def pass_on_kernel(core_ref, ring_ref, first, *out_refs):
    del first
    chip, core = place()
    rows = out_refs[0].shape[1]
    for i, out_ref in enumerate(out_refs):
        part = slice(i * rows, (i + 1) * rows)

        @pl.when(chip == core)
        def _():
            out_ref[...] = ring_ref[:, part]

        @pl.when(chip != core)
        def _():
            out_ref[...] = core_ref[:, part]


def pass_on(core_pair, ring, first):
    return pl.pallas_call(
        pass_on_kernel,
        in_specs=[VMEM] * 2 + [ANY],
        out_specs=[VMEM] * PARTS,
        out_shape=[jax.ShapeDtypeStruct((2, ring.shape[1] // PARTS, ring.shape[2]), ring.dtype)] * PARTS,
        compiler_params=params(8),
        cost_estimate=cost(ring.size, 8 * ring.size),
        name="pass_on",
    )(core_pair, ring, first)


def faces_kernel(moist_in, core_ref, rest_ref, ring_ref, rain_ref, *refs):
    del moist_in
    got_refs, (moist_out, tail_ref, ends, sems) = refs[:PARTS], refs[PARTS:]
    chip, core = place()
    layers = moist_out.shape[0]
    copies = [
        (moist_out.at[layer], ends.at[i], sems.at[i]) for i, layer in enumerate((0, layers - 1))
    ]
    loads = [pltpu.make_async_copy(src, dst, sem) for src, dst, sem in copies]
    stores = [pltpu.make_async_copy(dst, src, sem) for src, dst, sem in copies]
    for c in loads:
        c.start()
    for c in loads:
        c.wait()
    gain = soil_step / layer_thick
    face = 0.5 * gain
    last = (core == 1) & (chip == 1)

    def flux(upper, lower):
        return (upper[1] + lower[1]) * ((upper[0] - lower[0]) * (face / layer_thick) + face)

    def got_faces(which, sign, ref, below):
        for i, got in enumerate(got_refs):
            rows = got.shape[1]
            part = slice(i * rows, (i + 1) * rows)
            mine = ref[0, part], ref[1, part]
            change = flux(mine, got) if below else flux(got, mine)
            ends[which, part] = ends[which, part] + sign * change

    @pl.when((core == 0) & (chip == 0))
    def _():
        ends[0] = ends[0] + gain * rain_ref[...]
        got_faces(1, -1.0, core_ref, True)

    @pl.when((core == 1) & (chip == 0))
    def _():
        ends[0] = ends[0] + flux(ring_ref, core_ref)
        got_faces(1, -1.0, rest_ref, True)

    @pl.when((core == 0) & (chip == 1))
    def _():
        got_faces(0, 1.0, rest_ref, False)
        ends[1] = ends[1] - flux(core_ref, ring_ref)

    @pl.when(last)
    def _():
        got_faces(0, 1.0, core_ref, False)

    stores[0].start()

    @pl.when(last)
    def _():
        slope = rest_ref[1] * (gain / (0.5 * layer_thick))
        tail_ref[0] = ends[1] - (rest_ref[0] * slope + gain * rest_ref[1])
        tail_ref[1] = slope

    @pl.when(jnp.logical_not(last))
    def _():
        stores[1].start()
        stores[1].wait()

    stores[0].wait()


def faces(moist, core_pair, rest_pair, ring, got, rain):
    return pl.pallas_call(
        faces_kernel,
        in_specs=[ANY] + [VMEM] * (4 + PARTS),
        out_specs=[ANY, VMEM],
        out_shape=[
            jax.ShapeDtypeStruct(moist.shape, moist.dtype),
            jax.ShapeDtypeStruct((2,) + moist.shape[1:], moist.dtype),
        ],
        input_output_aliases={0: 0},
        scratch_shapes=[pltpu.VMEM((2,) + moist.shape[1:], jnp.float32), pltpu.SemaphoreType.DMA((2,))],
        compiler_params=params(12),
        cost_estimate=cost(20 * rain.size, 32 * rain.size),
        name="faces",
    )(moist, core_pair, rest_pair, ring, rain, *got)


def near_bottom_kernel(moist_in, tail_ref, own_ref, left_ref, right_ref, moist_out, head_ref, done, sem):
    del moist_in
    chip, core = place()
    layers = moist_out.shape[0]
    rows, half = own_ref.shape
    tile = half // 2
    mine = pl.ds(pl.multiple_of(core * rows, rows), rows)
    theirs = pl.ds(pl.multiple_of((1 - core) * rows, rows), rows)
    store = pltpu.make_async_copy(done, moist_out.at[layers - 1, :, half:], sem)

    @pl.when((core == 1) & (chip == 1))
    def _():
        for i, ref in enumerate((left_ref, right_ref)):
            to, at = slice(i * tile, (i + 1) * tile), slice(half + i * tile, half + (i + 1) * tile)
            done[:rows, to] = tail_ref[0, :rows, at] + tail_ref[1, :rows, at] * ref[...]
        done[rows:] = tail_ref[0, rows:, half:] + tail_ref[1, rows:, half:] * own_ref[...]
        store.start()

    head_ref[mine, :] = own_ref[:, pl.ds(pl.multiple_of(core * tile, tile), tile)]
    head_ref[theirs, :] = jnp.where(core == 0, left_ref[...], right_ref[...])

    @pl.when((core == 1) & (chip == 1))
    def _():
        store.wait()


def near_bottom(moist, tail, own, left, right):
    rows, half = own.shape
    return pl.pallas_call(
        near_bottom_kernel,
        in_specs=[ANY] + [VMEM] * 4,
        out_specs=[ANY, VMEM],
        out_shape=[
            jax.ShapeDtypeStruct(moist.shape, moist.dtype),
            jax.ShapeDtypeStruct((2 * rows, half // 2), jnp.float32),
        ],
        input_output_aliases={0: 0},
        scratch_shapes=[pltpu.VMEM((2 * rows, half), jnp.float32), pltpu.SemaphoreType.DMA],
        compiler_params=params(12),
        cost_estimate=cost(10 * own.size, 40 * own.size),
        name="near_bottom",
    )(moist, tail, own, left, right)


def bottom_kernel(moist_in, tail_ref, chip_far, both_far, moist_out, done, sem):
    del moist_in
    chip, core = place()
    layers = moist_out.shape[0]
    rows, half = chip_far.shape

    @pl.when((core == 1) & (chip == 1))
    def _():
        store = pltpu.make_async_copy(done, moist_out.at[layers - 1, :, :half], sem)
        for ref, where in ((both_far, slice(0, rows)), (chip_far, slice(rows, 2 * rows))):
            done[where] = tail_ref[0, where, :half] + tail_ref[1, where, :half] * ref[...]
        store.start()
        store.wait()


def bottom(moist, tail, chip_far, both_far):
    rows, half = chip_far.shape
    return pl.pallas_call(
        bottom_kernel,
        in_specs=[ANY] + [VMEM] * 3,
        out_specs=ANY,
        out_shape=jax.ShapeDtypeStruct(moist.shape, moist.dtype),
        input_output_aliases={0: 0},
        scratch_shapes=[pltpu.VMEM((2 * rows, half), jnp.float32), pltpu.SemaphoreType.DMA],
        compiler_params=params(12),
        cost_estimate=cost(4 * chip_far.size, 24 * chip_far.size),
        name="bottom",
    )(moist, tail, chip_far, both_far)


def gate_kernel(*refs):
    del refs


def gate(value, *first, stored=()):
    return pl.pallas_call(
        gate_kernel,
        in_specs=[ANY] * (1 + len(first)) + [HBM] * len(stored),
        out_specs=ANY,
        out_shape=jax.ShapeDtypeStruct(value.shape, value.dtype),
        input_output_aliases={0: 0},
        compiler_params=params(1),
        cost_estimate=cost(1, 1),
        name="gate",
    )(value, *first, *in_hbm(*stored))


def core_swap(value):
    return lax.ppermute(value, "depth", [(i, i ^ 1) for i in range(lax.axis_size("depth"))])


def chip_swap(value):
    return lax.ppermute(value, "depth", [(i, i ^ 2) for i in range(lax.axis_size("depth"))])


def ring_shift(value):
    return lax.ppermute(value, "depth", [(1, 3), (3, 2), (2, 0), (0, 1)])


def strip_swap(value, chips=0):
    depth, strips = lax.axis_size("depth"), lax.axis_size("strips")
    pairs = []
    for d in range(1, depth, 2):
        for s in range(strips):
            lower, upper = d * strips + s, ((d - 1) ^ chips) * strips + (s + 1) % strips
            pairs += [(lower, upper), (upper, lower)]
    return lax.ppermute(value, ("depth", "strips"), pairs)


def shards(pressure, texture, active, rain, k_sat, alpha, theta_sat, head_old, cell_code, section):
    tables = (k_sat[None], alpha[None], theta_sat[None])
    face_pair = face(tables, pressure, texture, active)
    ring = ring_shift(face_pair)
    moist, keep, send, mine, give, core_pair, rest_pair = soil(
        tables, pressure, texture, active, head_old, cell_code, section
    )
    recv, other = core_swap(send), core_swap(give)
    message = pack(keep, recv, mine, other)
    far = chip_swap(message)
    side, cross = rim(keep, recv, mine, other, message, ring)
    heads, left, right = sweeps(keep, recv, mine, other, far, strip_swap(side), strip_swap(cross, 2))
    got = [core_swap(part) for part in pass_on(core_pair, ring, side)]
    moist, tail = faces(moist, core_pair, rest_pair, ring, got, rain)
    moist, head = near_bottom(moist, tail, heads, core_swap(left), core_swap(right))
    heads_chip = gate(chip_swap(heads), stored=(moist,))
    return bottom(moist, tail, heads_chip, core_swap(heads_chip)), head


def solution(mesh):
    in_specs = (
        P("depth", "strips", None),
        P("depth", "strips", None),
        P("depth", "strips", None),
        P("strips", None),
        P(),
        P(),
        P(),
        P("strips", "depth"),
        P("strips", "depth"),
        P("strips", "depth"),
    )
    out_specs = (P("depth", "strips", None), P("strips", "depth"))
    return jax.shard_map(shards, mesh=mesh, in_specs=in_specs, out_specs=out_specs, check_vma=False)
```

```python
import functools
import math

import jax
import jax.numpy as jnp
from jax import lax
from jax.experimental import pallas as pl
from jax.experimental.pallas import tpu as pltpu
from jax.sharding import PartitionSpec as P

SWEEPS = 3
SUB = 8
PARTS = 2
LANE = 128
WIDTH = 4

layer_thick = 0.05
soil_step = 0.0002
spec_yield = 0.02
leak_rate = 0.5
river_cond = 0.5
fixed_cond = 3.0
residual = 0.15
mobile = 0.85

VMEM = pl.BlockSpec(memory_space=pltpu.VMEM)
ANY = pl.BlockSpec(memory_space=pl.ANY)
HBM = pl.BlockSpec(memory_space=pltpu.HBM)


def params(mib):
    return pltpu.CompilerParams(vmem_limit_bytes=mib * 2**20)


def cost(flops, nbytes, trans=0):
    return pl.CostEstimate(flops=int(flops), bytes_accessed=int(nbytes), transcendentals=int(trans))


def place():
    depth = lax.axis_index("depth")
    return depth // 2, depth % 2


def gathered(table, classes):
    return jnp.take_along_axis(table, classes, axis=1, mode="promise_in_bounds")


def picked(options, bits):
    for bit in bits:
        options = [
            jnp.where(bit, options[i + 1], options[i]) if i + 1 < len(options) else options[i]
            for i in range(0, len(options), 2)
        ]
    return options[0]


def fill_tables(tab, sat_ref, alpha_ref, theta_ref):
    classes = sat_ref.shape[1]
    scaled = (sat_ref, 1.0), (alpha_ref, 0.5 * math.log2(math.e)), (theta_ref, mobile)
    for i, (ref, scale) in enumerate(scaled):
        tab[i, :, :classes] = jnp.broadcast_to(ref[...] * scale, (SUB, classes))


def face_kernel(
    sat_hbm, alpha_hbm, psi_hbm, tex_hbm, act_hbm, out_ref, kinds, acts, given, tab, sems
):
    chip, _ = place()
    layer = (1 - chip) * (psi_hbm.shape[0] - 1)
    cols = psi_hbm.shape[2]
    classes = sat_hbm.shape[1]
    chunks = 2
    rows = kinds.shape[0] // chunks

    def copies(i):
        part = pl.ds(i * rows, rows)
        pairs = (
            (psi_hbm.at[layer, part], out_ref.at[0, part]),
            (tex_hbm.at[layer, part], kinds.at[part]),
            (act_hbm.at[layer, part], acts.at[part]),
        )
        return [pltpu.make_async_copy(src, dst, sems.at[i, k]) for k, (src, dst) in enumerate(pairs)]

    tables = [
        pltpu.make_async_copy(src, given.at[k], sems.at[chunks, k]) for k, src in enumerate((sat_hbm, alpha_hbm))
    ]
    for c in tables:
        c.start()
    for i in range(chunks):
        for c in copies(i):
            c.start()
    for c in tables:
        c.wait()
    for i, scale in enumerate((1.0, 0.5 * math.log2(math.e))):
        tab[i, :, :classes] = jnp.broadcast_to(given[i] * scale, (SUB, classes))

    for i in range(chunks):
        for c in copies(i):
            c.wait()

        def columns(q, carry):
            lanes = pl.ds(pl.multiple_of(q * LANE, LANE), LANE)
            for r in range(i * rows, (i + 1) * rows, SUB):
                rws = slice(r, r + SUB)
                kind = kinds[rws, lanes]
                wet = jnp.exp2(gathered(tab[1], kind) * jnp.minimum(out_ref[0, rws, lanes], 0.0))
                active = acts[rws, lanes].astype(jnp.float32)
                out_ref[1, rws, lanes] = gathered(tab[0], kind) * active * (wet * wet)
            return carry

        lax.fori_loop(0, cols // LANE, columns, 0, unroll=8)


def in_hbm(*arrays):
    return [pltpu.with_memory_space_constraint(x, pltpu.HBM) for x in arrays]


def face(tables, pressure, texture, active):
    _, nrows, cols = pressure.shape
    size = nrows * cols
    return pl.pallas_call(
        face_kernel,
        in_specs=[HBM] * 5,
        out_specs=VMEM,
        out_shape=jax.ShapeDtypeStruct((2, nrows, cols), jnp.float32),
        scratch_shapes=[
            pltpu.VMEM((nrows, cols), jnp.int32),
            pltpu.VMEM((nrows, cols), jnp.int32),
            pltpu.VMEM((2,) + tables[0].shape, jnp.float32),
            pltpu.VMEM((2, SUB, LANE), jnp.float32),
            pltpu.SemaphoreType.DMA((3, 3)),
        ],
        compiler_params=params(8),
        cost_estimate=cost(20 * size, 20 * size, size),
        name="face",
    )(*in_hbm(*tables[:2], pressure, texture, active))


def soil_kernel(
    sat_ref, alpha_ref, theta_ref, psi_ref, tex_ref, act_ref, old_ref, code_ref, section_ref,
    moist_ref, keep_ref, send_ref, mine_ref, give_ref, core_ref, rest_ref, tab, part, tile,
):
    step = pl.program_id(0)
    _, core = place()
    layers, rows, cols = psi_ref.shape
    classes = sat_ref.shape[1]

    @pl.when(step == 0)
    def _():
        fill_tables(tab, sat_ref, alpha_ref, theta_ref)

    sat_tab, par_tab = tab[0], tab[1]
    theta = [jnp.broadcast_to(tab[2, :, i : i + 1], (SUB, LANE)) for i in range(classes)]
    nbits = max(1, (classes - 1).bit_length())
    face = 0.5 * soil_step / layer_thick
    core_layer = (1 - core) * (layers - 1)
    rest_layer = core * (layers - 1)

    def columns(q, carry):
        lanes = pl.ds(pl.multiple_of(q * LANE, LANE), LANE)
        for r in range(0, rows, SUB):
            rws = slice(r, r + SUB)
            trans = store = charge = jnp.zeros((SUB, LANE), jnp.float32)
            for layer in range(layers):
                kind = tex_ref[layer, rws, lanes]
                psi = psi_ref[layer, rws, lanes]
                active = act_ref[layer, rws, lanes].astype(jnp.float32)
                bits = [(kind & (1 << b)) != 0 for b in range(nbits - 1)] + [kind >= 1 << (nbits - 1)]
                wet = jnp.exp2(gathered(par_tab, kind) * jnp.minimum(psi, 0.0))
                cond = gathered(sat_tab, kind) * active * (wet * wet)
                mob = picked(theta, bits)
                mobwet = mob * wet
                trans = trans + cond
                charge = charge + cond * wet
                store = store + (mob - mobwet)
                held = mob * (residual / mobile) + mobwet
                if layer == 0:
                    first, own = cond, held
                else:
                    flux = (cond_up + cond) * ((psi_up - psi) * (face / layer_thick) + face)
                    moist_ref[layer - 1, rws, lanes] = own - flux
                    own = held + flux
                psi_up, cond_up = psi, cond
            moist_ref[layers - 1, rws, lanes] = own
            part[r // SUB, 0, :, lanes] = trans
            part[r // SUB, 1, :, lanes] = store
            part[r // SUB, 2, :, lanes] = charge
            core_ref[0, rws, lanes] = psi_ref[core_layer, rws, lanes]
            core_ref[1, rws, lanes] = jnp.where(core == 0, cond, first)
            rest_ref[0, rws, lanes] = psi_ref[rest_layer, rws, lanes]
            rest_ref[1, rws, lanes] = jnp.where(core == 0, first, cond)
        return carry

    lax.fori_loop(0, cols // LANE, columns, 0, unroll=8)

    blocks = rows // SUB
    for r in range(blocks):
        at = pl.ds(pl.multiple_of(step * rows + r * SUB, SUB), SUB)
        code = code_ref[at]
        river = jnp.where(code == 1, river_cond, jnp.where(code == 2, fixed_cond, 0.0))
        for a, value in enumerate((old_ref[at], river, river * section_ref[at])):
            tile[r, a] = value

    half = keep_ref.shape[0] - 1
    for r in range(blocks):
        block = step * blocks + r

        def put(ref, tile_ref, at):
            ref[at] = part[r]
            tile_ref[at] = tile[r]

        @pl.when((block <= half) & (core == 0))
        def _():
            put(keep_ref, mine_ref, block)

        @pl.when((block <= half) & (core == 1))
        def _():
            put(send_ref, give_ref, block)

        @pl.when((block >= half - 1) & (core == 0))
        def _():
            put(send_ref, give_ref, block - (half - 1))

        @pl.when((block >= half - 1) & (core == 1))
        def _():
            put(keep_ref, mine_ref, block - (half - 1))


def soil(tables, pressure, texture, active, head_old, cell_code, section):
    layers, nrows, cols = pressure.shape
    classes = tables[0].shape[1]
    rows = nrows // 4
    blocks = nrows // (2 * SUB) + 1
    whole = pl.BlockSpec((1, classes), lambda j: (0, 0))
    block = pl.BlockSpec((layers, rows, cols), lambda j: (0, j, 0))
    pair = pl.BlockSpec((2, rows, cols), lambda j: (0, j, 0))
    msg = jax.ShapeDtypeStruct((blocks, 3, SUB, cols), jnp.float32)
    msg_spec = pl.BlockSpec(msg.shape, lambda j: (0, 0, 0, 0))
    tile = pl.BlockSpec(head_old.shape, lambda j: (0, 0))
    part = jax.ShapeDtypeStruct((blocks, 3, SUB, head_old.shape[1]), jnp.float32)
    part_spec = pl.BlockSpec(part.shape, lambda j: (0, 0, 0, 0))
    layer2 = jax.ShapeDtypeStruct((2, nrows, cols), jnp.float32)
    size = layers * nrows * cols
    return pl.pallas_call(
        soil_kernel,
        grid=(nrows // rows,),
        in_specs=[whole, whole, whole, block, block, block, tile, tile, tile],
        out_specs=[block, msg_spec, msg_spec, part_spec, part_spec, pair, pair],
        out_shape=[jax.ShapeDtypeStruct((layers, nrows, cols), jnp.float32), msg, msg, part, part, layer2, layer2],
        scratch_shapes=[
            pltpu.VMEM((3, SUB, LANE), jnp.float32),
            pltpu.VMEM((rows // SUB, 3, SUB, cols), jnp.float32),
            pltpu.VMEM((rows // SUB, 3, SUB, head_old.shape[1]), jnp.float32),
        ],
        compiler_params=params(32),
        cost_estimate=cost(60 * size, 20 * size, size),
        name="soil",
    )(*in_hbm(*tables, pressure, texture, active, head_old, cell_code, section))


def edge_lane(chip):
    return (1 - chip) * (LANE - WIDTH)


def on_edge(value, chip):
    lane = lax.broadcasted_iota(jnp.int32, value.shape, 1)
    base = edge_lane(chip)
    return jnp.where((lane >= base) & (lane < base + WIDTH), value, 0.0)


def shift(array, block=0):
    return WIDTH * (6 * block + array)


SHARE = LANE // (6 * WIDTH)


def packed(pieces, chip, block=0):
    total = None
    for a, piece in enumerate(pieces):
        moved = pltpu.roll(on_edge(piece, chip), shift(a, block), 1)
        total = moved if total is None else total + moved
    return total


def unpacked(tile, array, block=0):
    return pltpu.roll(tile, LANE - shift(array, block), 1)


def nearest(block, core):
    return jnp.where(core == 0, block[:SWEEPS], block[SUB - SWEEPS :])


def spread(rows, core):
    zeros = jnp.zeros((SUB - SWEEPS, rows.shape[1]), rows.dtype)
    return jnp.where(core == 0, jnp.concatenate([rows, zeros], 0), jnp.concatenate([zeros, rows], 0))


def put_rows(ref, plane, pieces):
    planes = ref.shape[0] - plane
    used = sum(piece.shape[0] for piece in pieces)
    spare = jnp.zeros((planes * SUB - used, pieces[0].shape[1]), jnp.float32)
    rows = jnp.concatenate([*pieces, spare], 0)
    for i in range(planes):
        ref[plane + i] = rows[i * SUB : (i + 1) * SUB]


def get_rows(ref, plane, counts):
    rows = jnp.concatenate([ref[i] for i in range(plane, ref.shape[0])], 0)
    out, at = [], 0
    for count in counts:
        out.append(rows[at : at + count])
        at += count
    return out


def fold(tiles):
    mid = SUB // 2
    return jnp.concatenate([part for tile in tiles for part in (tile[:mid], tile[mid:])], 1)


def unfold(rows):
    parts = [rows[:, i : i + LANE] for i in range(0, rows.shape[1], LANE)]
    return [jnp.concatenate(parts[i : i + 2], 0) for i in range(0, len(parts), 2)]


def half_lanes(which, half):
    return pl.ds(pl.multiple_of(which * half, half), half)


def slab_lanes(chip, half):
    return pl.ds(pl.multiple_of(half - LANE + chip * LANE, LANE), LANE)


def tile_rows(mine_ref, other_ref, b, core, which, array, start, stop):
    lanes = slice(start, stop)
    return jnp.where(core == which, mine_ref[b, array, :, lanes], other_ref[b, array, :, lanes])


def edge_inputs(mine_ref, other_ref, b, chip, core):
    tile = mine_ref.shape[3]
    out = []
    for a in range(3):
        left = tile_rows(mine_ref, other_ref, b, core, 1, a, tile - LANE, tile)
        right = tile_rows(mine_ref, other_ref, b, core, 0, a, 0, LANE)
        out.append(jnp.where(chip == 0, left, right))
    return out


def pack_kernel(keep_ref, recv_ref, mine_ref, other_ref, out_ref):
    chip, core = place()
    blocks, _, _, cols = keep_ref.shape
    half = cols // 2
    away = half_lanes(1 - chip, half)
    slab = slab_lanes(chip, half)
    main = 3 * (blocks - 1)
    tiles = [None] * -(-blocks // SHARE)
    for j in range(blocks):
        b = j + core if j < blocks - 1 else (1 - core) * (blocks - 1)
        sums = [keep_ref[b, a, :, away] + recv_ref[b, a, :, away] for a in range(3)]
        if j < blocks - 1:
            for a in range(3):
                out_ref[3 * j + a] = sums[a]
        else:
            rows = [nearest(v, core) for v in sums]
        pieces = [keep_ref[b, a, :, slab] + recv_ref[b, a, :, slab] for a in range(3)]
        pieces += edge_inputs(mine_ref, other_ref, b, chip, core)
        piece = packed(pieces, chip, j % SHARE)
        i = j // SHARE
        tiles[i] = piece if tiles[i] is None else tiles[i] + piece
    put_rows(out_ref, main, [*rows, fold(tiles)])


def pack(keep, recv, mine, other):
    blocks, _, _, cols = keep.shape
    half = cols // 2
    return pl.pallas_call(
        pack_kernel,
        in_specs=[VMEM] * 4,
        out_specs=VMEM,
        out_shape=jax.ShapeDtypeStruct((3 * blocks - 1, SUB, half), jnp.float32),
        compiler_params=params(8),
        cost_estimate=cost(keep.size, 12 * keep.size),
        name="pack",
    )(keep, recv, mine, other)


def rim_kernel(keep_ref, recv_ref, mine_ref, other_ref, *refs):
    side_ref, cross_ref = refs[-2:]
    chip, core = place()
    blocks, _, _, cols = keep_ref.shape
    half = cols // 2
    tile = half // 2
    b = core * (blocks - 1)
    near, away = half_lanes(chip, half), half_lanes(1 - chip, half)
    spare = jnp.zeros((SWEEPS, half - LANE), jnp.float32)

    def sums(lanes):
        return [keep_ref[b, a, :, lanes] + recv_ref[b, a, :, lanes] for a in range(3)]

    def rows(values):
        return [nearest(v, core) for v in values]

    tiles = [
        jnp.concatenate([tile_rows(mine_ref, other_ref, b, core, which, a, 0, tile) for which in range(2)], 1)
        for a in range(3)
    ]
    halo = nearest(packed(sums(slab_lanes(1 - chip, half)), 1 - chip), core)
    put_rows(side_ref, 0, [*rows(sums(near)), *rows(tiles), jnp.concatenate([halo, spare], 1)])
    inputs = edge_inputs(mine_ref, other_ref, b, chip, core)
    halo = nearest(packed(sums(slab_lanes(chip, half)) + inputs, chip), core)
    put_rows(cross_ref, 0, [*rows(sums(away)), jnp.concatenate([halo, spare], 1)])


def rim(keep, recv, mine, other, *first):
    half = keep.shape[3] // 2
    return pl.pallas_call(
        rim_kernel,
        in_specs=[VMEM] * 4 + [ANY] * len(first),
        out_specs=[VMEM] * 2,
        out_shape=[jax.ShapeDtypeStruct((n, SUB, half), jnp.float32) for n in (3, 2)],
        compiler_params=params(8),
        cost_estimate=cost(keep.size // 8, keep.size),
        name="rim",
    )(keep, recv, mine, other, *first)


def sweep_kernel(keep_ref, recv_ref, mine_ref, other_ref, far_ref, side_ref, cross_ref, out_ref, left_ref, right_ref, work):
    chip, core = place()
    strip = lax.axis_index("strips")
    blocks, _, _, cols = keep_ref.shape
    half = cols // 2
    tile = half // 2
    main = 3 * (blocks - 1)

    def cells(at, lanes, sums, inputs):
        trans = sums[0] * layer_thick
        store = spec_yield + sums[1] * layer_thick
        old, river, inflow = inputs
        rows = pl.ds(pl.multiple_of(at * SUB, SUB), SUB)
        work[0, rows, lanes] = trans
        work[1, rows, lanes] = store + river
        work[2, rows, lanes] = store * old + leak_rate * layer_thick * sums[2] + inflow
        work[3, rows, lanes] = old

    def halo(at, sums, inputs):
        sums, inputs = ([on_edge(v, 1 - chip) for v in values] for values in (sums, inputs))
        cells(at, slice(half, half + LANE), sums, inputs)

    near, slab = half_lanes(chip, half), slab_lanes(1 - chip, half)
    *beyond, tiles = get_rows(far_ref, main, (SWEEPS, SWEEPS, SWEEPS, SUB // 2))
    tiles = unfold(tiles)
    for j in range(blocks):
        b = j + core if j < blocks - 1 else (1 - core) * (blocks - 1)
        if j < blocks - 1:
            far = [far_ref[3 * j + a] for a in range(3)]
        else:
            far = [spread(v, core) for v in beyond]
        sums = [keep_ref[b, a, :, near] + recv_ref[b, a, :, near] + far[a] for a in range(3)]
        for which in range(2):
            lanes = slice(which * tile, (which + 1) * tile)
            inputs = [tile_rows(mine_ref, other_ref, b, core, which, a, 0, tile) for a in range(3)]
            cells(b, lanes, [s[:, lanes] for s in sums], inputs)
        far = [unpacked(tiles[j // SHARE], a, j % SHARE) for a in range(6)]
        sums = [keep_ref[b, a, :, slab] + recv_ref[b, a, :, slab] + far[a] for a in range(3)]
        halo(b, sums, far[3:])
    outside = ((core == 0) & (strip == 0)) | ((core == 1) & (strip == lax.axis_size("strips") - 1))

    def inside(value):
        return jnp.where(outside, 0.0, value)

    side = [spread(v, 1 - core) for v in get_rows(side_ref, 0, (SWEEPS,) * 7)]
    cross = [spread(v, 1 - core) for v in get_rows(cross_ref, 0, (SWEEPS,) * 4)]
    cells(blocks, slice(0, half), [inside(side[a] + cross[a]) for a in range(3)], [inside(v) for v in side[3:6]])
    side, cross = side[6][:, :LANE], cross[3][:, :LANE]
    sums = [inside(unpacked(side, a) + unpacked(cross, a)) for a in range(3)]
    halo(blocks, sums, [inside(unpacked(cross, a)) for a in range(3, 6)])

    trans, base, rhs, head = (work[i] for i in range(4))
    rows, lanes = trans.shape
    right = jnp.sqrt(trans * pltpu.roll(trans, lanes - 1, 1))
    left = pltpu.roll(right, 1, 1)
    down = jnp.sqrt(trans * pltpu.roll(trans, rows - 1, 0))
    up = pltpu.roll(down, 1, 0)
    inverse = 1.0 / (base + right + left + down + up)
    for _ in range(SWEEPS):
        head = inverse * (
            rhs
            + right * pltpu.roll(head, lanes - 1, 1)
            + left * pltpu.roll(head, 1, 1)
            + down * pltpu.roll(head, rows - 1, 0)
            + up * pltpu.roll(head, 1, 0)
        )
    work[0] = head
    out_ref[...] = work[0, pl.ds(pl.multiple_of(core * SUB, SUB), out_ref.shape[0]), :half]
    left_ref[...] = out_ref[:, :tile]
    right_ref[...] = out_ref[:, tile:]


def sweeps(keep, recv, mine, other, far, side, cross):
    blocks = keep.shape[0]
    half = keep.shape[3] // 2
    return pl.pallas_call(
        sweep_kernel,
        in_specs=[VMEM] * 7,
        out_specs=[VMEM] * 3,
        out_shape=[
            jax.ShapeDtypeStruct(((blocks - 1) * SUB, half // part), jnp.float32) for part in (1, 2, 2)
        ],
        scratch_shapes=[pltpu.VMEM((4, (blocks + 1) * SUB, half + LANE), jnp.float32)],
        compiler_params=params(12),
        cost_estimate=cost(20 * keep.size, 12 * keep.size),
        name="sweeps",
    )(keep, recv, mine, other, far, side, cross)


def pass_on_kernel(core_ref, ring_ref, first, *out_refs):
    del first
    chip, core = place()
    rows = out_refs[0].shape[1]
    for i, out_ref in enumerate(out_refs):
        part = slice(i * rows, (i + 1) * rows)

        @pl.when(chip == core)
        def _():
            out_ref[...] = ring_ref[:, part]

        @pl.when(chip != core)
        def _():
            out_ref[...] = core_ref[:, part]


def pass_on(core_pair, ring, first):
    return pl.pallas_call(
        pass_on_kernel,
        in_specs=[VMEM] * 2 + [ANY],
        out_specs=[VMEM] * PARTS,
        out_shape=[jax.ShapeDtypeStruct((2, ring.shape[1] // PARTS, ring.shape[2]), ring.dtype)] * PARTS,
        compiler_params=params(8),
        cost_estimate=cost(ring.size, 8 * ring.size),
        name="pass_on",
    )(core_pair, ring, first)


def faces_kernel(moist_in, core_ref, rest_ref, ring_ref, rain_ref, *refs):
    del moist_in
    got_refs, (moist_out, tail_ref, ends, sems) = refs[:PARTS], refs[PARTS:]
    chip, core = place()
    layers = moist_out.shape[0]
    copies = [
        (moist_out.at[layer], ends.at[i], sems.at[i]) for i, layer in enumerate((0, layers - 1))
    ]
    loads = [pltpu.make_async_copy(src, dst, sem) for src, dst, sem in copies]
    stores = [pltpu.make_async_copy(dst, src, sem) for src, dst, sem in copies]
    for c in loads:
        c.start()
    for c in loads:
        c.wait()
    gain = soil_step / layer_thick
    face = 0.5 * gain
    last = (core == 1) & (chip == 1)

    def flux(upper, lower):
        return (upper[1] + lower[1]) * ((upper[0] - lower[0]) * (face / layer_thick) + face)

    def got_faces(which, sign, ref, below):
        for i, got in enumerate(got_refs):
            rows = got.shape[1]
            part = slice(i * rows, (i + 1) * rows)
            mine = ref[0, part], ref[1, part]
            change = flux(mine, got) if below else flux(got, mine)
            ends[which, part] = ends[which, part] + sign * change

    @pl.when((core == 0) & (chip == 0))
    def _():
        ends[0] = ends[0] + gain * rain_ref[...]
        got_faces(1, -1.0, core_ref, True)

    @pl.when((core == 1) & (chip == 0))
    def _():
        ends[0] = ends[0] + flux(ring_ref, core_ref)
        got_faces(1, -1.0, rest_ref, True)

    @pl.when((core == 0) & (chip == 1))
    def _():
        got_faces(0, 1.0, rest_ref, False)
        ends[1] = ends[1] - flux(core_ref, ring_ref)

    @pl.when(last)
    def _():
        got_faces(0, 1.0, core_ref, False)

    stores[0].start()

    @pl.when(last)
    def _():
        slope = rest_ref[1] * (gain / (0.5 * layer_thick))
        tail_ref[0] = ends[1] - (rest_ref[0] * slope + gain * rest_ref[1])
        tail_ref[1] = slope

    @pl.when(jnp.logical_not(last))
    def _():
        stores[1].start()
        stores[1].wait()

    stores[0].wait()


def faces(moist, core_pair, rest_pair, ring, got, rain):
    return pl.pallas_call(
        faces_kernel,
        in_specs=[ANY] + [VMEM] * (4 + PARTS),
        out_specs=[ANY, VMEM],
        out_shape=[
            jax.ShapeDtypeStruct(moist.shape, moist.dtype),
            jax.ShapeDtypeStruct((2,) + moist.shape[1:], moist.dtype),
        ],
        input_output_aliases={0: 0},
        scratch_shapes=[pltpu.VMEM((2,) + moist.shape[1:], jnp.float32), pltpu.SemaphoreType.DMA((2,))],
        compiler_params=params(12),
        cost_estimate=cost(20 * rain.size, 32 * rain.size),
        name="faces",
    )(moist, core_pair, rest_pair, ring, rain, *got)


def near_bottom_kernel(moist_in, tail_ref, own_ref, left_ref, right_ref, moist_out, head_ref, done, sem):
    del moist_in
    chip, core = place()
    layers = moist_out.shape[0]
    rows, half = own_ref.shape
    tile = half // 2
    mine = pl.ds(pl.multiple_of(core * rows, rows), rows)
    theirs = pl.ds(pl.multiple_of((1 - core) * rows, rows), rows)
    store = pltpu.make_async_copy(done, moist_out.at[layers - 1, :, half:], sem)

    @pl.when((core == 1) & (chip == 1))
    def _():
        for i, ref in enumerate((left_ref, right_ref)):
            to, at = slice(i * tile, (i + 1) * tile), slice(half + i * tile, half + (i + 1) * tile)
            done[:rows, to] = tail_ref[0, :rows, at] + tail_ref[1, :rows, at] * ref[...]
        done[rows:] = tail_ref[0, rows:, half:] + tail_ref[1, rows:, half:] * own_ref[...]
        store.start()

    head_ref[mine, :] = own_ref[:, pl.ds(pl.multiple_of(core * tile, tile), tile)]
    head_ref[theirs, :] = jnp.where(core == 0, left_ref[...], right_ref[...])

    @pl.when((core == 1) & (chip == 1))
    def _():
        store.wait()


def near_bottom(moist, tail, own, left, right):
    rows, half = own.shape
    return pl.pallas_call(
        near_bottom_kernel,
        in_specs=[ANY] + [VMEM] * 4,
        out_specs=[ANY, VMEM],
        out_shape=[
            jax.ShapeDtypeStruct(moist.shape, moist.dtype),
            jax.ShapeDtypeStruct((2 * rows, half // 2), jnp.float32),
        ],
        input_output_aliases={0: 0},
        scratch_shapes=[pltpu.VMEM((2 * rows, half), jnp.float32), pltpu.SemaphoreType.DMA],
        compiler_params=params(12),
        cost_estimate=cost(10 * own.size, 40 * own.size),
        name="near_bottom",
    )(moist, tail, own, left, right)


def bottom_kernel(moist_in, tail_ref, chip_far, both_far, moist_out, done, sem):
    del moist_in
    chip, core = place()
    layers = moist_out.shape[0]
    rows, half = chip_far.shape

    @pl.when((core == 1) & (chip == 1))
    def _():
        store = pltpu.make_async_copy(done, moist_out.at[layers - 1, :, :half], sem)
        for ref, where in ((both_far, slice(0, rows)), (chip_far, slice(rows, 2 * rows))):
            done[where] = tail_ref[0, where, :half] + tail_ref[1, where, :half] * ref[...]
        store.start()
        store.wait()


def bottom(moist, tail, chip_far, both_far):
    rows, half = chip_far.shape
    return pl.pallas_call(
        bottom_kernel,
        in_specs=[ANY] + [VMEM] * 3,
        out_specs=ANY,
        out_shape=jax.ShapeDtypeStruct(moist.shape, moist.dtype),
        input_output_aliases={0: 0},
        scratch_shapes=[pltpu.VMEM((2 * rows, half), jnp.float32), pltpu.SemaphoreType.DMA],
        compiler_params=params(12),
        cost_estimate=cost(4 * chip_far.size, 24 * chip_far.size),
        name="bottom",
    )(moist, tail, chip_far, both_far)


def gate_kernel(*refs):
    del refs


def gate(value, *first, stored=()):
    return pl.pallas_call(
        gate_kernel,
        in_specs=[ANY] * (1 + len(first)) + [HBM] * len(stored),
        out_specs=ANY,
        out_shape=jax.ShapeDtypeStruct(value.shape, value.dtype),
        input_output_aliases={0: 0},
        compiler_params=params(1),
        cost_estimate=cost(1, 1),
        name="gate",
    )(value, *first, *in_hbm(*stored))


def core_swap(value):
    return lax.ppermute(value, "depth", [(i, i ^ 1) for i in range(lax.axis_size("depth"))])


def chip_swap(value):
    return lax.ppermute(value, "depth", [(i, i ^ 2) for i in range(lax.axis_size("depth"))])


def ring_shift(value):
    return lax.ppermute(value, "depth", [(1, 3), (3, 2), (2, 0), (0, 1)])


def strip_swap(value, chips=0):
    depth, strips = lax.axis_size("depth"), lax.axis_size("strips")
    pairs = []
    for d in range(1, depth, 2):
        for s in range(strips):
            lower, upper = d * strips + s, ((d - 1) ^ chips) * strips + (s + 1) % strips
            pairs += [(lower, upper), (upper, lower)]
    return lax.ppermute(value, ("depth", "strips"), pairs)


def shards(pressure, texture, active, rain, k_sat, alpha, theta_sat, head_old, cell_code, section):
    tables = (k_sat[None], alpha[None], theta_sat[None])
    face_pair = face(tables, pressure, texture, active)
    ring = ring_shift(face_pair)
    moist, keep, send, mine, give, core_pair, rest_pair = soil(
        tables, pressure, texture, active, head_old, cell_code, section
    )
    recv, other = core_swap(send), core_swap(give)
    message = pack(keep, recv, mine, other)
    far = chip_swap(message)
    side, cross = rim(keep, recv, mine, other, message, ring)
    heads, left, right = sweeps(keep, recv, mine, other, far, strip_swap(side), strip_swap(cross, 2))
    got = [core_swap(part) for part in pass_on(core_pair, ring, side)]
    moist, tail = faces(moist, core_pair, rest_pair, ring, got, rain)
    moist, head = near_bottom(moist, tail, heads, core_swap(left), core_swap(right))
    heads_chip = gate(chip_swap(heads), stored=(moist,))
    return bottom(moist, tail, heads_chip, core_swap(heads_chip)), head


def solution(mesh):
    in_specs = (
        P("depth", "strips", None),
        P("depth", "strips", None),
        P("depth", "strips", None),
        P("strips", None),
        P(),
        P(),
        P(),
        P("strips", "depth"),
        P("strips", "depth"),
        P("strips", "depth"),
    )
    out_specs = (P("depth", "strips", None), P("strips", "depth"))
    return jax.shard_map(shards, mesh=mesh, in_specs=in_specs, out_specs=out_specs, check_vma=False)
```
